512 devices in a mesh: wide: 32 (over z_lo, x, core), narrow: 16 (over z_hi, y).
Axes of the slice: x: 4, y: 4, z: 16 (z_hi: 4, z_lo: 4; z = z_hi * 4 + z_lo), core: 2. Of those that a mesh axis runs over, the one named last changes fastest.
Arguments:
- hidden_in: bfloat16 [65536, 4096], P(('wide', 'narrow')), may hold values from -6 to 6
- queries: bfloat16 [65536, 4096], P(('wide', 'narrow')), may hold values from -256 to 256, as said below
- keys: bfloat16 [65536, 512], P(('wide', 'narrow')), may hold values from -8 to 8, as said below
- lengths: int32 [512, 4], P(('wide', 'narrow')), may hold values from 1 to 64, 128 in all within a row
- master: float32 [4096, 512], P(('narrow', 'wide')), may hold values from -0.09375 to 0.09375
- moment: float32 [4096, 512], P(('narrow', 'wide')), may hold values from -0.0625 to 0.0625
- second: float32 [4096, 512], P(('narrow', 'wide')), may hold values from 1e-05 to 0.1
Outputs:
- attended: bfloat16 [65536, 4096], P(('wide', 'narrow'))
- grad_hidden: bfloat16 [65536, 4096], P(('wide', 'narrow'))
- master_new: float32 [4096, 512], P(('narrow', 'wide'))
- moment_new: float32 [4096, 512], P(('narrow', 'wide'))
- second_new: float32 [4096, 512], P(('narrow', 'wide'))
The draws below stay inside these ranges and needn't reach their ends.
Inputs may be any that keep to these rules, and one draw needn't show every extreme that they name: `queries`: queries are real-valued activations. `keys`: keys are real-valued activations. `lengths`: each row sums to 128; its largest entry is 64.
All inputs are finite; a program needn't handle non-finite values.
Results may differ from the reference program's by a relative error of at most 0.009.
Values may be sent and summed in bfloat16 or wider, within the bound.
No kernel may reach another device: no remote copies, remote signals or barrier semaphores. Data moves between devices by JAX's collectives and lax.ppermute only.
A program may use at most 64 MiB of HBM per device.

```python
import math
import jax
import jax.numpy as jnp
import numpy as np
from jax import lax

D = 4096
HD = 128
VH = 4
QH = 32
SEGS = 4
TOK_DEV = 128
MOST = 64
DEVICES_ALL = 512
TOKENS = 65536


def shared_keys(key):
    base = jax.random.normal(key, (TOKENS, VH * HD), jnp.float32)
    return jnp.clip(base, -6.0, 6.0)


def draw_keys(key, part):
    base = shared_keys(key)
    return base.astype(jnp.bfloat16)


def draw_queries(key, part):
    key = jax.random.fold_in(key, 7)
    groups = QH // VH
    drawn = jnp.clip(jax.random.normal(key, (TOKENS, VH, groups, HD), jnp.float32), -6.0, 6.0)
    return drawn.reshape(TOKENS, QH * HD).astype(jnp.bfloat16)


def block_levels(rng, shape, shards, least, top_value):
    loudness, own = 1.0, jax.random.fold_in(rng, 6)
    for axis_at, shards_of in shards:
        draws = jnp.exp(jax.random.uniform(jax.random.fold_in(own, axis_at), (shards_of,), jnp.float32, least / len(shards), top_value / len(shards)))
        loudness = loudness * jnp.repeat(draws, shape[axis_at] // shards_of).reshape([-1 if axis == axis_at else 1 for axis in range(len(shape))])
    return loudness


def split_up(number_of, total, limit, slope):
    weights = [(1 << 20) // math.isqrt(standing ** slope) + 1 for standing in range(2, number_of + 1)]
    rest, counts = total - limit - (number_of - 1), [1] * (number_of - 1)
    while rest > 0:
        free = [i for i in range(number_of - 1) if counts[i] < limit]
        whole, remaining = sum([weights[i] for i in free]), rest
        for i in free:
            extra = min(limit - counts[i], max(1, remaining * weights[i] // whole), rest)
            counts[i] = counts[i] + extra
            rest = rest - extra
    return np.array([limit] + counts)


def uneven(rng, count, total, most, slope):
    if count == 2:
        one = jax.random.randint(rng, (), max(1, total - most), min(most, total - 1) + 1)
        return jnp.stack([one, total - one])
    sizes = jnp.asarray(split_up(count, total, most, slope), jnp.int32)
    twos = (count - 1) // 2
    source_of, sink = sizes[1:1 + 2 * twos:2], sizes[2:2 + 2 * twos:2]
    slack = jnp.minimum(source_of - 1, most - sink)
    shifted = jax.random.randint(jax.random.fold_in(rng, 1), (twos,), 0, 1 << 20) % (slack + 1)
    sizes = sizes.at[1:1 + 2 * twos:2].set(source_of - shifted).at[2:2 + 2 * twos:2].set(sink + shifted)
    return sizes[jax.random.permutation(jax.random.fold_in(rng, 2), count)]


def normal_values(own_key, dims, width, most, split=(), held_as=jnp.bfloat16):
    factor_of = block_levels(own_key, dims, split, -0.22, 0.18) if split else 1.0
    array = jax.random.normal(own_key, dims, jnp.float32) * width * factor_of
    return jnp.minimum(jnp.maximum(array, -most), most).astype(held_as)


def setup_inputs(seed: int = 0) -> dict:
    key_list = jax.random.split(jax.random.key(seed), 8)
    hidden_in = normal_values(key_list[0], (TOKENS, D), 1.0, 6.0, ((0, 512),))
    queries = draw_queries(jax.random.fold_in(key_list[7], 71), 0)
    keys = draw_keys(jax.random.fold_in(key_list[7], 71), 0)
    lengths = jax.vmap(lambda own: uneven(own, SEGS, TOK_DEV, MOST, 2))(jax.random.split(key_list[3], DEVICES_ALL)).reshape((DEVICES_ALL, SEGS)).astype(jnp.int32)
    master = normal_values(key_list[4], (D, VH * HD), D ** -0.5, 0.09375, ((0, 512),), jnp.float32)
    moment = normal_values(key_list[5], (D, VH * HD), 0.004, 0.0625, ((0, 512),), jnp.float32)
    second = jnp.clip(jnp.exp(math.log(0.1) - 9.2103404 * jax.random.uniform(key_list[6], (D, VH * HD), jnp.float32) ** block_levels(key_list[6], (D, VH * HD), ((0, 512),), -0.2, 0.2)), 9.999999747378752e-06, 0.1)
    return {"hidden_in": hidden_in, "queries": queries, "keys": keys, "lengths": lengths, "master": master, "moment": moment, "second": second}


beta_one = 0.9
beta_two = 0.95
adam_eps = 1e-08
learn_rate = 0.001
decay_rate = 0.1

def attend_block(operands):
    query_blk, key_blk, value_blk, length_row = operands
    tok_rows = query_blk.shape[0]
    positions = jnp.arange(tok_rows, dtype=jnp.int32)
    seg_ends = jnp.cumsum(length_row).astype(jnp.int32)
    segment_ids = lax.optimization_barrier(jnp.sum((positions[:, None] >= seg_ends[None, :]).astype(jnp.int32), axis=1))
    allowed = (segment_ids[:, None] == segment_ids[None, :]) & (positions[None, :] <= positions[:, None])
    scores = jnp.einsum('tkgd,skd->kgts', query_blk.astype(jnp.float32), key_blk.astype(jnp.float32)) / jnp.sqrt(jnp.float32(HD))
    scores = jnp.where(allowed[None, None], scores, jnp.float32(-1000000000.0))
    top_score = lax.optimization_barrier(jnp.max(scores, axis=-1, keepdims=True))
    expos = jnp.exp(scores - top_score)
    probs = (expos / lax.optimization_barrier(jnp.sum(expos, axis=-1, keepdims=True))).astype(jnp.bfloat16)
    attended = jnp.einsum('kgts,skd->tkgd', probs.astype(jnp.float32), value_blk.astype(jnp.float32)).astype(jnp.bfloat16)
    grad_values = jnp.einsum('kgts,tkgd->skd', probs.astype(jnp.float32), attended.astype(jnp.float32)).astype(jnp.bfloat16)
    return (attended, grad_values)

def reference(hidden_in, queries, keys, lengths, master, moment, second):
    weight = master.astype(jnp.bfloat16)
    values = jnp.dot(hidden_in, weight, preferred_element_type=jnp.float32).astype(jnp.bfloat16)
    blocks = lengths.shape[0]
    groups = QH // VH
    query_all = queries.reshape(blocks, TOK_DEV, VH, groups, HD)
    key_all = keys.reshape(blocks, TOK_DEV, VH, HD)
    value_all = values.reshape(blocks, TOK_DEV, VH, HD)
    attended, grad_values = lax.map(attend_block, (query_all, key_all, value_all, lengths))
    attended = attended.reshape(blocks * TOK_DEV, QH * HD)
    grad_values = grad_values.reshape(blocks * TOK_DEV, VH * HD)
    grad_hidden = jnp.dot(grad_values, weight.T, preferred_element_type=jnp.float32).astype(jnp.bfloat16)

    def add_block(total, operands):
        hidden_blk, grad_blk = operands
        partial_value = jnp.dot(hidden_blk.T, grad_blk, preferred_element_type=jnp.float32).astype(jnp.bfloat16)
        return (total + partial_value.astype(jnp.float32), None)
    start_total = jnp.zeros(master.shape, jnp.float32)
    summed, _ = lax.scan(add_block, start_total, (hidden_in.reshape(blocks, TOK_DEV, D), grad_values.reshape(blocks, TOK_DEV, VH * HD)))
    gradient = summed / jnp.float32(blocks * TOK_DEV)
    moment_new = beta_one * moment + (1.0 - beta_one) * gradient
    second_new = beta_two * second + (1.0 - beta_two) * gradient * gradient
    moment_hat = moment_new / (1.0 - beta_one ** 10)
    second_hat = second_new / (1.0 - beta_two ** 10)
    master_new = master - learn_rate * (moment_hat / (jnp.sqrt(second_hat) + adam_eps) + decay_rate * master)
    return (attended, grad_hidden, master_new, moment_new, second_new)
```

```python
import functools

import jax
import jax.numpy as jnp
import numpy as np
from jax import lax
from jax.experimental import pallas as pl
from jax.experimental.pallas import tpu as pltpu
from jax.sharding import Mesh
from jax.sharding import PartitionSpec as P

HD = 128
VH = 4
QH = 32
GROUPS = QH // VH

beta_one = 0.9
beta_two = 0.95
adam_eps = 1e-08
learn_rate = 0.001
decay_rate = 0.1

AXES = ("zl", "x", "c", "zh", "y")
SIZES = (4, 4, 2, 4, 4)
TOK_SPEC = P(AXES, None)
ROW_SPEC = P(("zh", "y", "zl", "x", "c"), None)
GROUP = ("x", "c")
DEPTH = ("zl", "zh")

F32 = jnp.float32
BF16 = jnp.bfloat16


def shuffle_matrix():
    source = np.arange(1024).reshape(4, 4, 8, 8).transpose(2, 1, 0, 3).reshape(-1)
    matrix = np.zeros((1024, 1024), np.float32)
    matrix[source, np.arange(1024)] = 1.0
    return matrix


def split_kernel(hidden_ref, shuffle_ref, out_ref):
    for y in range(4):
        parts = [hidden_ref[:, zh * 1024 + y * 256 : zh * 1024 + y * 256 + 256] for zh in range(4)]
        cols = jnp.concatenate(parts, axis=1)
        moved = jnp.dot(cols, shuffle_ref[...], preferred_element_type=F32).astype(BF16)
        for g in range(8):
            out_ref[g, :, y * 128 : (y + 1) * 128] = moved[:, g * 128 : (g + 1) * 128]


def join_kernel(blocks_ref, shuffle_ref, out_ref):
    for y in range(4):
        cols = jnp.concatenate([blocks_ref[g, :, y * 128 : (y + 1) * 128] for g in range(8)], axis=1)
        moved = lax.dot_general(
            cols, shuffle_ref[...], (((1,), (1,)), ((), ())), preferred_element_type=F32
        ).astype(BF16)
        for zh in range(4):
            at = zh * 1024 + y * 256
            out_ref[:, at : at + 256] = moved[:, zh * 256 : (zh + 1) * 256]


def probs_kernel(queries_ref, keys_ref, seg_row_ref, seg_col_ref, out_ref):
    tok = queries_ref.shape[0]
    rows = lax.broadcasted_iota(jnp.int32, (tok, tok), 0)
    cols = lax.broadcasted_iota(jnp.int32, (tok, tok), 1)
    allowed = (seg_col_ref[...] == seg_row_ref[...]) & (cols <= rows)
    scale = F32(1.0 / np.sqrt(HD))
    for j in range(VH):
        key = keys_ref[:, j * HD : (j + 1) * HD]
        for h in range(GROUPS):
            at = (j * GROUPS + h) * HD
            scores = lax.dot_general(
                queries_ref[:, at : at + HD], key, (((1,), (1,)), ((), ())), preferred_element_type=F32
            )
            scores = jnp.where(allowed, scores * scale, F32(-1000000000.0))
            expos = jnp.exp(scores - jnp.max(scores, axis=-1, keepdims=True))
            total = jnp.sum(expos, axis=-1, keepdims=True)
            out_ref[j, h * tok : (h + 1) * tok, :] = (expos / total).astype(BF16)


def attend_kernel(partial_ref, probs_ref, attended_ref, grad_ref):
    tok = partial_ref.shape[1]
    for j in range(VH):
        cols = slice(j * HD, (j + 1) * HD)
        total = partial_ref[0, :, cols].astype(F32)
        for g in range(1, 8):
            total = total + partial_ref[g, :, cols].astype(F32)
        value = total.astype(BF16)
        attended = jnp.dot(probs_ref[j], value, preferred_element_type=F32).astype(BF16)
        grad = lax.dot_general(
            probs_ref[j], attended, (((0,), (0,)), ((), ())), preferred_element_type=F32
        ).astype(BF16)
        for h in range(GROUPS):
            at = (j * GROUPS + h) * HD
            attended_ref[:, at : at + HD] = attended[h * tok : (h + 1) * tok]
        for g in range(8):
            grad_ref[g, :, cols] = grad


def call(kernel, out_shape, flops, nbytes):
    return pl.pallas_call(
        kernel,
        out_shape=out_shape,
        compiler_params=pltpu.CompilerParams(vmem_limit_bytes=48 * 1024 * 1024),
        cost_estimate=pl.CostEstimate(flops=flops, bytes_accessed=nbytes, transcendentals=0),
    )


def exchange(blocks, axes):
    return lax.all_to_all(blocks, axes, split_axis=0, concat_axis=0, tiled=True)


def per_device(hidden_in, queries, keys, lengths, master, moment, second):
    tok, width = hidden_in.shape
    kv = keys.shape[1]
    rows = master.shape[0]
    shuffle = jnp.asarray(shuffle_matrix(), BF16)

    blocks = call(
        split_kernel, jax.ShapeDtypeStruct((8, tok, width // 8), BF16), 2 * tok * width * 1024, 4 << 20
    )(hidden_in, shuffle)
    hidden = exchange(blocks, GROUP).reshape(8 * tok, width // 8)

    weight = master.astype(BF16)
    weight = exchange(jnp.broadcast_to(weight[None], (16, rows, kv)), DEPTH).reshape(16 * rows, kv)
    weight = exchange(jnp.broadcast_to(weight[None], (4, 16 * rows, kv)), "y").reshape(64 * rows, kv)

    ends = jnp.cumsum(lengths[0])
    seg = jnp.sum((jnp.arange(tok, dtype=jnp.int32)[:, None] >= ends[None, :]).astype(jnp.int32), axis=1)
    probs = call(
        probs_kernel, jax.ShapeDtypeStruct((VH, GROUPS * tok, tok), BF16), 4 * tok * tok * QH * HD, 8 << 20
    )(queries, keys, seg[None, :], seg[:, None])

    partial = jnp.dot(hidden, weight, preferred_element_type=F32).astype(BF16)
    partial = exchange(partial.reshape(8, tok, kv), GROUP)
    attended, grad = call(
        attend_kernel,
        (jax.ShapeDtypeStruct((tok, QH * HD), BF16), jax.ShapeDtypeStruct((8, tok, kv), BF16)),
        4 * tok * tok * QH * HD,
        4 << 20,
    )(partial, probs)
    grad = exchange(grad, GROUP).reshape(8 * tok, kv)

    part = lax.dot_general(hidden, grad, (((0,), (0,)), ((), ())), preferred_element_type=F32)
    part = exchange(part.astype(BF16).reshape(4, 16 * rows, kv), "y")
    part = jnp.sum(part.astype(F32), axis=0).astype(BF16)
    part = exchange(part.reshape(16, rows, kv), DEPTH)
    gradient = jnp.sum(part.astype(F32), axis=0) / F32(tok * 512)

    back = lax.dot_general(grad, weight, (((1,), (1,)), ((), ())), preferred_element_type=F32).astype(BF16)
    back = exchange(back.reshape(8, tok, width // 8), GROUP)
    grad_hidden = call(
        join_kernel, jax.ShapeDtypeStruct((tok, width), BF16), 2 * tok * width * 1024, 4 << 20
    )(back, shuffle)

    moment_new = beta_one * moment + (1.0 - beta_one) * gradient
    second_new = beta_two * second + (1.0 - beta_two) * gradient * gradient
    moment_hat = moment_new / (1.0 - beta_one**10)
    second_hat = second_new / (1.0 - beta_two**10)
    master_new = master - learn_rate * (
        moment_hat / (jnp.sqrt(second_hat) + adam_eps) + decay_rate * master
    )
    return (attended, grad_hidden, master_new, moment_new, second_new)


def solution(mesh):
    named = Mesh(mesh.devices.reshape(SIZES), AXES)
    return jax.shard_map(
        per_device,
        mesh=named,
        in_specs=(TOK_SPEC, TOK_SPEC, TOK_SPEC, TOK_SPEC, ROW_SPEC, ROW_SPEC, ROW_SPEC),
        out_specs=(TOK_SPEC, TOK_SPEC, ROW_SPEC, ROW_SPEC, ROW_SPEC),
        check_vma=False,
    )
```

```python
import jax
import jax.numpy as jnp
import numpy as np
from jax import lax
from jax.experimental import pallas as pl
from jax.experimental.pallas import tpu as pltpu
from jax.sharding import Mesh
from jax.sharding import PartitionSpec as P

HD = 128
VH = 4
QH = 32
GROUPS = QH // VH

beta_one = 0.9
beta_two = 0.95
adam_eps = 1e-08
learn_rate = 0.001
decay_rate = 0.1

AXES = ("zl", "x", "c", "zh", "y")
SIZES = (4, 4, 2, 4, 4)
TOK_SPEC = P(AXES, None)
ROW_SPEC = P(("zh", "y", "zl", "x", "c"), None)
DEPTH = ("zl", "zh")

F32 = jnp.float32
BF16 = jnp.bfloat16


def shuffle_matrix():
    source = np.arange(1024).reshape(4, 4, 4, 2, 8).transpose(3, 2, 1, 0, 4).reshape(-1)
    matrix = np.zeros((1024, 1024), np.float32)
    matrix[source, np.arange(1024)] = 1.0
    return matrix


def split_kernel(at_ref, hidden_ref, shuffle_ref, keep_ref, send_ref):
    first = at_ref[1] == 0
    for y in range(4):
        parts = [hidden_ref[:, zh * 1024 + y * 256 : zh * 1024 + y * 256 + 256] for zh in range(4)]
        cols = jnp.concatenate(parts, axis=1)
        moved = jnp.dot(cols, shuffle_ref[...], preferred_element_type=F32).astype(BF16)
        low, high = moved[:, :512], moved[:, 512:]
        keep, send = jnp.where(first, low, high), jnp.where(first, high, low)
        for x in range(4):
            keep_ref[x, :, y * 128 : (y + 1) * 128] = keep[:, x * 128 : (x + 1) * 128]
            send_ref[x, :, y * 128 : (y + 1) * 128] = send[:, x * 128 : (x + 1) * 128]


def deal_kernel(at_ref, own_ref, other_ref, *out_refs):
    for d in range(4):
        x = lax.rem(at_ref[0] + d, 4)
        out_refs[d][0] = own_ref[x]
        out_refs[d][1] = other_ref[x]


def collect_kernel(at_ref, *refs):
    in_refs, own_ref, other_ref = refs[:4], refs[4], refs[5]
    for d in range(4):
        x = lax.rem(at_ref[0] + 4 - d, 4)
        own_ref[x] = in_refs[d][0]
        other_ref[x] = in_refs[d][1]


def join_kernel(at_ref, b0_ref, b1_ref, b2_ref, b3_ref, shuffle_ref, out_ref, cols_ref):
    core = at_ref[1]
    for d, ref in enumerate((b0_ref, b1_ref, b2_ref, b3_ref)):
        x = lax.rem(at_ref[0] + 4 - d, 4)
        cols_ref[core, x] = ref[0]
        cols_ref[1 - core, x] = ref[1]
    for y in range(4):
        parts = [cols_ref[c, x, :, y * 128 : (y + 1) * 128] for c in range(2) for x in range(4)]
        moved = jnp.dot(
            jnp.concatenate(parts, axis=1), shuffle_ref[...], preferred_element_type=F32
        ).astype(BF16)
        for zh in range(4):
            at = zh * 1024 + y * 256
            out_ref[:, at : at + 256] = moved[:, zh * 256 : (zh + 1) * 256]


def probs_kernel(queries_ref, keys_ref, seg_row_ref, seg_col_ref, out_ref):
    tok = queries_ref.shape[0]
    rows = lax.broadcasted_iota(jnp.int32, (tok, tok), 0)
    cols = lax.broadcasted_iota(jnp.int32, (tok, tok), 1)
    allowed = (seg_col_ref[...] == seg_row_ref[...]) & (cols <= rows)
    scale = F32(1.0 / np.sqrt(HD))
    for j in range(VH):
        key = keys_ref[:, j * HD : (j + 1) * HD]
        for h in range(GROUPS):
            at = (j * GROUPS + h) * HD
            scores = lax.dot_general(
                queries_ref[:, at : at + HD], key, (((1,), (1,)), ((), ())), preferred_element_type=F32
            )
            scores = jnp.where(allowed, scores * scale, F32(-1000000000.0))
            expos = jnp.exp(scores - jnp.max(scores, axis=-1, keepdims=True))
            total = jnp.sum(expos, axis=-1, keepdims=True)
            out_ref[j, h * tok : (h + 1) * tok, :] = (expos / total).astype(BF16)


def attend_kernel(partial_ref, probs_ref, attended_ref, grad_ref):
    tok = partial_ref.shape[1]
    for j in range(VH):
        cols = slice(j * HD, (j + 1) * HD)
        total = partial_ref[0, :, cols].astype(F32)
        for x in range(1, 4):
            total = total + partial_ref[x, :, cols].astype(F32)
        value = total.astype(BF16)
        attended = jnp.dot(probs_ref[j], value, preferred_element_type=F32).astype(BF16)
        grad = lax.dot_general(
            probs_ref[j], attended, (((0,), (0,)), ((), ())), preferred_element_type=F32
        ).astype(BF16)
        for h in range(GROUPS):
            at = (j * GROUPS + h) * HD
            attended_ref[:, at : at + HD] = attended[h * tok : (h + 1) * tok]
        for x in range(4):
            grad_ref[x, :, cols] = grad


SMEM = pl.BlockSpec(memory_space=pltpu.SMEM)
VMEM = pl.BlockSpec(memory_space=pltpu.VMEM)


def call(kernel, out_shape, flops, nbytes, *args, scratch=()):
    smem = [SMEM if a.dtype == jnp.int32 and a.ndim == 1 else VMEM for a in args]
    return pl.pallas_call(
        kernel,
        out_shape=out_shape,
        in_specs=smem,
        scratch_shapes=scratch,
        compiler_params=pltpu.CompilerParams(vmem_limit_bytes=48 * 1024 * 1024),
        cost_estimate=pl.CostEstimate(flops=flops, bytes_accessed=nbytes, transcendentals=0),
    )(*args)


def swap_core(array):
    return lax.ppermute(array, "c", [(0, 1), (1, 0)])


def along_x(array, step):
    return lax.ppermute(array, "x", [(i, (i + step) % 4) for i in range(4)])


def exchange(blocks, axes):
    return lax.all_to_all(blocks, axes, split_axis=0, concat_axis=0, tiled=True)


def per_device(hidden_in, queries, keys, lengths, master, moment, second):
    tok, width = hidden_in.shape
    kv = keys.shape[1]
    rows = master.shape[0]
    feats = width // 8
    at = jnp.stack([lax.axis_index("x"), lax.axis_index("c")]).astype(jnp.int32)
    shuffle = shuffle_matrix()
    back_shuffle = jnp.asarray(shuffle.T, BF16)
    shuffle = jnp.asarray(shuffle, BF16)
    half = jax.ShapeDtypeStruct((4, tok, feats), BF16)
    pair = jax.ShapeDtypeStruct((2, tok, feats), BF16)

    weight = master.astype(BF16)
    weight = exchange(jnp.broadcast_to(weight[None], (16, rows, kv)), DEPTH).reshape(16 * rows, kv)
    weight = exchange(jnp.broadcast_to(weight[None], (4, 16 * rows, kv)), "y").reshape(64 * rows, kv)

    keep, send = call(split_kernel, (half, half), 2 * tok * width * 1024, 4 << 20, at, hidden_in, shuffle)
    dealt = call(deal_kernel, (pair,) * 4, 0, 2 << 20, at, keep, swap_core(send))
    dealt = [dealt[0]] + [along_x(dealt[d], d) for d in range(1, 4)]
    hidden_own, hidden_other = call(collect_kernel, (half, half), 0, 2 << 20, at, *dealt)
    hidden_own = hidden_own.reshape(4 * tok, feats)
    hidden_other = hidden_other.reshape(4 * tok, feats)

    ends = jnp.cumsum(lengths[0])
    seg = jnp.sum((jnp.arange(tok, dtype=jnp.int32)[:, None] >= ends[None, :]).astype(jnp.int32), axis=1)
    probs = call(
        probs_kernel,
        jax.ShapeDtypeStruct((VH, GROUPS * tok, tok), BF16),
        4 * tok * tok * QH * HD,
        8 << 20,
        queries,
        keys,
        seg[None, :],
        seg[:, None],
    )

    sent = swap_core(jnp.dot(hidden_other, weight, preferred_element_type=F32).astype(BF16))
    partial = jnp.dot(hidden_own, weight, preferred_element_type=F32) + sent.astype(F32)
    partial = exchange(partial.astype(BF16).reshape(4, tok, kv), "x")
    attended, grad = call(
        attend_kernel,
        (jax.ShapeDtypeStruct((tok, QH * HD), BF16), jax.ShapeDtypeStruct((4, tok, kv), BF16)),
        4 * tok * tok * QH * HD,
        4 << 20,
        partial,
        probs,
    )
    grad_own = exchange(grad, "x").reshape(4 * tok, kv)
    grad_other = swap_core(grad_own)

    rowwise = (((0,), (0,)), ((), ()))
    part = lax.dot_general(hidden_own, grad_own, rowwise, preferred_element_type=F32)
    part = part + lax.dot_general(hidden_other, grad_other, rowwise, preferred_element_type=F32)
    part = exchange(part.astype(BF16).reshape(4, 16 * rows, kv), "y")
    part = jnp.sum(part.astype(F32), axis=0).astype(BF16)
    part = exchange(part.reshape(16, rows, kv), DEPTH)
    gradient = jnp.sum(part.astype(F32), axis=0) / F32(tok * 512)

    columnwise = (((1,), (1,)), ((), ()))
    back_other = lax.dot_general(grad_other, weight, columnwise, preferred_element_type=F32).astype(BF16)
    back_own = lax.dot_general(grad_own, weight, columnwise, preferred_element_type=F32).astype(BF16)
    back_other = swap_core(back_other).reshape(4, tok, feats)
    dealt = call(deal_kernel, (pair,) * 4, 0, 2 << 20, at, back_own.reshape(4, tok, feats), back_other)
    dealt = [dealt[0]] + [along_x(dealt[d], d) for d in range(1, 4)]
    grad_hidden = call(
        join_kernel,
        jax.ShapeDtypeStruct((tok, width), BF16),
        2 * tok * width * 1024,
        4 << 20,
        at,
        *dealt,
        back_shuffle,
        scratch=[pltpu.VMEM((2, 4, tok, feats), BF16)],
    )

    moment_new = beta_one * moment + (1.0 - beta_one) * gradient
    second_new = beta_two * second + (1.0 - beta_two) * gradient * gradient
    moment_hat = moment_new / (1.0 - beta_one**10)
    second_hat = second_new / (1.0 - beta_two**10)
    master_new = master - learn_rate * (
        moment_hat / (jnp.sqrt(second_hat) + adam_eps) + decay_rate * master
    )
    return (attended, grad_hidden, master_new, moment_new, second_new)


def solution(mesh):
    named = Mesh(mesh.devices.reshape(SIZES), AXES)
    return jax.shard_map(
        per_device,
        mesh=named,
        in_specs=(TOK_SPEC, TOK_SPEC, TOK_SPEC, TOK_SPEC, ROW_SPEC, ROW_SPEC, ROW_SPEC),
        out_specs=(TOK_SPEC, TOK_SPEC, ROW_SPEC, ROW_SPEC, ROW_SPEC),
        check_vma=False,
    )
```

```python
import jax
import jax.numpy as jnp
import numpy as np
from jax import lax
from jax.experimental import pallas as pl
from jax.experimental.pallas import tpu as pltpu
from jax.sharding import Mesh
from jax.sharding import PartitionSpec as P

HD = 128
VH = 4
QH = 32
GROUPS = QH // VH

beta_one = 0.9
beta_two = 0.95
adam_eps = 1e-08
learn_rate = 0.001
decay_rate = 0.1

AXES = ("zl", "x", "c", "zh", "y")
SIZES = (4, 4, 2, 4, 4)
TOK_SPEC = P(AXES, None)
ROW_SPEC = P(("zh", "y", "zl", "x", "c"), None)
DEPTH = ("zl", "zh")
RING = 4

F32 = jnp.float32
BF16 = jnp.bfloat16


def order_matrix(core):
    to = lax.broadcasted_iota(jnp.int32, (1, 1024), 1)
    source = ((to >> 3) & 3) * 256 + ((to >> 5) & 3) * 64 + ((to >> 7) & 3) * 16 + (to & 7)
    source = source + ((to >> 9) ^ core) * 8
    hit = lax.broadcasted_iota(jnp.int32, (1024, 1024), 0) == source
    return jnp.where(hit, F32(1), F32(0)).astype(BF16)


WEIGHTY = 32 << 30


def spread_kernel(rows_ref, *refs):
    rows = rows_ref[...].astype(BF16)
    for i in range(refs[-1].shape[0]):
        refs[-1][i] = rows


def columns_of(y, zh):
    return pl.ds(pl.multiple_of(zh * 1024 + y * 256, 256), 256)


def deal_kernel(at_ref, hidden_ref, *out_refs):
    for d in range(RING):
        for zh in range(4):
            out_refs[d][:, zh * 256 : (zh + 1) * 256] = hidden_ref[:, columns_of(at_ref[0] ^ d, zh)]


def collect_kernel(at_ref, *refs):
    in_refs, own_ref, other_ref, matrix_ref = refs[:RING], refs[RING], refs[RING + 1], refs[RING + 2]
    matrix_ref[...] = order_matrix(at_ref[1])
    for d in range(RING):
        moved = jnp.dot(in_refs[d][...], matrix_ref[...], preferred_element_type=F32).astype(BF16)
        own_ref[at_ref[0] ^ d] = moved[:, :512]
        other_ref[at_ref[0] ^ d] = moved[:, 512:]


def turn_kernel(at_ref, own_ref, other_ref, out_ref):
    matrix = order_matrix(at_ref[1])
    contract = (((0,), (1,)), ((), ()))
    total = lax.dot_general(own_ref[...], matrix[:, :512], contract, preferred_element_type=F32)
    total = total + lax.dot_general(other_ref[...], matrix[:, 512:], contract, preferred_element_type=F32)
    out_ref[...] = total.astype(BF16)


def back_kernel(at_ref, grad_ref, weight_ref, *refs):
    out_refs, rows_ref = refs[:RING], refs[RING]
    tok = out_refs[0].shape[0]
    rows = jnp.dot(grad_ref[...], weight_ref[...], preferred_element_type=F32).astype(BF16)
    for y in range(RING):
        rows_ref[y] = rows[y * tok : (y + 1) * tok]
    for d in range(RING):
        out_refs[d][...] = rows_ref[at_ref[0] ^ d]


def join_kernel(at_ref, *refs):
    for d in range(RING):
        for zh in range(4):
            refs[RING][:, columns_of(at_ref[0] ^ d, zh)] = refs[d][:, zh * 256 : (zh + 1) * 256]


def sum_kernel(parts_ref, out_ref):
    total = parts_ref[0].astype(F32)
    for y in range(1, 4):
        total = total + parts_ref[y].astype(F32)
    total = total.astype(BF16)
    rows = out_ref.shape[1]
    for z in range(out_ref.shape[0]):
        out_ref[z] = total[z * rows : (z + 1) * rows]


def probs_kernel(queries_ref, keys_ref, seg_row_ref, seg_col_ref, out_ref):
    tok = queries_ref.shape[0]
    rows = lax.broadcasted_iota(jnp.int32, (tok, tok), 0)
    cols = lax.broadcasted_iota(jnp.int32, (tok, tok), 1)
    allowed = (seg_col_ref[...] == seg_row_ref[...]) & (cols <= rows)
    scale = F32(1.0 / np.sqrt(HD))
    for j in range(VH):
        key = keys_ref[:, j * HD : (j + 1) * HD]
        for h in range(GROUPS):
            at = (j * GROUPS + h) * HD
            scores = lax.dot_general(
                queries_ref[:, at : at + HD], key, (((1,), (1,)), ((), ())), preferred_element_type=F32
            )
            scores = jnp.where(allowed, scores * scale, F32(-1000000000.0))
            expos = jnp.exp(scores - jnp.max(scores, axis=-1, keepdims=True))
            total = jnp.sum(expos, axis=-1, keepdims=True)
            out_ref[j, h * tok : (h + 1) * tok, :] = (expos / total).astype(BF16)


def attend_kernel(partial_ref, probs_ref, attended_ref, grad_ref):
    tok = partial_ref.shape[1]
    for j in range(VH):
        cols = slice(j * HD, (j + 1) * HD)
        total = partial_ref[0, :, cols].astype(F32)
        for x in range(1, 4):
            total = total + partial_ref[x, :, cols].astype(F32)
        value = total.astype(BF16)
        attended = jnp.dot(probs_ref[j], value, preferred_element_type=F32).astype(BF16)
        grad = lax.dot_general(
            probs_ref[j], attended, (((0,), (0,)), ((), ())), preferred_element_type=F32
        ).astype(BF16)
        for h in range(GROUPS):
            at = (j * GROUPS + h) * HD
            attended_ref[:, at : at + HD] = attended[h * tok : (h + 1) * tok]
        for x in range(4):
            grad_ref[x, :, cols] = grad


SMEM = pl.BlockSpec(memory_space=pltpu.SMEM)
VMEM = pl.BlockSpec(memory_space=pltpu.VMEM)


def call(kernel, out_shape, flops, nbytes, *args, scratch=()):
    specs = [SMEM if a.dtype == jnp.int32 and a.ndim == 1 else VMEM for a in args]
    return pl.pallas_call(
        kernel,
        out_shape=out_shape,
        in_specs=specs,
        scratch_shapes=scratch,
        compiler_params=pltpu.CompilerParams(vmem_limit_bytes=24 * 1024 * 1024),
        cost_estimate=pl.CostEstimate(flops=flops, bytes_accessed=nbytes, transcendentals=0),
    )(*args)


def swap_core(array):
    return lax.ppermute(array, "c", [(0, 1), (1, 0)])


def along_y(blocks):
    moved = [lax.ppermute(blocks[d], "y", [(i, i ^ d) for i in range(RING)]) for d in range(1, RING)]
    return [blocks[0]] + moved


def exchange(blocks, axes):
    return lax.all_to_all(blocks, axes, split_axis=0, concat_axis=0, tiled=True)


def per_device(hidden_in, queries, keys, lengths, master, moment, second):
    tok, width = hidden_in.shape
    kv = keys.shape[1]
    rows = master.shape[0]
    feats = width // RING
    at = jnp.stack([lax.axis_index("y"), lax.axis_index("c")]).astype(jnp.int32)
    block = jax.ShapeDtypeStruct((tok, feats), BF16)
    half = jax.ShapeDtypeStruct((RING, tok, feats // 2), BF16)
    matrix = pltpu.VMEM((feats, feats), BF16)

    weight = call(spread_kernel, jax.ShapeDtypeStruct((16, rows, kv), BF16), 0, 1 << 17, master)
    weight = exchange(weight, DEPTH).reshape(16 * rows, kv)

    dealt = along_y(call(deal_kernel, (block,) * RING, 0, 2 << 20, at, hidden_in))
    hidden_own, hidden_other = call(
        collect_kernel, (half, half), WEIGHTY, 3 << 20, at, *dealt, scratch=[matrix]
    )

    weight = call(spread_kernel, jax.ShapeDtypeStruct((RING, 16 * rows, kv), BF16), 0, 1 << 19, weight)
    weight = exchange(weight, "x").reshape(RING * 16 * rows, kv)
    weight, hidden_own, hidden_other = lax.optimization_barrier((weight, hidden_own, hidden_other))
    weight_other = swap_core(weight)
    hidden_own = hidden_own.reshape(RING * tok, feats // 2)
    hidden_other = hidden_other.reshape(RING * tok, feats // 2)

    ends = jnp.cumsum(lengths[0])
    seg = jnp.sum((jnp.arange(tok, dtype=jnp.int32)[:, None] >= ends[None, :]).astype(jnp.int32), axis=1)
    probs = call(
        probs_kernel,
        jax.ShapeDtypeStruct((VH, GROUPS * tok, tok), BF16),
        4 * tok * tok * QH * HD,
        8 << 20,
        queries,
        keys,
        seg[None, :],
        seg[:, None],
    )

    partial = jnp.dot(hidden_own, weight, preferred_element_type=F32)
    partial = partial + jnp.dot(hidden_other, weight_other, preferred_element_type=F32)
    partial = exchange(partial.astype(BF16).reshape(RING, tok, kv), "y")
    attended, grad = call(
        attend_kernel,
        (jax.ShapeDtypeStruct((tok, QH * HD), BF16), jax.ShapeDtypeStruct((RING, tok, kv), BF16)),
        4 * tok * tok * QH * HD,
        4 << 20,
        partial,
        probs,
    )
    weight_cols = call(
        turn_kernel, jax.ShapeDtypeStruct((kv, feats), BF16), 2 * feats * feats * kv, 3 << 20, at, weight, weight_other
    )
    grad = exchange(grad, "y").reshape(RING * tok, kv)
    grad, weight_cols = lax.optimization_barrier((grad, weight_cols))

    rowwise = (((0,), (0,)), ((), ()))
    part = swap_core(
        lax.dot_general(hidden_other, grad, rowwise, preferred_element_type=F32).astype(BF16)
    ).astype(F32)
    part = part + lax.dot_general(hidden_own, grad, rowwise, preferred_element_type=F32)
    part = part.astype(BF16).reshape(RING, 16 * rows, kv)

    dealt = call(
        back_kernel,
        (block,) * RING,
        2 * RING * tok * feats * kv,
        3 << 20,
        at,
        grad,
        weight_cols,
        scratch=[pltpu.VMEM((RING, tok, feats), BF16)],
    )
    part, dealt = lax.optimization_barrier((part, dealt))
    dealt = along_y(dealt)
    grad_hidden = call(
        join_kernel, jax.ShapeDtypeStruct((tok, width), BF16), WEIGHTY, 2 << 20, at, *dealt
    )

    part = exchange(part, "x")
    part = call(sum_kernel, jax.ShapeDtypeStruct((16, rows, kv), BF16), 0, 1 << 20, part)
    part = exchange(part, DEPTH)
    gradient = jnp.sum(part.astype(F32), axis=0) / F32(tok * 512)

    moment_new = beta_one * moment + (1.0 - beta_one) * gradient
    second_new = beta_two * second + (1.0 - beta_two) * gradient * gradient
    moment_hat = moment_new / (1.0 - beta_one**10)
    second_hat = second_new / (1.0 - beta_two**10)
    master_new = master - learn_rate * (
        moment_hat / (jnp.sqrt(second_hat) + adam_eps) + decay_rate * master
    )
    return (attended, grad_hidden, master_new, moment_new, second_new)


def solution(mesh):
    named = Mesh(mesh.devices.reshape(SIZES), AXES)
    return jax.shard_map(
        per_device,
        mesh=named,
        in_specs=(TOK_SPEC, TOK_SPEC, TOK_SPEC, TOK_SPEC, ROW_SPEC, ROW_SPEC, ROW_SPEC),
        out_specs=(TOK_SPEC, TOK_SPEC, ROW_SPEC, ROW_SPEC, ROW_SPEC),
        check_vma=False,
    )
```

```python
import jax
import jax.numpy as jnp
import numpy as np
from jax import lax
from jax.experimental import pallas as pl
from jax.experimental.pallas import tpu as pltpu
from jax.sharding import Mesh
from jax.sharding import PartitionSpec as P

HD = 128
VH = 4
QH = 32
GROUPS = QH // VH

beta_one = 0.9
beta_two = 0.95
adam_eps = 1e-08
learn_rate = 0.001
decay_rate = 0.1

AXES = ("zl", "x", "c", "zh", "y")
SIZES = (4, 4, 2, 4, 4)
TOK_SPEC = P(AXES, None)
ROW_SPEC = P(("zh", "y", "zl", "x", "c"), None)
DEPTH = ("zl", "zh")
RING = 4

F32 = jnp.float32
BF16 = jnp.bfloat16


def order_matrix(core):
    to = lax.broadcasted_iota(jnp.int32, (1, 1024), 1)
    source = ((to >> 3) & 3) * 256 + ((to >> 5) & 3) * 64 + ((to >> 7) & 3) * 16 + (to & 7)
    source = source + ((to >> 9) ^ core) * 8
    hit = lax.broadcasted_iota(jnp.int32, (1024, 1024), 0) == source
    return jnp.where(hit, F32(1), F32(0)).astype(BF16)


WEIGHTY = 32 << 30


def spread_kernel(rows_ref, *refs):
    rows = rows_ref[...].astype(BF16)
    for i in range(refs[-1].shape[0]):
        refs[-1][i] = rows


def columns_of(y, zh):
    return pl.ds(pl.multiple_of(zh * 1024 + y * 256, 256), 256)


def deal_kernel(at_ref, hidden_ref, *out_refs):
    for d in range(RING):
        for zh in range(4):
            out_refs[d][:, zh * 256 : (zh + 1) * 256] = hidden_ref[:, columns_of(at_ref[0] ^ d, zh)]


def collect_kernel(at_ref, *refs):
    in_refs, own_ref, other_ref, matrix_ref = refs[:RING], refs[RING], refs[RING + 1], refs[RING + 2]
    matrix_ref[...] = order_matrix(at_ref[1])
    for d in range(RING):
        moved = jnp.dot(in_refs[d][...], matrix_ref[...], preferred_element_type=F32).astype(BF16)
        own_ref[at_ref[0] ^ d] = moved[:, :512]
        other_ref[at_ref[0] ^ d] = moved[:, 512:]


def turn_kernel(at_ref, own_ref, other_ref, out_ref):
    matrix = order_matrix(at_ref[1])
    contract = (((0,), (1,)), ((), ()))
    total = lax.dot_general(own_ref[...], matrix[:, :512], contract, preferred_element_type=F32)
    total = total + lax.dot_general(other_ref[...], matrix[:, 512:], contract, preferred_element_type=F32)
    out_ref[...] = total.astype(BF16)


def back_kernel(at_ref, grad_ref, weight_ref, *refs):
    out_refs, rows_ref = refs[:RING], refs[RING]
    tok = out_refs[0].shape[0]
    rows = jnp.dot(grad_ref[...], weight_ref[...], preferred_element_type=F32).astype(BF16)
    for y in range(RING):
        rows_ref[y] = rows[y * tok : (y + 1) * tok]
    for d in range(RING):
        out_refs[d][...] = rows_ref[at_ref[0] ^ d]


def join_kernel(steps, at_ref, *refs):
    out_ref, sem_ref = refs[-2], refs[-1]
    copies = []
    for i, d in enumerate(steps):
        for zh in range(4):
            copies.append(
                pltpu.make_async_copy(
                    refs[i].at[:, zh * 256 : (zh + 1) * 256],
                    out_ref.at[:, columns_of(at_ref[0] ^ d, zh)],
                    sem_ref.at[i * 4 + zh],
                )
            )
    for copy in copies:
        copy.start()
    for copy in copies:
        copy.wait()


def join(steps, at, blocks, shape, flops, into=()):
    def kernel(at_ref, *refs):
        join_kernel(steps, at_ref, *refs[: len(steps)], refs[-2], refs[-1])

    return pl.pallas_call(
        kernel,
        out_shape=shape,
        in_specs=[SMEM] + [VMEM] * len(steps) + [ANY] * len(into),
        out_specs=ANY,
        scratch_shapes=[pltpu.SemaphoreType.DMA((4 * len(steps),))],
        input_output_aliases={1 + len(steps): 0} if into else {},
        compiler_params=pltpu.CompilerParams(vmem_limit_bytes=24 * 1024 * 1024),
        cost_estimate=pl.CostEstimate(flops=flops, bytes_accessed=1 << 20, transcendentals=0),
    )(at, *blocks, *into)


def values_kernel(own_ref, other_ref, weight_ref, weight_other_ref, out_ref):
    tok = out_ref.shape[1]
    for y in range(RING):
        rows = slice(y * tok, (y + 1) * tok)
        total = jnp.dot(own_ref[rows], weight_ref[...], preferred_element_type=F32)
        total = total + jnp.dot(other_ref[rows], weight_other_ref[...], preferred_element_type=F32)
        out_ref[y] = total.astype(BF16)


def sum_kernel(parts_ref, out_ref):
    total = parts_ref[0].astype(F32)
    for y in range(1, 4):
        total = total + parts_ref[y].astype(F32)
    total = total.astype(BF16)
    rows = out_ref.shape[1]
    for z in range(out_ref.shape[0]):
        out_ref[z] = total[z * rows : (z + 1) * rows]


def probs_kernel(queries_ref, keys_ref, seg_row_ref, seg_col_ref, out_ref):
    tok = queries_ref.shape[0]
    rows = lax.broadcasted_iota(jnp.int32, (tok, tok), 0)
    cols = lax.broadcasted_iota(jnp.int32, (tok, tok), 1)
    allowed = (seg_col_ref[...] == seg_row_ref[...]) & (cols <= rows)
    scale = F32(1.0 / np.sqrt(HD))
    for j in range(VH):
        key = keys_ref[:, j * HD : (j + 1) * HD]
        for h in range(GROUPS):
            at = (j * GROUPS + h) * HD
            scores = lax.dot_general(
                queries_ref[:, at : at + HD], key, (((1,), (1,)), ((), ())), preferred_element_type=F32
            )
            scores = jnp.where(allowed, scores * scale, F32(-1000000000.0))
            expos = jnp.exp(scores - jnp.max(scores, axis=-1, keepdims=True))
            total = jnp.sum(expos, axis=-1, keepdims=True)
            out_ref[j, h * tok : (h + 1) * tok, :] = (expos / total).astype(BF16)


def attend_kernel(partial_ref, probs_ref, attended_ref, grad_ref):
    tok = partial_ref.shape[1]
    for j in range(VH):
        cols = slice(j * HD, (j + 1) * HD)
        total = partial_ref[0, :, cols].astype(F32)
        for x in range(1, 4):
            total = total + partial_ref[x, :, cols].astype(F32)
        value = total.astype(BF16)
        attended = jnp.dot(probs_ref[j], value, preferred_element_type=F32).astype(BF16)
        grad = lax.dot_general(
            probs_ref[j], attended, (((0,), (0,)), ((), ())), preferred_element_type=F32
        ).astype(BF16)
        for h in range(GROUPS):
            at = (j * GROUPS + h) * HD
            attended_ref[:, at : at + HD] = attended[h * tok : (h + 1) * tok]
        for x in range(4):
            grad_ref[x, :, cols] = grad


SMEM = pl.BlockSpec(memory_space=pltpu.SMEM)
VMEM = pl.BlockSpec(memory_space=pltpu.VMEM)
ANY = pl.BlockSpec(memory_space=pl.ANY)


def call(kernel, out_shape, flops, nbytes, *args, scratch=()):
    specs = [SMEM if a.dtype == jnp.int32 and a.ndim == 1 else VMEM for a in args]
    return pl.pallas_call(
        kernel,
        out_shape=out_shape,
        in_specs=specs,
        scratch_shapes=scratch,
        compiler_params=pltpu.CompilerParams(vmem_limit_bytes=24 * 1024 * 1024),
        cost_estimate=pl.CostEstimate(flops=flops, bytes_accessed=nbytes, transcendentals=0),
    )(*args)


def swap_core(array):
    return lax.ppermute(array, "c", [(0, 1), (1, 0)])


def along_y(block, d):
    return lax.ppermute(block, "y", [(i, i ^ d) for i in range(RING)])


def exchange(blocks, axes):
    return lax.all_to_all(blocks, axes, split_axis=0, concat_axis=0, tiled=True)


def per_device(hidden_in, queries, keys, lengths, master, moment, second):
    tok, width = hidden_in.shape
    kv = keys.shape[1]
    rows = master.shape[0]
    feats = width // RING
    at = jnp.stack([lax.axis_index("y"), lax.axis_index("c")]).astype(jnp.int32)
    block = jax.ShapeDtypeStruct((tok, feats), BF16)
    half = jax.ShapeDtypeStruct((RING, tok, feats // 2), BF16)
    matrix = pltpu.VMEM((feats, feats), BF16)

    weight = call(spread_kernel, jax.ShapeDtypeStruct((16, rows, kv), BF16), 0, 1 << 17, master)
    weight = exchange(weight, DEPTH).reshape(16 * rows, kv)

    dealt = call(deal_kernel, (block,) * RING, 0, 2 << 20, at, hidden_in)
    dealt = [dealt[0]] + [along_y(dealt[d], d) for d in range(1, RING)]
    hidden_own, hidden_other = call(
        collect_kernel, (half, half), WEIGHTY, 3 << 20, at, *dealt, scratch=[matrix]
    )

    weight = call(spread_kernel, jax.ShapeDtypeStruct((RING, 16 * rows, kv), BF16), 0, 1 << 19, weight)
    weight = exchange(weight, "x").reshape(RING * 16 * rows, kv)
    weight, hidden_own, hidden_other = lax.optimization_barrier((weight, hidden_own, hidden_other))
    weight_other = swap_core(weight)
    hidden_own = hidden_own.reshape(RING * tok, feats // 2)
    hidden_other = hidden_other.reshape(RING * tok, feats // 2)

    ends = jnp.cumsum(lengths[0])
    seg = jnp.sum((jnp.arange(tok, dtype=jnp.int32)[:, None] >= ends[None, :]).astype(jnp.int32), axis=1)
    probs = call(
        probs_kernel,
        jax.ShapeDtypeStruct((VH, GROUPS * tok, tok), BF16),
        4 * tok * tok * QH * HD,
        8 << 20,
        queries,
        keys,
        seg[None, :],
        seg[:, None],
    )

    partial = call(
        values_kernel,
        jax.ShapeDtypeStruct((RING, tok, kv), BF16),
        2 * RING * tok * feats * kv,
        3 << 20,
        hidden_own,
        hidden_other,
        weight,
        weight_other,
    )
    partial = exchange(partial, "y")
    attended, grad = call(
        attend_kernel,
        (jax.ShapeDtypeStruct((tok, QH * HD), BF16), jax.ShapeDtypeStruct((RING, tok, kv), BF16)),
        4 * tok * tok * QH * HD,
        4 << 20,
        partial,
        probs,
    )
    weight_cols = call(
        turn_kernel, jax.ShapeDtypeStruct((kv, feats), BF16), 2 * feats * feats * kv, 3 << 20, at, weight, weight_other
    )
    grad = exchange(grad, "y").reshape(RING * tok, kv)
    grad, weight_cols = lax.optimization_barrier((grad, weight_cols))

    rowwise = (((0,), (0,)), ((), ()))
    part = swap_core(
        lax.dot_general(hidden_other, grad, rowwise, preferred_element_type=F32).astype(BF16)
    ).astype(F32)
    part = part + lax.dot_general(hidden_own, grad, rowwise, preferred_element_type=F32)
    part = part.astype(BF16).reshape(RING, 16 * rows, kv)

    dealt = call(
        back_kernel,
        (block,) * RING,
        2 * RING * tok * feats * kv,
        3 << 20,
        at,
        grad,
        weight_cols,
        scratch=[pltpu.VMEM((RING, tok, feats), BF16)],
    )
    part, dealt = lax.optimization_barrier((part, dealt))
    near = [dealt[0], along_y(dealt[2], 2), along_y(dealt[1], 1)]
    whole = jax.ShapeDtypeStruct((tok, width), BF16)
    grad_hidden = join((0, 2, 1), at, near, whole, WEIGHTY)

    part = exchange(part, "x")
    part = call(sum_kernel, jax.ShapeDtypeStruct((16, rows, kv), BF16), 0, 1 << 20, part)
    part, last = lax.optimization_barrier((part, dealt[3]))
    part = exchange(part, DEPTH)
    grad_hidden = join((3,), at, [along_y(last, 3)], whole, 0, [grad_hidden])
    gradient = jnp.sum(part.astype(F32), axis=0) / F32(tok * 512)

    moment_new = beta_one * moment + (1.0 - beta_one) * gradient
    second_new = beta_two * second + (1.0 - beta_two) * gradient * gradient
    moment_hat = moment_new / (1.0 - beta_one**10)
    second_hat = second_new / (1.0 - beta_two**10)
    master_new = master - learn_rate * (
        moment_hat / (jnp.sqrt(second_hat) + adam_eps) + decay_rate * master
    )
    return (attended, grad_hidden, master_new, moment_new, second_new)


def solution(mesh):
    named = Mesh(mesh.devices.reshape(SIZES), AXES)
    return jax.shard_map(
        per_device,
        mesh=named,
        in_specs=(TOK_SPEC, TOK_SPEC, TOK_SPEC, TOK_SPEC, ROW_SPEC, ROW_SPEC, ROW_SPEC),
        out_specs=(TOK_SPEC, TOK_SPEC, ROW_SPEC, ROW_SPEC, ROW_SPEC),
        check_vma=False,
    )
```

```python
import jax
import jax.numpy as jnp
import numpy as np
from jax import lax
from jax.experimental import pallas as pl
from jax.experimental.pallas import tpu as pltpu
from jax.sharding import Mesh
from jax.sharding import PartitionSpec as P

HD = 128
VH = 4
QH = 32
GROUPS = QH // VH

beta_one = 0.9
beta_two = 0.95
adam_eps = 1e-08
learn_rate = 0.001
decay_rate = 0.1

AXES = ("zl", "x", "c", "zh", "y")
SIZES = (4, 4, 2, 4, 4)
TOK_SPEC = P(AXES, None)
ROW_SPEC = P(("zh", "y", "zl", "x", "c"), None)
DEPTH = 16
RING = 4
GATHER_FIRST = 3
REDUCE_FIRST = 6

F32 = jnp.float32
BF16 = jnp.bfloat16


def order_matrix(core):
    to = lax.broadcasted_iota(jnp.int32, (1, 1024), 1)
    z = ((to >> 3) & 15) ^ GATHER_FIRST
    source = (z & 3) * 256 + (z >> 2) * 64 + ((to >> 7) & 3) * 16 + (to & 7)
    source = source + ((to >> 9) ^ core) * 8
    hit = lax.broadcasted_iota(jnp.int32, (1024, 1024), 0) == source
    return jnp.where(hit, F32(1), F32(0)).astype(BF16)


WEIGHTY = 32 << 30


def run_copies(sem_ref, pairs):
    copies = [pltpu.make_async_copy(a, b, sem_ref.at[i]) for i, (a, b) in enumerate(pairs)]
    for copy in copies:
        copy.start()
    for copy in copies:
        copy.wait()


def master_kernel(master_ref, out_ref, rows_ref, sem_ref):
    run_copies(sem_ref, [(master_ref, rows_ref)])
    weight = rows_ref[...].astype(BF16)
    for z in range(DEPTH):
        out_ref[z] = weight


def spread_kernel(rows_ref, out_ref, sem_ref):
    run_copies(sem_ref, [(rows_ref, out_ref.at[i]) for i in range(RING)])


def columns_of(y, zh):
    return pl.ds(pl.multiple_of(zh * 1024 + y * 256, 256), 256)


def block_columns(at_ref, blocks, whole_ref):
    return [
        (blocks[d].at[:, zh * 256 : (zh + 1) * 256], whole_ref.at[:, columns_of(at_ref[0] ^ d, zh)])
        for d in range(RING)
        for zh in range(4)
    ]


def deal_kernel(at_ref, hidden_ref, *refs):
    run_copies(refs[RING], [(b, a) for a, b in block_columns(at_ref, refs[:RING], hidden_ref)])


def join_kernel(at_ref, *refs):
    run_copies(refs[RING + 1], block_columns(at_ref, refs[:RING], refs[RING]))


def collect_kernel(at_ref, *refs):
    in_refs, own_ref, other_ref, matrix_ref = refs[:RING], refs[RING], refs[RING + 1], refs[RING + 2]
    matrix_ref[...] = order_matrix(at_ref[1])
    for d in range(RING):
        moved = jnp.dot(in_refs[d][...], matrix_ref[...], preferred_element_type=F32).astype(BF16)
        own_ref[at_ref[0] ^ d] = moved[:, :512]
        other_ref[at_ref[0] ^ d] = moved[:, 512:]


def turn_kernel(at_ref, own_ref, other_ref, out_ref):
    matrix = order_matrix(at_ref[1])
    contract = (((0,), (1,)), ((), ()))
    total = lax.dot_general(own_ref[...], matrix[:, :512], contract, preferred_element_type=F32)
    total = total + lax.dot_general(other_ref[...], matrix[:, 512:], contract, preferred_element_type=F32)
    out_ref[...] = total.astype(BF16)


def back_kernel(at_ref, grad_ref, weight_ref, *refs):
    out_refs, rows_ref = refs[:RING], refs[RING]
    tok = out_refs[0].shape[0]
    rows = jnp.dot(grad_ref[...], weight_ref[...], preferred_element_type=F32).astype(BF16)
    for y in range(RING):
        rows_ref[y] = rows[y * tok : (y + 1) * tok]
    for d in range(RING):
        out_refs[d][...] = rows_ref[at_ref[0] ^ d]


def values_kernel(own_ref, other_ref, weight_ref, weight_other_ref, out_ref, rows_ref, sem_ref):
    tok = out_ref.shape[1]
    copies = []
    for y in range(RING):
        rows = slice(y * tok, (y + 1) * tok)
        total = jnp.dot(own_ref[rows], weight_ref[...], preferred_element_type=F32)
        total = total + jnp.dot(other_ref[rows], weight_other_ref[...], preferred_element_type=F32)
        rows_ref[y] = total.astype(BF16)
        copies.append(pltpu.make_async_copy(rows_ref.at[y], out_ref.at[y], sem_ref.at[y]))
        copies[-1].start()
    for copy in copies:
        copy.wait()


def fold_kernel(own_ref, grad_ref, sent_ref, out_ref, rows_ref, sem_ref):
    copies = []
    step = out_ref.shape[1]
    for x in range(RING):
        at = slice(x * step, (x + 1) * step)
        part = lax.dot_general(own_ref[:, at], grad_ref[...], (((0,), (0,)), ((), ())), preferred_element_type=F32)
        rows_ref[x] = (part + sent_ref[at].astype(F32)).astype(BF16)
        copies.append(pltpu.make_async_copy(rows_ref.at[x], out_ref.at[x], sem_ref.at[x]))
        copies[-1].start()
    for copy in copies:
        copy.wait()


def sum_kernel(parts_ref, out_ref):
    total = parts_ref[0].astype(F32)
    for y in range(1, 4):
        total = total + parts_ref[y].astype(F32)
    total = total.astype(BF16)
    rows = out_ref.shape[1]
    for z in range(out_ref.shape[0]):
        out_ref[z ^ GATHER_FIRST ^ REDUCE_FIRST] = total[z * rows : (z + 1) * rows]


def probs_kernel(queries_ref, keys_ref, seg_row_ref, seg_col_ref, out_ref):
    tok = queries_ref.shape[0]
    rows = lax.broadcasted_iota(jnp.int32, (tok, tok), 0)
    cols = lax.broadcasted_iota(jnp.int32, (tok, tok), 1)
    allowed = (seg_col_ref[...] == seg_row_ref[...]) & (cols <= rows)
    scale = F32(1.0 / np.sqrt(HD))
    for j in range(VH):
        key = keys_ref[:, j * HD : (j + 1) * HD]
        for h in range(GROUPS):
            at = (j * GROUPS + h) * HD
            scores = lax.dot_general(
                queries_ref[:, at : at + HD], key, (((1,), (1,)), ((), ())), preferred_element_type=F32
            )
            scores = jnp.where(allowed, scores * scale, F32(-1000000000.0))
            expos = jnp.exp(scores - jnp.max(scores, axis=-1, keepdims=True))
            total = jnp.sum(expos, axis=-1, keepdims=True)
            out_ref[j, h * tok : (h + 1) * tok, :] = (expos / total).astype(BF16)


def attend_kernel(partial_ref, probs_ref, attended_ref, grad_ref, rows_ref, sum_ref, sem_ref):
    tok = partial_ref.shape[1]
    wide = GROUPS * HD
    copies = []
    for j in range(VH):
        cols = slice(j * HD, (j + 1) * HD)
        total = partial_ref[0, :, cols].astype(F32)
        for y in range(1, RING):
            total = total + partial_ref[y, :, cols].astype(F32)
        value = total.astype(BF16)
        attended = jnp.dot(probs_ref[j], value, preferred_element_type=F32).astype(BF16)
        for h in range(GROUPS):
            rows_ref[j, :, h * HD : (h + 1) * HD] = attended[h * tok : (h + 1) * tok]
        copies.append(
            pltpu.make_async_copy(rows_ref.at[j], attended_ref.at[:, j * wide : (j + 1) * wide], sem_ref.at[j])
        )
        copies[-1].start()
        sum_ref[:, cols] = lax.dot_general(
            probs_ref[j], attended, (((0,), (0,)), ((), ())), preferred_element_type=F32
        ).astype(BF16)
    for y in range(RING):
        copies.append(pltpu.make_async_copy(sum_ref, grad_ref.at[y], sem_ref.at[VH + y]))
        copies[-1].start()
    for copy in copies:
        copy.wait()


SMEM = pl.BlockSpec(memory_space=pltpu.SMEM)
VMEM = pl.BlockSpec(memory_space=pltpu.VMEM)
HBM = pl.BlockSpec(memory_space=pltpu.HBM)


def copies(n):
    return pltpu.SemaphoreType.DMA((n,))


def call(kernel, out_shape, flops, nbytes, *args, scratch=(), out=VMEM, hbm=()):
    specs = [SMEM if a.dtype == jnp.int32 and a.ndim == 1 else VMEM for a in args]
    specs = [HBM if i in hbm else spec for i, spec in enumerate(specs)]
    args = [pltpu.with_memory_space_constraint(a, pltpu.HBM) if i in hbm else a for i, a in enumerate(args)]
    return pl.pallas_call(
        kernel,
        out_shape=out_shape,
        in_specs=specs,
        out_specs=(out,) * len(out_shape) if isinstance(out_shape, tuple) else out,
        scratch_shapes=scratch,
        compiler_params=pltpu.CompilerParams(vmem_limit_bytes=24 * 1024 * 1024),
        cost_estimate=pl.CostEstimate(flops=flops, bytes_accessed=nbytes, transcendentals=0),
    )(*args)


def swap_core(array):
    return lax.ppermute(array, "c", [(0, 1), (1, 0)])


def along_y(block, d):
    return lax.ppermute(block, "y", [(i, i ^ d) for i in range(RING)])


def exchange(blocks, axes):
    return lax.all_to_all(blocks, axes, split_axis=0, concat_axis=0, tiled=True)


def exchange_z(blocks, first):
    ids = np.arange(np.prod(SIZES)).reshape(SIZES).transpose(1, 2, 4, 0, 3).reshape(-1, DEPTH)
    groups = ids[:, np.arange(DEPTH) ^ first].tolist()
    return lax.all_to_all(blocks, AXES, split_axis=0, concat_axis=0, axis_index_groups=groups, tiled=True)


def per_device(hidden_in, queries, keys, lengths, master, moment, second):
    tok, width = hidden_in.shape
    kv = keys.shape[1]
    rows = master.shape[0]
    feats = width // RING
    at = jnp.stack([lax.axis_index("y"), lax.axis_index("c")]).astype(jnp.int32)
    block = jax.ShapeDtypeStruct((tok, feats), BF16)
    half = jax.ShapeDtypeStruct((RING, tok, feats // 2), BF16)
    matrix = pltpu.VMEM((feats, feats), BF16)

    weight = call(
        master_kernel,
        jax.ShapeDtypeStruct((DEPTH, rows, kv), BF16),
        0,
        1 << 17,
        master,
        scratch=[pltpu.VMEM((rows, kv), F32), copies(1)],
        hbm=(0,),
    )
    weight = exchange_z(weight, GATHER_FIRST).reshape(DEPTH * rows, kv)

    dealt = call(
        deal_kernel, (block,) * RING, 0, 2 << 20, at, hidden_in, scratch=[copies(4 * RING)], hbm=(1,)
    )
    dealt = [dealt[0]] + [along_y(dealt[d], d) for d in range(1, RING)]
    hidden_own, hidden_other = call(
        collect_kernel, (half, half), WEIGHTY, 3 << 20, at, *dealt, scratch=[matrix]
    )

    weight = call(
        spread_kernel,
        jax.ShapeDtypeStruct((RING, DEPTH * rows, kv), BF16),
        0,
        1 << 19,
        weight,
        scratch=[copies(RING)],
        out=HBM,
    )
    weight = exchange(weight, "x").reshape(RING * DEPTH * rows, kv)
    weight, hidden_own, hidden_other = lax.optimization_barrier((weight, hidden_own, hidden_other))
    weight_other = swap_core(weight)
    hidden_own = hidden_own.reshape(RING * tok, feats // 2)
    hidden_other = hidden_other.reshape(RING * tok, feats // 2)

    ends = jnp.cumsum(lengths[0])
    seg = jnp.sum((jnp.arange(tok, dtype=jnp.int32)[:, None] >= ends[None, :]).astype(jnp.int32), axis=1)
    probs = call(
        probs_kernel,
        jax.ShapeDtypeStruct((VH, GROUPS * tok, tok), BF16),
        4 * tok * tok * QH * HD,
        8 << 20,
        queries,
        keys,
        seg[None, :],
        seg[:, None],
    )

    partial = call(
        values_kernel,
        jax.ShapeDtypeStruct((RING, tok, kv), BF16),
        2 * RING * tok * feats * kv,
        3 << 20,
        hidden_own,
        hidden_other,
        weight,
        weight_other,
        scratch=[pltpu.VMEM((RING, tok, kv), BF16), copies(RING)],
        out=HBM,
    )
    partial = exchange(partial, "y")
    attended, grad = call(
        attend_kernel,
        (jax.ShapeDtypeStruct((tok, QH * HD), BF16), jax.ShapeDtypeStruct((RING, tok, kv), BF16)),
        4 * tok * tok * QH * HD,
        4 << 20,
        partial,
        probs,
        scratch=[pltpu.VMEM((VH, tok, GROUPS * HD), BF16), pltpu.VMEM((tok, kv), BF16), copies(VH + RING)],
        out=HBM,
    )
    weight_cols = call(
        turn_kernel, jax.ShapeDtypeStruct((kv, feats), BF16), 2 * feats * feats * kv, 3 << 20, at, weight, weight_other
    )
    grad = exchange(grad, "y").reshape(RING * tok, kv)
    grad, weight_cols = lax.optimization_barrier((grad, weight_cols))

    rowwise = (((0,), (0,)), ((), ()))
    sent = lax.dot_general(hidden_other, grad, rowwise, preferred_element_type=F32).astype(BF16)
    part = call(
        fold_kernel,
        jax.ShapeDtypeStruct((RING, DEPTH * rows, kv), BF16),
        2 * RING * tok * feats * kv // 2,
        2 << 20,
        hidden_own,
        grad,
        swap_core(sent),
        scratch=[pltpu.VMEM((RING, DEPTH * rows, kv), BF16), copies(RING)],
        out=HBM,
    )

    dealt = call(
        back_kernel,
        (block,) * RING,
        2 * RING * tok * feats * kv,
        3 << 20,
        at,
        grad,
        weight_cols,
        scratch=[pltpu.VMEM((RING, tok, feats), BF16)],
    )
    part, dealt = lax.optimization_barrier((part, dealt))
    dealt = [dealt[0]] + [along_y(dealt[d], d) for d in range(1, RING)]
    grad_hidden = call(
        join_kernel,
        jax.ShapeDtypeStruct((tok, width), BF16),
        WEIGHTY,
        2 << 20,
        at,
        *dealt,
        scratch=[copies(4 * RING)],
        out=HBM,
    )

    part = exchange(part, "x")
    part = call(sum_kernel, jax.ShapeDtypeStruct((DEPTH, rows, kv), BF16), 0, 1 << 20, part)
    part = exchange_z(part, REDUCE_FIRST)
    gradient = jnp.sum(part.astype(F32), axis=0) / F32(tok * 512)

    moment_new = beta_one * moment + (1.0 - beta_one) * gradient
    second_new = beta_two * second + (1.0 - beta_two) * gradient * gradient
    moment_hat = moment_new / (1.0 - beta_one**10)
    second_hat = second_new / (1.0 - beta_two**10)
    master_new = master - learn_rate * (
        moment_hat / (jnp.sqrt(second_hat) + adam_eps) + decay_rate * master
    )
    return (attended, grad_hidden, master_new, moment_new, second_new)


def solution(mesh):
    named = Mesh(mesh.devices.reshape(SIZES), AXES)
    return jax.shard_map(
        per_device,
        mesh=named,
        in_specs=(TOK_SPEC, TOK_SPEC, TOK_SPEC, TOK_SPEC, ROW_SPEC, ROW_SPEC, ROW_SPEC),
        out_specs=(TOK_SPEC, TOK_SPEC, ROW_SPEC, ROW_SPEC, ROW_SPEC),
        check_vma=False,
    )
```

```python
import jax
import jax.numpy as jnp
import numpy as np
from jax import lax
from jax.experimental import pallas as pl
from jax.experimental.pallas import tpu as pltpu
from jax.sharding import Mesh
from jax.sharding import PartitionSpec as P

HD = 128
VH = 4
QH = 32
GROUPS = QH // VH

beta_one = 0.9
beta_two = 0.95
adam_eps = 1e-08
learn_rate = 0.001
decay_rate = 0.1

AXES = ("zl", "x", "c", "zh", "yh", "yl")
SIZES = (4, 4, 2, 4, 2, 2)
TOK_SPEC = P(AXES, None)
ROW_SPEC = P(("zh", "yh", "yl", "zl", "x", "c"), None)
DEPTH = 16
PLANE = ("x", "yh")
GATHER_FIRST = 3
REDUCE_FIRST = 6

F32 = jnp.float32
BF16 = jnp.bfloat16


def order_matrix(core):
    to = lax.broadcasted_iota(jnp.int32, (1, 1024), 1)
    z = ((to >> 3) & 15) ^ GATHER_FIRST
    source = (z & 3) * 256 + (z >> 2) * 64 + ((to >> 7) & 3) * 16 + (to & 7)
    source = source + ((to >> 9) ^ core) * 8
    hit = lax.broadcasted_iota(jnp.int32, (1024, 1024), 0) == source
    return jnp.where(hit, F32(1), F32(0)).astype(BF16)


def return_matrix(core):
    to = lax.broadcasted_iota(jnp.int32, (1, 1024), 1)
    z = (((to >> 6) & 3) * 4 + (to >> 8)) ^ GATHER_FIRST
    source = z * 8 + ((to >> 4) & 3) * 128 + (to & 7)
    source = source + (((to >> 3) & 1) ^ core) * 512
    hit = lax.broadcasted_iota(jnp.int32, (1024, 1024), 0) == source
    return jnp.where(hit, F32(1), F32(0)).astype(BF16)


WEIGHTY = 32 << 30


def run_copies(sem_ref, pairs):
    copies = [pltpu.make_async_copy(a, b, sem_ref.at[i]) for i, (a, b) in enumerate(pairs)]
    for copy in copies:
        copy.start()
    for copy in copies:
        copy.wait()


def master_kernel(master_ref, out_ref, rows_ref, sem_ref):
    run_copies(sem_ref, [(master_ref, rows_ref)])
    weight = rows_ref[...].astype(BF16)
    for z in range(DEPTH):
        out_ref[z] = weight


def spread_kernel(rows_ref, out_ref, sem_ref):
    run_copies(sem_ref, [(rows_ref, out_ref.at[i]) for i in range(out_ref.shape[0])])


def block_columns(yl, block_ref, whole_ref):
    pairs = []
    for yh in range(2):
        for zh in range(4):
            at = pl.ds(pl.multiple_of(zh * 1024 + yh * 512 + yl * 256, 256), 256)
            pairs.append((block_ref.at[:, yh * 1024 + zh * 256 : yh * 1024 + zh * 256 + 256], whole_ref.at[:, at]))
    return pairs


def deal_kernel(at_ref, hidden_ref, keep_ref, send_ref, sem_ref):
    yl = at_ref[0]
    pairs = block_columns(yl, keep_ref, hidden_ref) + block_columns(1 - yl, send_ref, hidden_ref)
    run_copies(sem_ref, [(b, a) for a, b in pairs])


def join_kernel(at_ref, keep_ref, got_ref, out_ref, sem_ref):
    yl = at_ref[0]
    run_copies(sem_ref, block_columns(yl, keep_ref, out_ref) + block_columns(1 - yl, got_ref, out_ref))


def collect_kernel(at_ref, block_ref, own_ref, other_ref, matrix_ref):
    matrix_ref[...] = order_matrix(at_ref[1])
    for yh in range(2):
        moved = jnp.dot(
            block_ref[:, yh * 1024 : yh * 1024 + 1024], matrix_ref[...], preferred_element_type=F32
        ).astype(BF16)
        for x in range(4):
            to = slice((x * 2 + yh) * 128, (x * 2 + yh) * 128 + 128)
            own_ref[:, to] = moved[:, x * 128 : x * 128 + 128]
            other_ref[:, to] = moved[:, 512 + x * 128 : 640 + x * 128]


def first_kernel(near_ref, far_ref, weight_ref, near_out_ref, far_out_ref):
    near_out_ref[...] = jnp.dot(near_ref[...], weight_ref[...], preferred_element_type=F32)
    far_out_ref[...] = jnp.dot(far_ref[...], weight_ref[...], preferred_element_type=F32)


def second_kernel(rows_ref, weight_ref, first_ref, out_ref):
    total = first_ref[...] + jnp.dot(rows_ref[...], weight_ref[...], preferred_element_type=F32)
    out_ref[...] = total.astype(out_ref.dtype)


def flip_kernel(near_own_ref, near_other_ref, far_own_ref, far_other_ref, own_ref, other_ref):
    tok = near_own_ref.shape[0]
    own_ref[:, :tok] = near_own_ref[...].T
    own_ref[:, tok:] = far_own_ref[...].T
    other_ref[:, :tok] = near_other_ref[...].T
    other_ref[:, tok:] = far_other_ref[...].T


def part_kernel(hidden_ref, near_ref, far_ref, out_ref):
    grad = jnp.concatenate([near_ref[...], far_ref[...]], axis=0)
    out_ref[...] = jnp.dot(hidden_ref[...], grad, preferred_element_type=F32).astype(BF16)


def fold_kernel(hidden_ref, near_ref, far_ref, sent_ref, out_ref, rows_ref, sem_ref):
    grad = jnp.concatenate([near_ref[...], far_ref[...]], axis=0)
    step = out_ref.shape[1]
    copies = []
    for i in range(out_ref.shape[0]):
        at = slice(i * step, (i + 1) * step)
        part = jnp.dot(hidden_ref[at], grad, preferred_element_type=F32)
        rows_ref[i] = (part + sent_ref[at].astype(F32)).astype(BF16)
        copies.append(pltpu.make_async_copy(rows_ref.at[i], out_ref.at[i], sem_ref.at[i]))
        copies[-1].start()
    for copy in copies:
        copy.wait()


def back_kernel(at_ref, near_ref, far_ref, own_ref, other_ref, keep_ref, send_ref, cols_ref, matrix_ref):
    tok = near_ref.shape[0]
    matrix_ref[...] = return_matrix(at_ref[1])
    grad = jnp.concatenate([near_ref[...], far_ref[...]], axis=0)
    for c, weight_ref in enumerate((own_ref, other_ref)):
        rows = lax.dot_general(
            grad, weight_ref[...], (((1,), (1,)), ((), ())), preferred_element_type=F32
        ).astype(BF16)
        for x in range(4):
            for yh in range(2):
                at = (x * 2 + yh) * 128
                cols_ref[yh, :, c * 512 + x * 128 : c * 512 + x * 128 + 128] = rows[:, at : at + 128]
    for yh in range(2):
        moved = jnp.dot(cols_ref[yh], matrix_ref[...], preferred_element_type=F32).astype(BF16)
        keep_ref[:, yh * 1024 : yh * 1024 + 1024] = moved[:tok]
        send_ref[:, yh * 1024 : yh * 1024 + 1024] = moved[tok:]


def sum_kernel(parts_ref, out_ref):
    total = parts_ref[0].astype(F32)
    for i in range(1, parts_ref.shape[0]):
        total = total + parts_ref[i].astype(F32)
    total = total.astype(BF16)
    rows = out_ref.shape[1]
    for z in range(out_ref.shape[0]):
        out_ref[z ^ GATHER_FIRST ^ REDUCE_FIRST] = total[z * rows : (z + 1) * rows]


def probs_kernel(queries_ref, keys_ref, seg_row_ref, seg_col_ref, out_ref):
    tok = queries_ref.shape[0]
    rows = lax.broadcasted_iota(jnp.int32, (tok, tok), 0)
    cols = lax.broadcasted_iota(jnp.int32, (tok, tok), 1)
    allowed = (seg_col_ref[...] == seg_row_ref[...]) & (cols <= rows)
    scale = F32(1.0 / np.sqrt(HD))
    for j in range(VH):
        key = keys_ref[:, j * HD : (j + 1) * HD]
        for h in range(GROUPS):
            at = (j * GROUPS + h) * HD
            scores = lax.dot_general(
                queries_ref[:, at : at + HD], key, (((1,), (1,)), ((), ())), preferred_element_type=F32
            )
            scores = jnp.where(allowed, scores * scale, F32(-1000000000.0))
            expos = jnp.exp(scores - jnp.max(scores, axis=-1, keepdims=True))
            total = jnp.sum(expos, axis=-1, keepdims=True)
            out_ref[j, h * tok : (h + 1) * tok, :] = (expos / total).astype(BF16)


def attend_kernel(near_ref, sent_ref, probs_ref, attended_ref, grad_ref, rows_ref, sem_ref):
    tok = near_ref.shape[0]
    wide = GROUPS * HD
    copies = []
    for j in range(VH):
        cols = slice(j * HD, (j + 1) * HD)
        value = (near_ref[:, cols] + sent_ref[:, cols].astype(F32)).astype(BF16)
        attended = jnp.dot(probs_ref[j], value, preferred_element_type=F32).astype(BF16)
        for h in range(GROUPS):
            rows_ref[j, :, h * HD : (h + 1) * HD] = attended[h * tok : (h + 1) * tok]
        copies.append(
            pltpu.make_async_copy(rows_ref.at[j], attended_ref.at[:, j * wide : (j + 1) * wide], sem_ref.at[j])
        )
        copies[-1].start()
        grad_ref[:, cols] = lax.dot_general(
            probs_ref[j], attended, (((0,), (0,)), ((), ())), preferred_element_type=F32
        ).astype(BF16)
    for copy in copies:
        copy.wait()


SMEM = pl.BlockSpec(memory_space=pltpu.SMEM)
VMEM = pl.BlockSpec(memory_space=pltpu.VMEM)
HBM = pl.BlockSpec(memory_space=pltpu.HBM)


def copies(n):
    return pltpu.SemaphoreType.DMA((n,))


def call(kernel, out_shape, flops, nbytes, *args, scratch=(), out=None, hbm=()):
    specs = [SMEM if a.dtype == jnp.int32 and a.ndim == 1 else VMEM for a in args]
    specs = [HBM if i in hbm else spec for i, spec in enumerate(specs)]
    if out is None:
        out = (VMEM,) * len(out_shape) if isinstance(out_shape, tuple) else VMEM
    if out is HBM:
        out_shape = pltpu.HBM(out_shape.shape, out_shape.dtype)
    args = [pltpu.with_memory_space_constraint(a, pltpu.HBM) if i in hbm else a for i, a in enumerate(args)]
    return pl.pallas_call(
        kernel,
        out_shape=out_shape,
        in_specs=specs,
        out_specs=out,
        scratch_shapes=scratch,
        compiler_params=pltpu.CompilerParams(vmem_limit_bytes=24 * 1024 * 1024),
        cost_estimate=pl.CostEstimate(flops=flops, bytes_accessed=nbytes, transcendentals=0),
    )(*args)


def swap_core(array):
    return lax.ppermute(array, "c", [(0, 1), (1, 0)])


def swap_pair(array):
    return lax.ppermute(array, "yl", [(0, 1), (1, 0)])


def exchange(blocks, axes):
    return lax.all_to_all(blocks, axes, split_axis=0, concat_axis=0, tiled=True)


def exchange_z(blocks, first):
    ids = np.arange(np.prod(SIZES)).reshape(SIZES).transpose(1, 2, 4, 5, 0, 3).reshape(-1, DEPTH)
    groups = ids[:, np.arange(DEPTH) ^ first].tolist()
    return lax.all_to_all(blocks, AXES, split_axis=0, concat_axis=0, axis_index_groups=groups, tiled=True)


def per_device(hidden_in, queries, keys, lengths, master, moment, second):
    tok, width = hidden_in.shape
    kv = keys.shape[1]
    rows = master.shape[0]
    feats = width // 4
    peers = 8
    at = jnp.stack([lax.axis_index("yl"), lax.axis_index("c")]).astype(jnp.int32)
    block = jax.ShapeDtypeStruct((tok, 2 * feats), BF16)
    half = jax.ShapeDtypeStruct((tok, feats), BF16)
    value = jax.ShapeDtypeStruct((tok, kv), BF16)
    total = jax.ShapeDtypeStruct((tok, kv), F32)
    matrix = pltpu.VMEM((1024, 1024), BF16)

    weight = call(
        master_kernel,
        jax.ShapeDtypeStruct((DEPTH, rows, kv), BF16),
        0,
        1 << 17,
        master,
        scratch=[pltpu.VMEM((rows, kv), F32), copies(1)],
        hbm=(0,),
    )
    weight = exchange_z(weight, GATHER_FIRST).reshape(DEPTH * rows, kv)

    keep, send = call(
        deal_kernel, (block, block), 0, 2 << 20, at, hidden_in, scratch=[copies(16)], hbm=(1,)
    )
    got = swap_pair(send)

    weight = call(
        spread_kernel,
        jax.ShapeDtypeStruct((peers, DEPTH * rows, kv), BF16),
        0,
        1 << 20,
        weight,
        scratch=[copies(peers)],
        out=HBM,
    )
    weight, keep, keys = lax.optimization_barrier((weight, keep, keys))
    weight = exchange(weight, PLANE).reshape(peers * DEPTH * rows, kv)

    def collect(array):
        return call(collect_kernel, (half, half), WEIGHTY, 3 << 20, at, array, scratch=[matrix])

    near_own, near_other = collect(keep)
    far_own, far_other = collect(got)

    ends = jnp.cumsum(lengths[0])
    seg = jnp.sum((jnp.arange(tok, dtype=jnp.int32)[:, None] >= ends[None, :]).astype(jnp.int32), axis=1)
    probs = call(
        probs_kernel,
        jax.ShapeDtypeStruct((VH, GROUPS * tok, tok), BF16),
        4 * tok * tok * QH * HD,
        8 << 20,
        queries,
        keys,
        seg[None, :],
        seg[:, None],
    )
    flipped = jax.ShapeDtypeStruct((feats, 2 * tok), BF16)
    columns_own, columns_other = call(
        flip_kernel, (flipped, flipped), 0, 2 << 20, near_own, near_other, far_own, far_other
    )

    weight, near_own, near_other, far_own, far_other, columns_own, columns_other, probs = lax.optimization_barrier(
        (weight, near_own, near_other, far_own, far_other, columns_own, columns_other, probs)
    )
    weight_other = swap_core(weight)

    flops = 2 * tok * feats * kv
    near, far = call(first_kernel, (total, total), 2 * flops, 2 << 20, near_own, far_own, weight)
    far = call(second_kernel, value, flops, 2 << 20, far_other, weight_other, far)
    sent = swap_pair(far)
    near = call(second_kernel, total, flops, 2 << 20, near_other, weight_other, near)
    attended, grad = call(
        attend_kernel,
        (jax.ShapeDtypeStruct((tok, QH * HD), BF16), value),
        4 * tok * tok * QH * HD,
        4 << 20,
        near,
        sent,
        probs,
        scratch=[pltpu.VMEM((VH, tok, GROUPS * HD), BF16), copies(VH)],
        out=(HBM, VMEM),
    )
    grad_far = swap_pair(grad)

    part = call(
        part_kernel,
        jax.ShapeDtypeStruct((feats, kv), BF16),
        2 * flops,
        2 << 20,
        columns_other,
        grad,
        grad_far,
    )
    part = call(
        fold_kernel,
        jax.ShapeDtypeStruct((peers, DEPTH * rows, kv), BF16),
        2 * flops,
        2 << 20,
        columns_own,
        grad,
        grad_far,
        swap_core(part),
        scratch=[pltpu.VMEM((peers, DEPTH * rows, kv), BF16), copies(peers)],
        out=HBM,
    )
    part, grad, grad_far = lax.optimization_barrier((part, grad, grad_far))

    keep, send = call(
        back_kernel,
        (block, block),
        8 * tok * feats * kv,
        4 << 20,
        at,
        grad,
        grad_far,
        weight,
        weight_other,
        scratch=[pltpu.VMEM((2, 2 * tok, 1024), BF16), matrix],
    )
    grad_hidden = call(
        join_kernel,
        jax.ShapeDtypeStruct((tok, width), BF16),
        WEIGHTY,
        2 << 20,
        at,
        keep,
        swap_pair(send),
        scratch=[copies(16)],
        out=HBM,
    )

    part = exchange(part, PLANE)
    part = call(sum_kernel, jax.ShapeDtypeStruct((DEPTH, rows, kv), BF16), 0, 1 << 20, part)
    part = exchange_z(part, REDUCE_FIRST)
    gradient = jnp.sum(part.astype(F32), axis=0) / F32(tok * 512)

    moment_new = beta_one * moment + (1.0 - beta_one) * gradient
    second_new = beta_two * second + (1.0 - beta_two) * gradient * gradient
    moment_hat = moment_new / (1.0 - beta_one**10)
    second_hat = second_new / (1.0 - beta_two**10)
    master_new = master - learn_rate * (
        moment_hat / (jnp.sqrt(second_hat) + adam_eps) + decay_rate * master
    )
    return (attended, grad_hidden, master_new, moment_new, second_new)


def solution(mesh):
    named = Mesh(mesh.devices.reshape(SIZES), AXES)
    return jax.shard_map(
        per_device,
        mesh=named,
        in_specs=(TOK_SPEC, TOK_SPEC, TOK_SPEC, TOK_SPEC, ROW_SPEC, ROW_SPEC, ROW_SPEC),
        out_specs=(TOK_SPEC, TOK_SPEC, ROW_SPEC, ROW_SPEC, ROW_SPEC),
        check_vma=False,
    )
```

```python
import jax
import jax.numpy as jnp
import numpy as np
from jax import lax
from jax.experimental import pallas as pl
from jax.experimental.pallas import tpu as pltpu
from jax.sharding import Mesh
from jax.sharding import PartitionSpec as P

HD = 128
VH = 4
QH = 32
GROUPS = QH // VH

beta_one = 0.9
beta_two = 0.95
adam_eps = 1e-08
learn_rate = 0.001
decay_rate = 0.1

AXES = ("zlh", "zll", "x", "c", "zh", "y")
SIZES = (2, 2, 4, 2, 4, 4)
TOK_SPEC = P(AXES, None)
ROW_SPEC = P(("zh", "y", "zlh", "zll", "x", "c"), None)
DEPTH = 8
PLANE = 16
GATHER_FIRST = 3
REDUCE_FIRST = 2

F32 = jnp.float32
BF16 = jnp.bfloat16


def order_matrix(zll, core):
    to = lax.broadcasted_iota(jnp.int32, (1, 1024), 1)
    z = ((to >> 3) & 7) ^ GATHER_FIRST
    source = (z & 3) * 256 + (z >> 2) * 128 + ((to >> 6) & 3) * 16 + (to & 7)
    source = source + ((to >> 9) ^ zll) * 64 + (((to >> 8) & 1) ^ core) * 8
    hit = lax.broadcasted_iota(jnp.int32, (1024, 1024), 0) == source
    return jnp.where(hit, F32(1), F32(0)).astype(BF16)


def return_matrix(zll, core):
    to = lax.broadcasted_iota(jnp.int32, (1, 1024), 1)
    z = (((to >> 7) & 1) * 4 + (to >> 8)) ^ GATHER_FIRST
    source = z * 8 + ((to >> 4) & 3) * 64 + (to & 7)
    source = source + (((to >> 6) & 1) ^ zll) * 512 + (((to >> 3) & 1) ^ core) * 256
    hit = lax.broadcasted_iota(jnp.int32, (1024, 1024), 0) == source
    return jnp.where(hit, F32(1), F32(0)).astype(BF16)


WEIGHTY = 32 << 30


def run_copies(sem_ref, pairs):
    copies = [pltpu.make_async_copy(a, b, sem_ref.at[i]) for i, (a, b) in enumerate(pairs)]
    for copy in copies:
        copy.start()
    for copy in copies:
        copy.wait()


def master_kernel(master_ref, out_ref, rows_ref, sem_ref):
    run_copies(sem_ref, [(master_ref, rows_ref)])
    weight = rows_ref[...].astype(BF16)
    for z in range(DEPTH):
        out_ref[z] = weight


def spread_kernel(rows_ref, out_ref, sem_ref):
    run_copies(sem_ref, [(rows_ref, out_ref.at[i]) for i in range(out_ref.shape[0])])


def whole_columns(whole_ref, cols_ref):
    tok = whole_ref.shape[0]
    return [
        (
            whole_ref.at[:, zh * 1024 + y * 256 : zh * 1024 + y * 256 + 256],
            cols_ref.at[y * tok : (y + 1) * tok, zh * 256 : (zh + 1) * 256],
        )
        for y in range(4)
        for zh in range(4)
    ]


def split_kernel(at_ref, hidden_ref, own_ref, other_ref, send_ref, cols_ref, matrix_ref, sem_ref):
    tok = own_ref.shape[0]
    half = own_ref.shape[1]
    copies = [pltpu.make_async_copy(a, b, sem_ref.at[i]) for i, (a, b) in enumerate(whole_columns(hidden_ref, cols_ref))]
    for copy in copies:
        copy.start()
    matrix_ref[...] = order_matrix(at_ref[0], at_ref[1])
    for copy in copies:
        copy.wait()
    moved = jnp.dot(cols_ref[...], matrix_ref[...], preferred_element_type=F32).astype(BF16)
    for y in range(4):
        rows = slice(y * tok, (y + 1) * tok)
        to = slice(y * 256, (y + 1) * 256)
        own_ref[:, to] = moved[rows, :256]
        other_ref[:, to] = moved[rows, 256:512]
        send_ref[:, to] = moved[rows, 512:768]
        send_ref[:, half + y * 256 : half + (y + 1) * 256] = moved[rows, 768:]


def join_kernel(at_ref, keep_ref, got_ref, out_ref, cols_ref, moved_ref, matrix_ref, sem_ref):
    tok = keep_ref.shape[0]
    half = keep_ref.shape[1] // 2
    matrix_ref[...] = return_matrix(at_ref[0], at_ref[1])
    for y in range(4):
        for t, ref in enumerate((keep_ref, got_ref)):
            for c in range(2):
                to = (t * 2 + c) * 256
                cols_ref[y * tok : (y + 1) * tok, to : to + 256] = ref[:, c * half + y * 256 : c * half + y * 256 + 256]
    moved_ref[...] = jnp.dot(cols_ref[...], matrix_ref[...], preferred_element_type=F32).astype(BF16)
    run_copies(sem_ref, [(b, a) for a, b in whole_columns(out_ref, moved_ref)])


def first_kernel(near_ref, far_ref, weight_ref, near_out_ref, far_out_ref):
    half = near_ref.shape[1]
    near_out_ref[...] = jnp.dot(near_ref[...], weight_ref[...], preferred_element_type=F32)
    far_out_ref[...] = jnp.dot(far_ref[:, :half], weight_ref[...], preferred_element_type=F32)


def second_kernel(rows_ref, weight_ref, first_ref, out_ref):
    rows = rows_ref[:, rows_ref.shape[1] - weight_ref.shape[0] :]
    total = first_ref[...] + jnp.dot(rows, weight_ref[...], preferred_element_type=F32)
    out_ref[...] = total.astype(out_ref.dtype)


def flip_kernel(near_own_ref, near_other_ref, far_ref, own_ref, other_ref):
    tok, half = near_own_ref.shape
    own_ref[:, :tok] = near_own_ref[...].T
    own_ref[:, tok:] = far_ref[:, :half].T
    other_ref[:, :tok] = near_other_ref[...].T
    other_ref[:, tok:] = far_ref[:, half:].T


def part_kernel(hidden_ref, near_ref, far_ref, out_ref):
    grad = jnp.concatenate([near_ref[...], far_ref[...]], axis=0)
    out_ref[...] = jnp.dot(hidden_ref[...], grad, preferred_element_type=F32).astype(BF16)


def fold_kernel(hidden_ref, near_ref, far_ref, sent_ref, out_ref, rows_ref, sem_ref):
    grad = jnp.concatenate([near_ref[...], far_ref[...]], axis=0)
    step = out_ref.shape[1]
    copies = []
    for i in range(out_ref.shape[0]):
        at = slice(i * step, (i + 1) * step)
        part = jnp.dot(hidden_ref[at], grad, preferred_element_type=F32)
        rows_ref[i] = (part + sent_ref[at].astype(F32)).astype(BF16)
        copies.append(pltpu.make_async_copy(rows_ref.at[i], out_ref.at[i], sem_ref.at[i]))
        copies[-1].start()
    for copy in copies:
        copy.wait()


def back_kernel(near_ref, far_ref, own_ref, other_ref, keep_ref, send_ref):
    tok = near_ref.shape[0]
    half = own_ref.shape[0]
    grad = jnp.concatenate([near_ref[...], far_ref[...]], axis=0)
    for c, weight_ref in enumerate((own_ref, other_ref)):
        rows = lax.dot_general(
            grad, weight_ref[...], (((1,), (1,)), ((), ())), preferred_element_type=F32
        ).astype(BF16)
        keep_ref[:, c * half : (c + 1) * half] = rows[:tok]
        send_ref[:, c * half : (c + 1) * half] = rows[tok:]


def sum_kernel(parts_ref, out_ref):
    total = parts_ref[0].astype(F32)
    for i in range(1, parts_ref.shape[0]):
        total = total + parts_ref[i].astype(F32)
    total = total.astype(BF16)
    rows = out_ref.shape[1]
    for z in range(out_ref.shape[0]):
        out_ref[z ^ GATHER_FIRST ^ REDUCE_FIRST] = total[z * rows : (z + 1) * rows]


def probs_kernel(queries_ref, keys_ref, seg_row_ref, seg_col_ref, out_ref):
    tok = queries_ref.shape[0]
    rows = lax.broadcasted_iota(jnp.int32, (tok, tok), 0)
    cols = lax.broadcasted_iota(jnp.int32, (tok, tok), 1)
    allowed = (seg_col_ref[...] == seg_row_ref[...]) & (cols <= rows)
    scale = F32(1.0 / np.sqrt(HD))
    for j in range(VH):
        key = keys_ref[:, j * HD : (j + 1) * HD]
        for h in range(GROUPS):
            at = (j * GROUPS + h) * HD
            scores = lax.dot_general(
                queries_ref[:, at : at + HD], key, (((1,), (1,)), ((), ())), preferred_element_type=F32
            )
            scores = jnp.where(allowed, scores * scale, F32(-1000000000.0))
            expos = jnp.exp(scores - jnp.max(scores, axis=-1, keepdims=True))
            total = jnp.sum(expos, axis=-1, keepdims=True)
            out_ref[j, h * tok : (h + 1) * tok, :] = (expos / total).astype(BF16)


def attend_kernel(near_ref, sent_ref, probs_ref, attended_ref, grad_ref, rows_ref, sem_ref):
    tok = near_ref.shape[0]
    wide = GROUPS * HD
    copies = []
    for j in range(VH):
        cols = slice(j * HD, (j + 1) * HD)
        value = (near_ref[:, cols] + sent_ref[:, cols].astype(F32)).astype(BF16)
        attended = jnp.dot(probs_ref[j], value, preferred_element_type=F32).astype(BF16)
        for h in range(GROUPS):
            rows_ref[j, :, h * HD : (h + 1) * HD] = attended[h * tok : (h + 1) * tok]
        copies.append(
            pltpu.make_async_copy(rows_ref.at[j], attended_ref.at[:, j * wide : (j + 1) * wide], sem_ref.at[j])
        )
        copies[-1].start()
        grad_ref[:, cols] = lax.dot_general(
            probs_ref[j], attended, (((0,), (0,)), ((), ())), preferred_element_type=F32
        ).astype(BF16)
    for copy in copies:
        copy.wait()


SMEM = pl.BlockSpec(memory_space=pltpu.SMEM)
VMEM = pl.BlockSpec(memory_space=pltpu.VMEM)
HBM = pl.BlockSpec(memory_space=pltpu.HBM)


def copies(n):
    return pltpu.SemaphoreType.DMA((n,))


def call(kernel, out_shape, flops, nbytes, *args, scratch=(), out=None, hbm=(), late=()):
    specs = [SMEM if a.dtype == jnp.int32 and a.ndim == 1 else VMEM for a in args]
    specs = [HBM if i in hbm else spec for i, spec in enumerate(specs)]
    if out is None:
        out = (VMEM,) * len(out_shape) if isinstance(out_shape, tuple) else VMEM
    if out is HBM:
        out_shape = pltpu.HBM(out_shape.shape, out_shape.dtype)
    if late:
        out_shape = tuple(pltpu.HBM(o.shape, o.dtype) if i in late else o for i, o in enumerate(out_shape))
    args = [pltpu.with_memory_space_constraint(a, pltpu.HBM) if i in hbm else a for i, a in enumerate(args)]
    return pl.pallas_call(
        kernel,
        out_shape=out_shape,
        in_specs=specs,
        out_specs=out,
        scratch_shapes=scratch,
        compiler_params=pltpu.CompilerParams(vmem_limit_bytes=24 * 1024 * 1024),
        cost_estimate=pl.CostEstimate(flops=flops, bytes_accessed=nbytes, transcendentals=0),
    )(*args)


def swap_core(array):
    return lax.ppermute(array, "c", [(0, 1), (1, 0)])


def swap_pair(array):
    return lax.ppermute(array, "zll", [(0, 1), (1, 0)])


def exchange(blocks, members, first):
    ids = np.arange(np.prod(SIZES)).reshape(SIZES)
    last = [AXES.index(a) for a in members]
    ids = ids.transpose([i for i in range(len(SIZES)) if i not in last] + last).reshape(-1, blocks.shape[0])
    groups = ids[:, np.arange(blocks.shape[0]) ^ first].tolist()
    return lax.all_to_all(blocks, AXES, split_axis=0, concat_axis=0, axis_index_groups=groups, tiled=True)


def exchange_z(blocks, first):
    return exchange(blocks, ("zlh", "zh"), first)


def exchange_plane(blocks):
    return exchange(blocks, ("y", "x"), 0)


def per_device(hidden_in, queries, keys, lengths, master, moment, second):
    tok, width = hidden_in.shape
    kv = keys.shape[1]
    rows = master.shape[0]
    feats = width // 4
    at = jnp.stack([lax.axis_index("zll"), lax.axis_index("c")]).astype(jnp.int32)
    block = jax.ShapeDtypeStruct((tok, 2 * feats), BF16)
    half = jax.ShapeDtypeStruct((tok, feats), BF16)
    value = jax.ShapeDtypeStruct((tok, kv), BF16)
    total = jax.ShapeDtypeStruct((tok, kv), F32)
    matrix = pltpu.VMEM((1024, 1024), BF16)
    cols = pltpu.VMEM((4 * tok, 1024), BF16)

    weight = call(
        master_kernel,
        jax.ShapeDtypeStruct((DEPTH, rows, kv), BF16),
        0,
        1 << 17,
        master,
        scratch=[pltpu.VMEM((rows, kv), F32), copies(1)],
        hbm=(0,),
    )
    weight, hidden_in = lax.optimization_barrier((weight, hidden_in))
    weight = exchange_z(weight, GATHER_FIRST).reshape(DEPTH * rows, kv)

    near_own, near_other, send = call(
        split_kernel,
        (half, half, block),
        8 * tok * 1024 * 1024,
        2 << 20,
        at,
        hidden_in,
        scratch=[cols, matrix, copies(16)],
        hbm=(1,),
        late=(0, 1),
    )
    far = swap_pair(send)

    weight = call(
        spread_kernel,
        jax.ShapeDtypeStruct((PLANE, DEPTH * rows, kv), BF16),
        0,
        1 << 20,
        weight,
        scratch=[copies(PLANE)],
        out=HBM,
    )
    weight, keys = lax.optimization_barrier((weight, keys))
    weight = exchange_plane(weight).reshape(PLANE * DEPTH * rows, kv)

    ends = jnp.cumsum(lengths[0])
    seg = jnp.sum((jnp.arange(tok, dtype=jnp.int32)[:, None] >= ends[None, :]).astype(jnp.int32), axis=1)
    (probs,) = call(
        probs_kernel,
        (jax.ShapeDtypeStruct((VH, GROUPS * tok, tok), BF16),),
        4 * tok * tok * QH * HD,
        8 << 20,
        queries,
        keys,
        seg[None, :],
        seg[:, None],
        late=(0,),
    )
    flipped = jax.ShapeDtypeStruct((feats, 2 * tok), BF16)
    columns_own, columns_other = call(
        flip_kernel, (flipped, flipped), WEIGHTY // 6, 2 << 20, near_own, near_other, far, late=(0, 1)
    )
    weight, near_own, near_other, far, columns_own, columns_other, probs = lax.optimization_barrier(
        (weight, near_own, near_other, far, columns_own, columns_other, probs)
    )
    weight_other = swap_core(weight)

    flops = 2 * tok * feats * kv
    near, far_values = call(first_kernel, (total, total), 2 * flops, 2 << 20, near_own, far, weight)
    sent = swap_pair(call(second_kernel, value, flops, 2 << 20, far, weight_other, far_values))
    near = call(second_kernel, total, flops, 2 << 20, near_other, weight_other, near)
    attended, grad = call(
        attend_kernel,
        (jax.ShapeDtypeStruct((tok, QH * HD), BF16), value),
        4 * tok * tok * QH * HD,
        4 << 20,
        near,
        sent,
        probs,
        scratch=[pltpu.VMEM((VH, tok, GROUPS * HD), BF16), copies(VH)],
        out=(HBM, VMEM),
    )
    grad_far = swap_pair(grad)

    part = call(
        part_kernel,
        jax.ShapeDtypeStruct((feats, kv), BF16),
        2 * flops,
        2 << 20,
        columns_other,
        grad,
        grad_far,
    )
    part = call(
        fold_kernel,
        jax.ShapeDtypeStruct((PLANE, DEPTH * rows, kv), BF16),
        2 * flops,
        2 << 20,
        columns_own,
        grad,
        grad_far,
        swap_core(part),
        scratch=[pltpu.VMEM((PLANE, DEPTH * rows, kv), BF16), copies(PLANE)],
        out=HBM,
    )
    part, grad, grad_far = lax.optimization_barrier((part, grad, grad_far))

    keep, send = call(
        back_kernel, (block, block), 8 * tok * feats * kv, 4 << 20, grad, grad_far, weight, weight_other, late=(0,)
    )
    grad_hidden = call(
        join_kernel,
        jax.ShapeDtypeStruct((tok, width), BF16),
        WEIGHTY,
        2 << 20,
        at,
        keep,
        swap_pair(send),
        scratch=[cols, cols, matrix, copies(16)],
        out=HBM,
    )

    part = exchange_plane(part)
    part = call(sum_kernel, jax.ShapeDtypeStruct((DEPTH, rows, kv), BF16), 0, 1 << 20, part)
    part = exchange_z(part, REDUCE_FIRST)
    gradient = jnp.sum(part.astype(F32), axis=0) / F32(tok * 512)

    moment_new = beta_one * moment + (1.0 - beta_one) * gradient
    second_new = beta_two * second + (1.0 - beta_two) * gradient * gradient
    moment_hat = moment_new / (1.0 - beta_one**10)
    second_hat = second_new / (1.0 - beta_two**10)
    master_new = master - learn_rate * (
        moment_hat / (jnp.sqrt(second_hat) + adam_eps) + decay_rate * master
    )
    return (attended, grad_hidden, master_new, moment_new, second_new)


def solution(mesh):
    named = Mesh(mesh.devices.reshape(SIZES), AXES)
    return jax.shard_map(
        per_device,
        mesh=named,
        in_specs=(TOK_SPEC, TOK_SPEC, TOK_SPEC, TOK_SPEC, ROW_SPEC, ROW_SPEC, ROW_SPEC),
        out_specs=(TOK_SPEC, TOK_SPEC, ROW_SPEC, ROW_SPEC, ROW_SPEC),
        check_vma=False,
    )
```

```python
import jax
import jax.numpy as jnp
import numpy as np
from jax import lax
from jax.experimental import pallas as pl
from jax.experimental.pallas import tpu as pltpu
from jax.sharding import Mesh
from jax.sharding import PartitionSpec as P

HD = 128
VH = 4
QH = 32
GROUPS = QH // VH

beta_one = 0.9
beta_two = 0.95
adam_eps = 1e-08
learn_rate = 0.001
decay_rate = 0.1

AXES = ("zlh", "zll", "x", "c", "zh", "y")
SIZES = (2, 2, 4, 2, 4, 4)
TOK_SPEC = P(AXES, None)
ROW_SPEC = P(("zh", "y", "zlh", "zll", "x", "c"), None)
DEPTH = 8
PLANE = 16
GATHER_FIRST = 3
REDUCE_FIRST = 2

F32 = jnp.float32
BF16 = jnp.bfloat16


def order_matrix(zll, core):
    to = lax.broadcasted_iota(jnp.int32, (1, 1024), 1)
    z = ((to >> 3) & 7) ^ GATHER_FIRST
    source = (z & 3) * 256 + (z >> 2) * 128 + ((to >> 6) & 3) * 16 + (to & 7)
    source = source + ((to >> 9) ^ zll) * 64 + (((to >> 8) & 1) ^ core) * 8
    hit = lax.broadcasted_iota(jnp.int32, (1024, 1024), 0) == source
    return jnp.where(hit, F32(1), F32(0)).astype(BF16)


def return_matrix(zll, core):
    to = lax.broadcasted_iota(jnp.int32, (1, 1024), 1)
    z = (((to >> 7) & 1) * 4 + (to >> 8)) ^ GATHER_FIRST
    source = z * 8 + ((to >> 4) & 3) * 64 + (to & 7)
    source = source + (((to >> 6) & 1) ^ zll) * 512 + (((to >> 3) & 1) ^ core) * 256
    hit = lax.broadcasted_iota(jnp.int32, (1024, 1024), 0) == source
    return jnp.where(hit, F32(1), F32(0)).astype(BF16)


WEIGHTY = 32 << 30


def run_copies(sem_ref, pairs):
    copies = [pltpu.make_async_copy(a, b, sem_ref.at[i]) for i, (a, b) in enumerate(pairs)]
    for copy in copies:
        copy.start()
    for copy in copies:
        copy.wait()


def master_kernel(master_ref, out_ref, rows_ref, sem_ref):
    run_copies(sem_ref, [(master_ref, rows_ref)])
    weight = rows_ref[...].astype(BF16)
    for z in range(DEPTH):
        out_ref[z] = weight


def spread_kernel(rows_ref, out_ref, sem_ref):
    run_copies(sem_ref, [(rows_ref, out_ref.at[i]) for i in range(out_ref.shape[0])])


def whole_columns(whole_ref, cols_ref):
    tok = whole_ref.shape[0]
    return [
        (
            whole_ref.at[:, zh * 1024 + y * 256 : zh * 1024 + y * 256 + 256],
            cols_ref.at[y * tok : (y + 1) * tok, zh * 256 : (zh + 1) * 256],
        )
        for y in range(4)
        for zh in range(4)
    ]


def split_kernel(at_ref, hidden_ref, own_ref, other_ref, send_ref, cols_ref, matrix_ref, sem_ref):
    tok = own_ref.shape[0]
    half = own_ref.shape[1]
    copies = [pltpu.make_async_copy(a, b, sem_ref.at[i]) for i, (a, b) in enumerate(whole_columns(hidden_ref, cols_ref))]
    for copy in copies:
        copy.start()
    matrix_ref[...] = order_matrix(at_ref[0], at_ref[1])
    for copy in copies:
        copy.wait()
    moved = jnp.dot(cols_ref[...], matrix_ref[...], preferred_element_type=F32).astype(BF16)
    for y in range(4):
        rows = slice(y * tok, (y + 1) * tok)
        to = slice(y * 256, (y + 1) * 256)
        own_ref[:, to] = moved[rows, :256]
        other_ref[:, to] = moved[rows, 256:512]
        send_ref[:, to] = moved[rows, 512:768]
        send_ref[:, half + y * 256 : half + (y + 1) * 256] = moved[rows, 768:]


def join_kernel(at_ref, keep_ref, got_ref, out_ref, cols_ref, moved_ref, matrix_ref, sem_ref):
    tok = keep_ref.shape[0]
    half = keep_ref.shape[1] // 2
    matrix_ref[...] = return_matrix(at_ref[0], at_ref[1])
    for y in range(4):
        for t, ref in enumerate((keep_ref, got_ref)):
            for c in range(2):
                to = (t * 2 + c) * 256
                cols_ref[y * tok : (y + 1) * tok, to : to + 256] = ref[:, c * half + y * 256 : c * half + y * 256 + 256]
    moved_ref[...] = jnp.dot(cols_ref[...], matrix_ref[...], preferred_element_type=F32).astype(BF16)
    run_copies(sem_ref, [(b, a) for a, b in whole_columns(out_ref, moved_ref)])


def first_kernel(near_ref, far_ref, weight_ref, near_out_ref, far_out_ref):
    half = near_ref.shape[1]
    near_out_ref[...] = jnp.dot(near_ref[...], weight_ref[...], preferred_element_type=F32)
    far_out_ref[...] = jnp.dot(far_ref[:, :half], weight_ref[...], preferred_element_type=F32)


def second_kernel(rows_ref, weight_ref, first_ref, out_ref):
    rows = rows_ref[:, rows_ref.shape[1] - weight_ref.shape[0] :]
    total = first_ref[...] + jnp.dot(rows, weight_ref[...], preferred_element_type=F32)
    out_ref[...] = total.astype(out_ref.dtype)


def flip_kernel(near_own_ref, near_other_ref, far_ref, own_ref, other_ref):
    tok, half = near_own_ref.shape
    own_ref[:, :tok] = near_own_ref[...].T
    own_ref[:, tok:] = far_ref[:, :half].T
    other_ref[:, :tok] = near_other_ref[...].T
    other_ref[:, tok:] = far_ref[:, half:].T


def part_kernel(hidden_ref, near_ref, far_ref, out_ref):
    grad = jnp.concatenate([near_ref[...], far_ref[...]], axis=0)
    out_ref[...] = jnp.dot(hidden_ref[...], grad, preferred_element_type=F32).astype(BF16)


def fold_kernel(hidden_ref, near_ref, far_ref, sent_ref, out_ref, rows_ref, sem_ref):
    grad = jnp.concatenate([near_ref[...], far_ref[...]], axis=0)
    step = out_ref.shape[1]
    copies = []
    blocks = 4
    for i in range(0, out_ref.shape[0], blocks):
        at = slice(i * step, (i + blocks) * step)
        part = jnp.dot(hidden_ref[at], grad, preferred_element_type=F32)
        part = (part + sent_ref[at].astype(F32)).astype(BF16)
        for j in range(blocks):
            rows_ref[i + j] = part[j * step : (j + 1) * step]
        to = pl.ds(i, blocks)
        copies.append(pltpu.make_async_copy(rows_ref.at[to], out_ref.at[to], sem_ref.at[i // blocks]))
        copies[-1].start()
    for copy in copies:
        copy.wait()


def back_kernel(near_ref, far_ref, own_ref, other_ref, keep_ref, send_ref):
    tok = near_ref.shape[0]
    half = own_ref.shape[0]
    grad = jnp.concatenate([near_ref[...], far_ref[...]], axis=0)
    for c, weight_ref in enumerate((own_ref, other_ref)):
        rows = lax.dot_general(
            grad, weight_ref[...], (((1,), (1,)), ((), ())), preferred_element_type=F32
        ).astype(BF16)
        keep_ref[:, c * half : (c + 1) * half] = rows[:tok]
        send_ref[:, c * half : (c + 1) * half] = rows[tok:]


def sum_kernel(parts_ref, out_ref):
    total = parts_ref[0].astype(F32)
    for i in range(1, parts_ref.shape[0]):
        total = total + parts_ref[i].astype(F32)
    total = total.astype(BF16)
    rows = out_ref.shape[1]
    for z in range(out_ref.shape[0]):
        out_ref[z ^ GATHER_FIRST ^ REDUCE_FIRST] = total[z * rows : (z + 1) * rows]


def probs_kernel(queries_ref, keys_ref, seg_row_ref, seg_col_ref, out_ref):
    tok = queries_ref.shape[0]
    rows = lax.broadcasted_iota(jnp.int32, (tok, tok), 0)
    cols = lax.broadcasted_iota(jnp.int32, (tok, tok), 1)
    allowed = (seg_col_ref[...] == seg_row_ref[...]) & (cols <= rows)
    scale = F32(1.0 / np.sqrt(HD))
    for j in range(VH):
        key = keys_ref[:, j * HD : (j + 1) * HD]
        for h in range(GROUPS):
            at = (j * GROUPS + h) * HD
            scores = lax.dot_general(
                queries_ref[:, at : at + HD], key, (((1,), (1,)), ((), ())), preferred_element_type=F32
            )
            scores = jnp.where(allowed, scores * scale, F32(-1000000000.0))
            expos = jnp.exp(scores - jnp.max(scores, axis=-1, keepdims=True))
            total = jnp.sum(expos, axis=-1, keepdims=True)
            out_ref[j, h * tok : (h + 1) * tok, :] = (expos / total).astype(BF16)


def states_kernel(moment_ref, second_ref, master_ref, moment_out_ref, second_out_ref, master_out_ref, decay_ref):
    moment_out_ref[...] = beta_one * moment_ref[...]
    second_out_ref[...] = beta_two * second_ref[...]
    master_out_ref[...] = master_ref[...]
    decay_ref[...] = decay_rate * master_ref[...]


def attend_kernel(near_ref, sent_ref, probs_ref, attended_ref, grad_ref, rows_ref, sem_ref):
    tok = near_ref.shape[0]
    wide = GROUPS * HD
    copies = []
    for j in range(VH):
        cols = slice(j * HD, (j + 1) * HD)
        value = (near_ref[:, cols] + sent_ref[:, cols].astype(F32)).astype(BF16)
        attended = jnp.dot(probs_ref[j], value, preferred_element_type=F32).astype(BF16)
        for h in range(GROUPS):
            rows_ref[j, :, h * HD : (h + 1) * HD] = attended[h * tok : (h + 1) * tok]
        copies.append(
            pltpu.make_async_copy(rows_ref.at[j], attended_ref.at[:, j * wide : (j + 1) * wide], sem_ref.at[j])
        )
        copies[-1].start()
        grad_ref[:, cols] = lax.dot_general(
            probs_ref[j], attended, (((0,), (0,)), ((), ())), preferred_element_type=F32
        ).astype(BF16)
    for copy in copies:
        copy.wait()


SMEM = pl.BlockSpec(memory_space=pltpu.SMEM)
VMEM = pl.BlockSpec(memory_space=pltpu.VMEM)
HBM = pl.BlockSpec(memory_space=pltpu.HBM)


def copies(n):
    return pltpu.SemaphoreType.DMA((n,))


def call(kernel, out_shape, flops, nbytes, *args, scratch=(), out=None, hbm=(), late=()):
    specs = [SMEM if a.dtype == jnp.int32 and a.ndim == 1 else VMEM for a in args]
    specs = [HBM if i in hbm else spec for i, spec in enumerate(specs)]
    if out is None:
        out = (VMEM,) * len(out_shape) if isinstance(out_shape, tuple) else VMEM
    if out is HBM:
        out_shape = pltpu.HBM(out_shape.shape, out_shape.dtype)
    if late:
        out_shape = tuple(pltpu.HBM(o.shape, o.dtype) if i in late else o for i, o in enumerate(out_shape))
    args = [pltpu.with_memory_space_constraint(a, pltpu.HBM) if i in hbm else a for i, a in enumerate(args)]
    return pl.pallas_call(
        kernel,
        out_shape=out_shape,
        in_specs=specs,
        out_specs=out,
        scratch_shapes=scratch,
        compiler_params=pltpu.CompilerParams(vmem_limit_bytes=24 * 1024 * 1024),
        cost_estimate=pl.CostEstimate(flops=flops, bytes_accessed=nbytes, transcendentals=0),
    )(*args)


def swap_core(array):
    return lax.ppermute(array, "c", [(0, 1), (1, 0)])


def swap_pair(array):
    return lax.ppermute(array, "zll", [(0, 1), (1, 0)])


def exchange(blocks, members, first):
    ids = np.arange(np.prod(SIZES)).reshape(SIZES)
    last = [AXES.index(a) for a in members]
    ids = ids.transpose([i for i in range(len(SIZES)) if i not in last] + last).reshape(-1, blocks.shape[0])
    groups = ids[:, np.arange(blocks.shape[0]) ^ first].tolist()
    return lax.all_to_all(blocks, AXES, split_axis=0, concat_axis=0, axis_index_groups=groups, tiled=True)


def exchange_z(blocks, first):
    return exchange(blocks, ("zlh", "zh"), first)


def exchange_plane(blocks):
    return exchange(blocks, ("y", "x"), 0)


def per_device(hidden_in, queries, keys, lengths, master, moment, second):
    tok, width = hidden_in.shape
    kv = keys.shape[1]
    rows = master.shape[0]
    feats = width // 4
    at = jnp.stack([lax.axis_index("zll"), lax.axis_index("c")]).astype(jnp.int32)
    block = jax.ShapeDtypeStruct((tok, 2 * feats), BF16)
    half = jax.ShapeDtypeStruct((tok, feats), BF16)
    value = jax.ShapeDtypeStruct((tok, kv), BF16)
    total = jax.ShapeDtypeStruct((tok, kv), F32)
    matrix = pltpu.VMEM((1024, 1024), BF16)
    cols = pltpu.VMEM((4 * tok, 1024), BF16)

    weight = call(
        master_kernel,
        jax.ShapeDtypeStruct((DEPTH, rows, kv), BF16),
        0,
        1 << 17,
        master,
        scratch=[pltpu.VMEM((rows, kv), F32), copies(1)],
        hbm=(0,),
    )
    weight, hidden_in = lax.optimization_barrier((weight, hidden_in))
    weight = exchange_z(weight, GATHER_FIRST).reshape(DEPTH * rows, kv)

    near_own, near_other, send = call(
        split_kernel,
        (half, half, block),
        8 * tok * 1024 * 1024,
        2 << 20,
        at,
        hidden_in,
        scratch=[cols, matrix, copies(16)],
        hbm=(1,),
        late=(0, 1),
    )
    far = swap_pair(send)

    weight = call(
        spread_kernel,
        jax.ShapeDtypeStruct((PLANE, DEPTH * rows, kv), BF16),
        0,
        1 << 20,
        weight,
        scratch=[copies(PLANE)],
        out=HBM,
    )
    weight, keys = lax.optimization_barrier((weight, keys))
    weight = exchange_plane(weight).reshape(PLANE * DEPTH * rows, kv)

    ends = jnp.cumsum(lengths[0])
    seg = jnp.sum((jnp.arange(tok, dtype=jnp.int32)[:, None] >= ends[None, :]).astype(jnp.int32), axis=1)
    (probs,) = call(
        probs_kernel,
        (jax.ShapeDtypeStruct((VH, GROUPS * tok, tok), BF16),),
        4 * tok * tok * QH * HD,
        8 << 20,
        queries,
        keys,
        seg[None, :],
        seg[:, None],
        late=(0,),
    )
    flipped = jax.ShapeDtypeStruct((feats, 2 * tok), BF16)
    columns_own, columns_other = call(
        flip_kernel, (flipped, flipped), WEIGHTY // 6, 2 << 20, near_own, near_other, far, late=(0, 1)
    )
    weight, near_own, near_other, far, columns_own, columns_other, probs = lax.optimization_barrier(
        (weight, near_own, near_other, far, columns_own, columns_other, probs)
    )
    weight_other = swap_core(weight)

    flops = 2 * tok * feats * kv
    near, far_values = call(first_kernel, (total, total), 2 * flops, 2 << 20, near_own, far, weight)
    sent = swap_pair(call(second_kernel, value, flops, 2 << 20, far, weight_other, far_values))
    near = call(second_kernel, total, flops, 2 << 20, near_other, weight_other, near)
    attended, grad = call(
        attend_kernel,
        (jax.ShapeDtypeStruct((tok, QH * HD), BF16), value),
        4 * tok * tok * QH * HD,
        4 << 20,
        near,
        sent,
        probs,
        scratch=[pltpu.VMEM((VH, tok, GROUPS * HD), BF16), copies(VH)],
        out=(HBM, VMEM),
    )
    grad_far = swap_pair(grad)

    part = call(
        part_kernel,
        jax.ShapeDtypeStruct((feats, kv), BF16),
        2 * flops,
        2 << 20,
        columns_other,
        grad,
        grad_far,
    )
    part = call(
        fold_kernel,
        jax.ShapeDtypeStruct((PLANE, DEPTH * rows, kv), BF16),
        2 * flops,
        2 << 20,
        columns_own,
        grad,
        grad_far,
        swap_core(part),
        scratch=[pltpu.VMEM((PLANE, DEPTH * rows, kv), BF16), copies(PLANE // 4)],
        out=HBM,
    )
    keep, send = call(
        back_kernel, (block, block), 8 * tok * feats * kv, 4 << 20, grad, grad_far, weight, weight_other, late=(0,)
    )
    part, keep, send = lax.optimization_barrier((part, keep, send))
    grad_hidden = call(
        join_kernel,
        jax.ShapeDtypeStruct((tok, width), BF16),
        8 * tok * 1024 * 1024,
        2 << 20,
        at,
        keep,
        swap_pair(send),
        scratch=[cols, cols, matrix, copies(16)],
        out=HBM,
    )

    part = exchange_plane(part)
    part = call(sum_kernel, jax.ShapeDtypeStruct((DEPTH, rows, kv), BF16), 0, 1 << 20, part)
    part, grad_hidden, moment, second, master = lax.optimization_barrier(
        (part, grad_hidden, moment, second, master)
    )
    part = exchange_z(part, REDUCE_FIRST)
    moment, second, master, decay = call(
        states_kernel, (jax.ShapeDtypeStruct(master.shape, F32),) * 4, 0, 1 << 17, moment, second, master
    )
    gradient = jnp.sum(part.astype(F32), axis=0) / F32(tok * 512)

    moment_new = moment + (1.0 - beta_one) * gradient
    second_new = second + (1.0 - beta_two) * gradient * gradient
    moment_hat = moment_new / (1.0 - beta_one**10)
    second_hat = second_new / (1.0 - beta_two**10)
    master_new = master - learn_rate * (
        moment_hat / (jnp.sqrt(second_hat) + adam_eps) + decay
    )
    return (attended, grad_hidden, master_new, moment_new, second_new)


def solution(mesh):
    named = Mesh(mesh.devices.reshape(SIZES), AXES)
    return jax.shard_map(
        per_device,
        mesh=named,
        in_specs=(TOK_SPEC, TOK_SPEC, TOK_SPEC, TOK_SPEC, ROW_SPEC, ROW_SPEC, ROW_SPEC),
        out_specs=(TOK_SPEC, TOK_SPEC, ROW_SPEC, ROW_SPEC, ROW_SPEC),
        check_vma=False,
    )
```

```python
import jax
import jax.numpy as jnp
import numpy as np
from jax import lax
from jax.experimental import pallas as pl
from jax.experimental.pallas import tpu as pltpu
from jax.sharding import Mesh
from jax.sharding import PartitionSpec as P

HD = 128
VH = 4
QH = 32
GROUPS = QH // VH

beta_one = 0.9
beta_two = 0.95
adam_eps = 1e-08
learn_rate = 0.001
decay_rate = 0.1

AXES = ("zlh", "zll", "x", "c", "zh", "y")
SIZES = (2, 2, 4, 2, 4, 4)
TOK_SPEC = P(AXES, None)
ROW_SPEC = P(("zh", "y", "zlh", "zll", "x", "c"), None)
DEPTH = 8
PLANE = 16
GATHER_FIRST = 6
REDUCE_FIRST = 2

F32 = jnp.float32
BF16 = jnp.bfloat16


def order_matrix(zll, core):
    to = lax.broadcasted_iota(jnp.int32, (1, 1024), 1)
    z = ((to >> 3) & 7) ^ GATHER_FIRST
    source = (z & 3) * 256 + (z >> 2) * 128 + ((to >> 6) & 3) * 16 + (to & 7)
    source = source + ((to >> 9) ^ zll) * 64 + (((to >> 8) & 1) ^ core) * 8
    hit = lax.broadcasted_iota(jnp.int32, (1024, 1024), 0) == source
    return jnp.where(hit, F32(1), F32(0)).astype(BF16)


def return_matrix(zll, core):
    to = lax.broadcasted_iota(jnp.int32, (1, 1024), 1)
    z = (((to >> 7) & 1) * 4 + (to >> 8)) ^ GATHER_FIRST
    source = z * 8 + ((to >> 4) & 3) * 64 + (to & 7)
    source = source + (((to >> 6) & 1) ^ zll) * 512 + (((to >> 3) & 1) ^ core) * 256
    hit = lax.broadcasted_iota(jnp.int32, (1024, 1024), 0) == source
    return jnp.where(hit, F32(1), F32(0)).astype(BF16)


WEIGHTY = 32 << 30


def run_copies(sem_ref, pairs):
    copies = [pltpu.make_async_copy(a, b, sem_ref.at[i]) for i, (a, b) in enumerate(pairs)]
    for copy in copies:
        copy.start()
    for copy in copies:
        copy.wait()


def master_kernel(master_ref, out_ref, rows_ref, sem_ref):
    run_copies(sem_ref, [(master_ref, rows_ref)])
    weight = rows_ref[...].astype(BF16)
    for z in range(DEPTH):
        out_ref[z] = weight


def spread_kernel(rows_ref, out_ref, sem_ref):
    run_copies(sem_ref, [(rows_ref, out_ref.at[i]) for i in range(out_ref.shape[0])])


def whole_columns(whole_ref, cols_ref):
    tok = whole_ref.shape[0]
    return [
        (
            whole_ref.at[:, zh * 1024 + y * 256 : zh * 1024 + y * 256 + 256],
            cols_ref.at[y * tok : (y + 1) * tok, zh * 256 : (zh + 1) * 256],
        )
        for y in range(4)
        for zh in range(4)
    ]


def split_kernel(at_ref, hidden_ref, own_ref, other_ref, send_ref, cols_ref, matrix_ref, sem_ref):
    tok = own_ref.shape[0]
    half = own_ref.shape[1]
    copies = [pltpu.make_async_copy(a, b, sem_ref.at[i]) for i, (a, b) in enumerate(whole_columns(hidden_ref, cols_ref))]
    for copy in copies:
        copy.start()
    matrix_ref[...] = order_matrix(at_ref[0], at_ref[1])
    for copy in copies:
        copy.wait()
    moved = jnp.dot(cols_ref[...], matrix_ref[...], preferred_element_type=F32).astype(BF16)
    for y in range(4):
        rows = slice(y * tok, (y + 1) * tok)
        to = slice(y * 256, (y + 1) * 256)
        own_ref[:, to] = moved[rows, :256]
        other_ref[:, to] = moved[rows, 256:512]
        send_ref[:, to] = moved[rows, 512:768]
        send_ref[:, half + y * 256 : half + (y + 1) * 256] = moved[rows, 768:]


def join_kernel(at_ref, keep_ref, got_ref, out_ref, cols_ref, moved_ref, matrix_ref, sem_ref):
    tok = keep_ref.shape[0]
    half = keep_ref.shape[1] // 2
    matrix_ref[...] = return_matrix(at_ref[0], at_ref[1])
    for y in range(4):
        for t, ref in enumerate((keep_ref, got_ref)):
            for c in range(2):
                to = (t * 2 + c) * 256
                cols_ref[y * tok : (y + 1) * tok, to : to + 256] = ref[:, c * half + y * 256 : c * half + y * 256 + 256]
    moved_ref[...] = jnp.dot(cols_ref[...], matrix_ref[...], preferred_element_type=F32).astype(BF16)
    run_copies(sem_ref, [(b, a) for a, b in whole_columns(out_ref, moved_ref)])


def first_kernel(near_ref, far_ref, weight_ref, near_out_ref, far_out_ref):
    half = near_ref.shape[1]
    near_out_ref[...] = jnp.dot(near_ref[...], weight_ref[...], preferred_element_type=F32)
    far_out_ref[...] = jnp.dot(far_ref[:, :half], weight_ref[...], preferred_element_type=F32)


def second_kernel(rows_ref, weight_ref, first_ref, out_ref):
    rows = rows_ref[:, rows_ref.shape[1] - weight_ref.shape[0] :]
    total = first_ref[...] + jnp.dot(rows, weight_ref[...], preferred_element_type=F32)
    out_ref[...] = total.astype(out_ref.dtype)


def flip_kernel(near_own_ref, near_other_ref, far_ref, own_ref, other_ref):
    tok, half = near_own_ref.shape
    own_ref[:, :tok] = near_own_ref[...].T
    own_ref[:, tok:] = far_ref[:, :half].T
    other_ref[:, :tok] = near_other_ref[...].T
    other_ref[:, tok:] = far_ref[:, half:].T


def part_kernel(hidden_ref, near_ref, far_ref, out_ref):
    grad = jnp.concatenate([near_ref[...], far_ref[...]], axis=0)
    out_ref[...] = jnp.dot(hidden_ref[...], grad, preferred_element_type=F32).astype(BF16)


def fold_kernel(hidden_ref, near_ref, far_ref, sent_ref, out_ref, rows_ref, sem_ref):
    grad = jnp.concatenate([near_ref[...], far_ref[...]], axis=0)
    step = out_ref.shape[1]
    copies = []
    blocks = 4
    for i in range(0, out_ref.shape[0], blocks):
        at = slice(i * step, (i + blocks) * step)
        part = jnp.dot(hidden_ref[at], grad, preferred_element_type=F32)
        part = (part + sent_ref[at].astype(F32)).astype(BF16)
        for j in range(blocks):
            rows_ref[i + j] = part[j * step : (j + 1) * step]
        to = pl.ds(i, blocks)
        copies.append(pltpu.make_async_copy(rows_ref.at[to], out_ref.at[to], sem_ref.at[i // blocks]))
        copies[-1].start()
    for copy in copies:
        copy.wait()


def back_kernel(near_ref, far_ref, own_ref, other_ref, keep_ref, send_ref):
    tok = near_ref.shape[0]
    half = own_ref.shape[0]
    grad = jnp.concatenate([near_ref[...], far_ref[...]], axis=0)
    for c, weight_ref in enumerate((own_ref, other_ref)):
        rows = lax.dot_general(
            grad, weight_ref[...], (((1,), (1,)), ((), ())), preferred_element_type=F32
        ).astype(BF16)
        keep_ref[:, c * half : (c + 1) * half] = rows[:tok]
        send_ref[:, c * half : (c + 1) * half] = rows[tok:]


def sum_kernel(parts_ref, out_ref):
    total = parts_ref[0].astype(F32)
    for i in range(1, parts_ref.shape[0]):
        total = total + parts_ref[i].astype(F32)
    total = total.astype(BF16)
    rows = out_ref.shape[1]
    for z in range(out_ref.shape[0]):
        out_ref[z ^ GATHER_FIRST ^ REDUCE_FIRST] = total[z * rows : (z + 1) * rows]


def probs_kernel(queries_ref, keys_ref, seg_row_ref, seg_col_ref, out_ref, turned_ref):
    tok = queries_ref.shape[0]
    rows = lax.broadcasted_iota(jnp.int32, (tok, tok), 0)
    cols = lax.broadcasted_iota(jnp.int32, (tok, tok), 1)
    allowed = (seg_col_ref[...] == seg_row_ref[...]) & (cols <= rows)
    scale = F32(1.0 / np.sqrt(HD))
    for j in range(VH):
        key = keys_ref[:, j * HD : (j + 1) * HD]
        for h in range(GROUPS):
            at = (j * GROUPS + h) * HD
            scores = lax.dot_general(
                queries_ref[:, at : at + HD], key, (((1,), (1,)), ((), ())), preferred_element_type=F32
            )
            scores = jnp.where(allowed, scores * scale, F32(-1000000000.0))
            expos = jnp.exp(scores - jnp.max(scores, axis=-1, keepdims=True))
            total = jnp.sum(expos, axis=-1, keepdims=True)
            probs = (expos / total).astype(BF16)
            out_ref[j, h * tok : (h + 1) * tok, :] = probs
            turned_ref[j, :, h * tok : (h + 1) * tok] = probs.T


def states_kernel(moment_ref, second_ref, master_ref, moment_out_ref, second_out_ref, master_out_ref, decay_ref):
    moment_out_ref[...] = beta_one * moment_ref[...]
    second_out_ref[...] = beta_two * second_ref[...]
    master_out_ref[...] = master_ref[...]
    decay_ref[...] = decay_rate * master_ref[...]


def attend_kernel(near_ref, sent_ref, probs_ref, turned_ref, attended_ref, grad_ref, rows_ref, sem_ref):
    tok = near_ref.shape[0]
    wide = GROUPS * HD
    copies = []
    for j in range(VH):
        cols = slice(j * HD, (j + 1) * HD)
        value = (near_ref[:, cols] + sent_ref[:, cols].astype(F32)).astype(BF16)
        attended = jnp.dot(probs_ref[j], value, preferred_element_type=F32).astype(BF16)
        for h in range(GROUPS):
            rows_ref[j, :, h * HD : (h + 1) * HD] = attended[h * tok : (h + 1) * tok]
        copies.append(
            pltpu.make_async_copy(rows_ref.at[j], attended_ref.at[:, j * wide : (j + 1) * wide], sem_ref.at[j])
        )
        copies[-1].start()
        grad_ref[:, cols] = jnp.dot(turned_ref[j], attended, preferred_element_type=F32).astype(BF16)
    for copy in copies:
        copy.wait()


SMEM = pl.BlockSpec(memory_space=pltpu.SMEM)
VMEM = pl.BlockSpec(memory_space=pltpu.VMEM)
HBM = pl.BlockSpec(memory_space=pltpu.HBM)


def copies(n):
    return pltpu.SemaphoreType.DMA((n,))


def call(kernel, out_shape, flops, nbytes, *args, scratch=(), out=None, hbm=(), late=()):
    specs = [SMEM if a.dtype == jnp.int32 and a.ndim == 1 else VMEM for a in args]
    specs = [HBM if i in hbm else spec for i, spec in enumerate(specs)]
    if out is None:
        out = (VMEM,) * len(out_shape) if isinstance(out_shape, tuple) else VMEM
    if out is HBM:
        out_shape = pltpu.HBM(out_shape.shape, out_shape.dtype)
    if late:
        out_shape = tuple(pltpu.HBM(o.shape, o.dtype) if i in late else o for i, o in enumerate(out_shape))
    args = [pltpu.with_memory_space_constraint(a, pltpu.HBM) if i in hbm else a for i, a in enumerate(args)]
    return pl.pallas_call(
        kernel,
        out_shape=out_shape,
        in_specs=specs,
        out_specs=out,
        scratch_shapes=scratch,
        compiler_params=pltpu.CompilerParams(vmem_limit_bytes=24 * 1024 * 1024),
        cost_estimate=pl.CostEstimate(flops=flops, bytes_accessed=nbytes, transcendentals=0),
    )(*args)


def swap_core(array):
    return lax.ppermute(array, "c", [(0, 1), (1, 0)])


def swap_pair(array):
    return lax.ppermute(array, "zll", [(0, 1), (1, 0)])


def exchange(blocks, members, first):
    ids = np.arange(np.prod(SIZES)).reshape(SIZES)
    last = [AXES.index(a) for a in members]
    ids = ids.transpose([i for i in range(len(SIZES)) if i not in last] + last).reshape(-1, blocks.shape[0])
    groups = ids[:, np.arange(blocks.shape[0]) ^ first].tolist()
    return lax.all_to_all(blocks, AXES, split_axis=0, concat_axis=0, axis_index_groups=groups, tiled=True)


def exchange_z(blocks, first):
    return exchange(blocks, ("zlh", "zh"), first)


def exchange_plane(blocks):
    return exchange(blocks, ("y", "x"), 0)


def per_device(hidden_in, queries, keys, lengths, master, moment, second):
    tok, width = hidden_in.shape
    kv = keys.shape[1]
    rows = master.shape[0]
    feats = width // 4
    at = jnp.stack([lax.axis_index("zll"), lax.axis_index("c")]).astype(jnp.int32)
    block = jax.ShapeDtypeStruct((tok, 2 * feats), BF16)
    half = jax.ShapeDtypeStruct((tok, feats), BF16)
    value = jax.ShapeDtypeStruct((tok, kv), BF16)
    total = jax.ShapeDtypeStruct((tok, kv), F32)
    matrix = pltpu.VMEM((1024, 1024), BF16)
    cols = pltpu.VMEM((4 * tok, 1024), BF16)

    weight = call(
        master_kernel,
        jax.ShapeDtypeStruct((DEPTH, rows, kv), BF16),
        0,
        1 << 17,
        master,
        scratch=[pltpu.VMEM((rows, kv), F32), copies(1)],
        hbm=(0,),
    )
    weight, hidden_in = lax.optimization_barrier((weight, hidden_in))
    weight = exchange_z(weight, GATHER_FIRST).reshape(DEPTH * rows, kv)

    near_own, near_other, send = call(
        split_kernel,
        (half, half, block),
        8 * tok * 1024 * 1024,
        2 << 20,
        at,
        hidden_in,
        scratch=[cols, matrix, copies(16)],
        hbm=(1,),
        late=(0, 1),
    )
    far = swap_pair(send)

    weight = call(
        spread_kernel,
        jax.ShapeDtypeStruct((PLANE, DEPTH * rows, kv), BF16),
        0,
        1 << 20,
        weight,
        scratch=[copies(PLANE)],
        out=HBM,
    )
    weight, keys = lax.optimization_barrier((weight, keys))
    weight = exchange_plane(weight).reshape(PLANE * DEPTH * rows, kv)

    ends = jnp.cumsum(lengths[0])
    seg = jnp.sum((jnp.arange(tok, dtype=jnp.int32)[:, None] >= ends[None, :]).astype(jnp.int32), axis=1)
    probs, turned = call(
        probs_kernel,
        (
            jax.ShapeDtypeStruct((VH, GROUPS * tok, tok), BF16),
            jax.ShapeDtypeStruct((VH, tok, GROUPS * tok), BF16),
        ),
        4 * tok * tok * QH * HD,
        8 << 20,
        queries,
        keys,
        seg[None, :],
        seg[:, None],
        late=(0, 1),
    )
    flipped = jax.ShapeDtypeStruct((feats, 2 * tok), BF16)
    columns_own, columns_other = call(
        flip_kernel, (flipped, flipped), WEIGHTY // 6, 2 << 20, near_own, near_other, far, late=(0, 1)
    )
    weight, near_own, near_other, far, columns_own, columns_other, probs, turned = lax.optimization_barrier(
        (weight, near_own, near_other, far, columns_own, columns_other, probs, turned)
    )
    weight_other = swap_core(weight)

    flops = 2 * tok * feats * kv
    near, far_values = call(first_kernel, (total, total), 2 * flops, 2 << 20, near_own, far, weight)
    sent = swap_pair(call(second_kernel, value, flops, 2 << 20, far, weight_other, far_values))
    near = call(second_kernel, total, flops, 2 << 20, near_other, weight_other, near)
    attended, grad = call(
        attend_kernel,
        (jax.ShapeDtypeStruct((tok, QH * HD), BF16), value),
        4 * tok * tok * QH * HD,
        4 << 20,
        near,
        sent,
        probs,
        turned,
        scratch=[pltpu.VMEM((VH, tok, GROUPS * HD), BF16), copies(VH)],
        out=(HBM, VMEM),
    )
    grad_far = swap_pair(grad)

    part = call(
        part_kernel,
        jax.ShapeDtypeStruct((feats, kv), BF16),
        2 * flops,
        2 << 20,
        columns_other,
        grad,
        grad_far,
    )
    part = call(
        fold_kernel,
        jax.ShapeDtypeStruct((PLANE, DEPTH * rows, kv), BF16),
        2 * flops,
        2 << 20,
        columns_own,
        grad,
        grad_far,
        swap_core(part),
        scratch=[pltpu.VMEM((PLANE, DEPTH * rows, kv), BF16), copies(PLANE // 4)],
        out=HBM,
    )
    keep, send = call(
        back_kernel, (block, block), 8 * tok * feats * kv, 4 << 20, grad, grad_far, weight, weight_other, late=(0,)
    )
    part, keep, send, moment, second, master = lax.optimization_barrier(
        (part, keep, send, moment, second, master)
    )
    moment, second, master, decay = call(
        states_kernel, (jax.ShapeDtypeStruct(master.shape, F32),) * 4, 0, 1 << 17, moment, second, master
    )
    grad_hidden = call(
        join_kernel,
        jax.ShapeDtypeStruct((tok, width), BF16),
        WEIGHTY,
        2 << 20,
        at,
        keep,
        swap_pair(send),
        scratch=[cols, cols, matrix, copies(16)],
        out=HBM,
    )

    part = exchange_plane(part)
    part = call(sum_kernel, jax.ShapeDtypeStruct((DEPTH, rows, kv), BF16), 0, 1 << 20, part)
    part = exchange_z(part, REDUCE_FIRST)
    gradient = jnp.sum(part.astype(F32), axis=0) / F32(tok * 512)

    moment_new = moment + (1.0 - beta_one) * gradient
    second_new = second + (1.0 - beta_two) * gradient * gradient
    moment_hat = moment_new / (1.0 - beta_one**10)
    second_hat = second_new / (1.0 - beta_two**10)
    master_new = master - learn_rate * (
        moment_hat / (jnp.sqrt(second_hat) + adam_eps) + decay
    )
    return (attended, grad_hidden, master_new, moment_new, second_new)


def solution(mesh):
    named = Mesh(mesh.devices.reshape(SIZES), AXES)
    return jax.shard_map(
        per_device,
        mesh=named,
        in_specs=(TOK_SPEC, TOK_SPEC, TOK_SPEC, TOK_SPEC, ROW_SPEC, ROW_SPEC, ROW_SPEC),
        out_specs=(TOK_SPEC, TOK_SPEC, ROW_SPEC, ROW_SPEC, ROW_SPEC),
        check_vma=False,
    )
```

```python
import functools

import jax
import jax.numpy as jnp
import numpy as np
from jax import lax
from jax.experimental import pallas as pl
from jax.experimental.pallas import tpu as pltpu
from jax.sharding import Mesh
from jax.sharding import PartitionSpec as P

HD = 128
VH = 4
QH = 32
GROUPS = QH // VH

beta_one = 0.9
beta_two = 0.95
adam_eps = 1e-08
learn_rate = 0.001
decay_rate = 0.1

AXES = ("zlh", "zll", "x", "c", "zh", "y")
SIZES = (2, 2, 4, 2, 4, 4)
TOK_SPEC = P(AXES, None)
ROW_SPEC = P(("zh", "y", "zlh", "zll", "x", "c"), None)
DEPTH = 8
PLANE = 16
GATHER_FIRST = 6
REDUCE_FIRST = 2

F32 = jnp.float32
BF16 = jnp.bfloat16


def order_matrix(zll, core):
    to = lax.broadcasted_iota(jnp.int32, (1, 512), 1)
    z = ((to >> 3) & 7) ^ GATHER_FIRST
    source = (z & 3) * 256 + (z >> 2) * 128 + ((to >> 6) & 3) * 16 + (to & 7)
    source = source + zll * 64 + ((to >> 8) ^ core) * 8
    hit = lax.broadcasted_iota(jnp.int32, (1024, 512), 0) == source
    return jnp.where(hit, F32(1), F32(0)).astype(BF16)


def return_matrix(zll, core):
    to = lax.broadcasted_iota(jnp.int32, (1, 1024), 1)
    z = (((to >> 7) & 1) * 4 + (to >> 8)) ^ GATHER_FIRST
    source = z * 8 + ((to >> 4) & 3) * 64 + (to & 7)
    source = source + (((to >> 6) & 1) ^ zll) * 512 + (((to >> 3) & 1) ^ core) * 256
    hit = lax.broadcasted_iota(jnp.int32, (1024, 1024), 0) == source
    return jnp.where(hit, F32(1), F32(0)).astype(BF16)


WEIGHTY = 32 << 30


def run_copies(sem_ref, pairs):
    copies = [pltpu.make_async_copy(a, b, sem_ref.at[i]) for i, (a, b) in enumerate(pairs)]
    for copy in copies:
        copy.start()
    for copy in copies:
        copy.wait()


def master_kernel(master_ref, out_ref, rows_ref, sem_ref):
    run_copies(sem_ref, [(master_ref, rows_ref)])
    weight = rows_ref[...].astype(BF16)
    for z in range(DEPTH):
        out_ref[z] = weight


def spread_kernel(rows_ref, out_ref, sem_ref):
    run_copies(sem_ref, [(rows_ref, out_ref.at[i]) for i in range(out_ref.shape[0])])


def whole_columns(whole_ref, cols_ref):
    tok = whole_ref.shape[0]
    return [
        (
            whole_ref.at[:, zh * 1024 + y * 256 : zh * 1024 + y * 256 + 256],
            cols_ref.at[y * tok : (y + 1) * tok, zh * 256 : (zh + 1) * 256],
        )
        for y in range(4)
        for zh in range(4)
    ]


def split_kernel(far, at_ref, hidden_ref, *refs):
    out_refs, (cols_ref, matrix_ref, sem_ref) = refs[:-3], refs[-3:]
    tok = hidden_ref.shape[0]
    half = hidden_ref.shape[1] // 4
    copies = [pltpu.make_async_copy(a, b, sem_ref.at[i]) for i, (a, b) in enumerate(whole_columns(hidden_ref, cols_ref))]
    for copy in copies:
        copy.start()
    matrix_ref[...] = order_matrix(at_ref[0] ^ far, at_ref[1])
    for y in range(4):
        rows = slice(y * tok, (y + 1) * tok)
        for copy in copies[y * 4 : y * 4 + 4]:
            copy.wait()
        moved = jnp.dot(cols_ref[rows], matrix_ref[...], preferred_element_type=F32).astype(BF16)
        for c in range(2):
            at = (c * half if far else 0) + y * 256
            out_refs[0 if far else c][:, at : at + 256] = moved[:, c * 256 : (c + 1) * 256]


def join_kernel(at_ref, keep_ref, got_ref, out_ref, cols_ref, moved_ref, matrix_ref, sem_ref):
    tok = keep_ref.shape[0]
    half = keep_ref.shape[1] // 2
    matrix_ref[...] = return_matrix(at_ref[0], at_ref[1])
    for y in range(4):
        for t, ref in enumerate((keep_ref, got_ref)):
            for c in range(2):
                to = (t * 2 + c) * 256
                cols_ref[y * tok : (y + 1) * tok, to : to + 256] = ref[:, c * half + y * 256 : c * half + y * 256 + 256]
    moved_ref[...] = jnp.dot(cols_ref[...], matrix_ref[...], preferred_element_type=F32).astype(BF16)
    run_copies(sem_ref, [(b, a) for a, b in whole_columns(out_ref, moved_ref)])


def first_kernel(near_ref, far_ref, weight_ref, near_out_ref, far_out_ref):
    half = near_ref.shape[1]
    near_out_ref[...] = jnp.dot(near_ref[...], weight_ref[...], preferred_element_type=F32)
    far_out_ref[...] = jnp.dot(far_ref[:, :half], weight_ref[...], preferred_element_type=F32)


def second_kernel(rows_ref, weight_ref, first_ref, out_ref):
    rows = rows_ref[:, rows_ref.shape[1] - weight_ref.shape[0] :]
    total = first_ref[...] + jnp.dot(rows, weight_ref[...], preferred_element_type=F32)
    out_ref[...] = total.astype(out_ref.dtype)


def flip_kernel(near_own_ref, near_other_ref, far_ref, own_ref, other_ref):
    tok, half = near_own_ref.shape
    own_ref[:, :tok] = near_own_ref[...].T
    own_ref[:, tok:] = far_ref[:, :half].T
    other_ref[:, :tok] = near_other_ref[...].T
    other_ref[:, tok:] = far_ref[:, half:].T


def part_kernel(hidden_ref, near_ref, far_ref, out_ref):
    grad = jnp.concatenate([near_ref[...], far_ref[...]], axis=0)
    out_ref[...] = jnp.dot(hidden_ref[...], grad, preferred_element_type=F32).astype(BF16)


def fold_kernel(hidden_ref, near_ref, far_ref, sent_ref, out_ref, rows_ref, sem_ref):
    grad = jnp.concatenate([near_ref[...], far_ref[...]], axis=0)
    step = out_ref.shape[1]
    copies = []
    blocks = 4
    for i in range(0, out_ref.shape[0], blocks):
        at = slice(i * step, (i + blocks) * step)
        part = jnp.dot(hidden_ref[at], grad, preferred_element_type=F32)
        part = (part + sent_ref[at].astype(F32)).astype(BF16)
        for j in range(blocks):
            rows_ref[i + j] = part[j * step : (j + 1) * step]
        to = pl.ds(i, blocks)
        copies.append(pltpu.make_async_copy(rows_ref.at[to], out_ref.at[to], sem_ref.at[i // blocks]))
        copies[-1].start()
    for copy in copies:
        copy.wait()


def back_kernel(near_ref, far_ref, own_ref, other_ref, keep_ref, send_ref):
    tok = near_ref.shape[0]
    half = own_ref.shape[0]
    grad = jnp.concatenate([near_ref[...], far_ref[...]], axis=0)
    for c, weight_ref in enumerate((own_ref, other_ref)):
        rows = lax.dot_general(
            grad, weight_ref[...], (((1,), (1,)), ((), ())), preferred_element_type=F32
        ).astype(BF16)
        keep_ref[:, c * half : (c + 1) * half] = rows[:tok]
        send_ref[:, c * half : (c + 1) * half] = rows[tok:]


def sum_kernel(parts_ref, out_ref):
    total = parts_ref[0].astype(F32)
    for i in range(1, parts_ref.shape[0]):
        total = total + parts_ref[i].astype(F32)
    total = total.astype(BF16)
    rows = out_ref.shape[1]
    for z in range(out_ref.shape[0]):
        out_ref[z ^ GATHER_FIRST ^ REDUCE_FIRST] = total[z * rows : (z + 1) * rows]


def probs_kernel(queries_ref, keys_ref, seg_row_ref, seg_col_ref, out_ref, turned_ref):
    tok = queries_ref.shape[0]
    rows = lax.broadcasted_iota(jnp.int32, (tok, tok), 0)
    cols = lax.broadcasted_iota(jnp.int32, (tok, tok), 1)
    allowed = (seg_col_ref[...] == seg_row_ref[...]) & (cols <= rows)
    scale = F32(1.0 / np.sqrt(HD))
    for j in range(VH):
        key = keys_ref[:, j * HD : (j + 1) * HD]
        for h in range(GROUPS):
            at = (j * GROUPS + h) * HD
            scores = lax.dot_general(
                queries_ref[:, at : at + HD], key, (((1,), (1,)), ((), ())), preferred_element_type=F32
            )
            scores = jnp.where(allowed, scores * scale, F32(-1000000000.0))
            expos = jnp.exp(scores - jnp.max(scores, axis=-1, keepdims=True))
            total = jnp.sum(expos, axis=-1, keepdims=True)
            probs = (expos / total).astype(BF16)
            out_ref[j, h * tok : (h + 1) * tok, :] = probs
            turned_ref[j, :, h * tok : (h + 1) * tok] = probs.T


def states_kernel(moment_ref, second_ref, master_ref, moment_out_ref, second_out_ref, master_out_ref, decay_ref):
    moment_out_ref[...] = beta_one * moment_ref[...]
    second_out_ref[...] = beta_two * second_ref[...]
    master_out_ref[...] = master_ref[...]
    decay_ref[...] = decay_rate * master_ref[...]


def attend_kernel(near_ref, sent_ref, probs_ref, turned_ref, attended_ref, grad_ref, rows_ref, sem_ref):
    tok = near_ref.shape[0]
    wide = GROUPS * HD
    copies = []
    for j in range(VH):
        cols = slice(j * HD, (j + 1) * HD)
        value = (near_ref[:, cols] + sent_ref[:, cols].astype(F32)).astype(BF16)
        attended = jnp.dot(probs_ref[j], value, preferred_element_type=F32).astype(BF16)
        for h in range(GROUPS):
            rows_ref[j, :, h * HD : (h + 1) * HD] = attended[h * tok : (h + 1) * tok]
        copies.append(
            pltpu.make_async_copy(rows_ref.at[j], attended_ref.at[:, j * wide : (j + 1) * wide], sem_ref.at[j])
        )
        copies[-1].start()
        grad_ref[:, cols] = jnp.dot(turned_ref[j], attended, preferred_element_type=F32).astype(BF16)
    for copy in copies:
        copy.wait()


SMEM = pl.BlockSpec(memory_space=pltpu.SMEM)
VMEM = pl.BlockSpec(memory_space=pltpu.VMEM)
HBM = pl.BlockSpec(memory_space=pltpu.HBM)


def copies(n):
    return pltpu.SemaphoreType.DMA((n,))


def call(kernel, out_shape, flops, nbytes, *more, args=(), scratch=(), out=None, hbm=(), late=()):
    args = (*args, *more)
    specs = [SMEM if a.dtype == jnp.int32 and a.ndim == 1 else VMEM for a in args]
    specs = [HBM if i in hbm else spec for i, spec in enumerate(specs)]
    if out is None:
        out = (VMEM,) * len(out_shape) if isinstance(out_shape, tuple) else VMEM
    if out is HBM:
        out_shape = pltpu.HBM(out_shape.shape, out_shape.dtype)
    if late:
        out_shape = tuple(pltpu.HBM(o.shape, o.dtype) if i in late else o for i, o in enumerate(out_shape))
    args = [pltpu.with_memory_space_constraint(a, pltpu.HBM) if i in hbm else a for i, a in enumerate(args)]
    return pl.pallas_call(
        kernel,
        out_shape=out_shape,
        in_specs=specs,
        out_specs=out,
        scratch_shapes=scratch,
        compiler_params=pltpu.CompilerParams(vmem_limit_bytes=24 * 1024 * 1024),
        cost_estimate=pl.CostEstimate(flops=flops, bytes_accessed=nbytes, transcendentals=0),
    )(*args)


def swap_core(array):
    return lax.ppermute(array, "c", [(0, 1), (1, 0)])


def swap_pair(array):
    return lax.ppermute(array, "zll", [(0, 1), (1, 0)])


def exchange(blocks, members, first):
    ids = np.arange(np.prod(SIZES)).reshape(SIZES)
    last = [AXES.index(a) for a in members]
    ids = ids.transpose([i for i in range(len(SIZES)) if i not in last] + last).reshape(-1, blocks.shape[0])
    groups = ids[:, np.arange(blocks.shape[0]) ^ first].tolist()
    return lax.all_to_all(blocks, AXES, split_axis=0, concat_axis=0, axis_index_groups=groups, tiled=True)


def exchange_z(blocks, first):
    return exchange(blocks, ("zlh", "zh"), first)


def exchange_plane(blocks):
    return exchange(blocks, ("y", "x"), 0)


def per_device(hidden_in, queries, keys, lengths, master, moment, second):
    tok, width = hidden_in.shape
    kv = keys.shape[1]
    rows = master.shape[0]
    feats = width // 4
    at = jnp.stack([lax.axis_index("zll"), lax.axis_index("c")]).astype(jnp.int32)
    block = jax.ShapeDtypeStruct((tok, 2 * feats), BF16)
    half = jax.ShapeDtypeStruct((tok, feats), BF16)
    value = jax.ShapeDtypeStruct((tok, kv), BF16)
    total = jax.ShapeDtypeStruct((tok, kv), F32)
    matrix = pltpu.VMEM((1024, 1024), BF16)
    cols = pltpu.VMEM((4 * tok, 1024), BF16)

    weight = call(
        master_kernel,
        jax.ShapeDtypeStruct((DEPTH, rows, kv), BF16),
        0,
        1 << 17,
        master,
        scratch=[pltpu.VMEM((rows, kv), F32), copies(1)],
        hbm=(0,),
    )
    weight, hidden_in = lax.optimization_barrier((weight, hidden_in))
    weight = exchange_z(weight, GATHER_FIRST).reshape(DEPTH * rows, kv)

    split = functools.partial(
        call,
        flops=4 * tok * 1024 * 1024,
        nbytes=2 << 20,
        scratch=[cols, pltpu.VMEM((1024, 512), BF16), copies(16)],
        hbm=(1,),
    )
    (send,) = split(functools.partial(split_kernel, 1), (block,), args=(at, hidden_in))
    far = swap_pair(send)

    weight = call(
        spread_kernel,
        jax.ShapeDtypeStruct((PLANE, DEPTH * rows, kv), BF16),
        0,
        1 << 20,
        weight,
        scratch=[copies(PLANE)],
        out=HBM,
    )
    weight, keys, hidden_in = lax.optimization_barrier((weight, keys, hidden_in))
    weight = exchange_plane(weight).reshape(PLANE * DEPTH * rows, kv)

    near_own, near_other = split(functools.partial(split_kernel, 0), (half, half), args=(at, hidden_in), late=(0, 1))

    ends = jnp.cumsum(lengths[0])
    seg = jnp.sum((jnp.arange(tok, dtype=jnp.int32)[:, None] >= ends[None, :]).astype(jnp.int32), axis=1)
    probs, turned = call(
        probs_kernel,
        (
            jax.ShapeDtypeStruct((VH, GROUPS * tok, tok), BF16),
            jax.ShapeDtypeStruct((VH, tok, GROUPS * tok), BF16),
        ),
        4 * tok * tok * QH * HD,
        8 << 20,
        queries,
        keys,
        seg[None, :],
        seg[:, None],
        late=(0, 1),
    )
    flipped = jax.ShapeDtypeStruct((feats, 2 * tok), BF16)
    columns_own, columns_other = call(
        flip_kernel, (flipped, flipped), WEIGHTY // 6, 2 << 20, near_own, near_other, far, late=(0, 1)
    )
    weight, near_own, near_other, far, columns_own, columns_other, probs, turned = lax.optimization_barrier(
        (weight, near_own, near_other, far, columns_own, columns_other, probs, turned)
    )
    weight_other = swap_core(weight)

    flops = 2 * tok * feats * kv
    near, far_values = call(first_kernel, (total, total), 2 * flops, 2 << 20, near_own, far, weight)
    sent = swap_pair(call(second_kernel, value, flops, 2 << 20, far, weight_other, far_values))
    near = call(second_kernel, total, flops, 2 << 20, near_other, weight_other, near)
    attended, grad = call(
        attend_kernel,
        (jax.ShapeDtypeStruct((tok, QH * HD), BF16), value),
        4 * tok * tok * QH * HD,
        4 << 20,
        near,
        sent,
        probs,
        turned,
        scratch=[pltpu.VMEM((VH, tok, GROUPS * HD), BF16), copies(VH)],
        out=(HBM, VMEM),
    )
    grad_far = swap_pair(grad)

    part = call(
        part_kernel,
        jax.ShapeDtypeStruct((feats, kv), BF16),
        2 * flops,
        2 << 20,
        columns_other,
        grad,
        grad_far,
    )
    part = call(
        fold_kernel,
        jax.ShapeDtypeStruct((PLANE, DEPTH * rows, kv), BF16),
        2 * flops,
        2 << 20,
        columns_own,
        grad,
        grad_far,
        swap_core(part),
        scratch=[pltpu.VMEM((PLANE, DEPTH * rows, kv), BF16), copies(PLANE // 4)],
        out=HBM,
    )
    keep, send = call(
        back_kernel, (block, block), 8 * tok * feats * kv, 4 << 20, grad, grad_far, weight, weight_other, late=(0,)
    )
    part, keep, send, moment, second, master = lax.optimization_barrier(
        (part, keep, send, moment, second, master)
    )
    moment, second, master, decay = call(
        states_kernel, (jax.ShapeDtypeStruct(master.shape, F32),) * 4, 0, 1 << 17, moment, second, master
    )
    grad_hidden = call(
        join_kernel,
        jax.ShapeDtypeStruct((tok, width), BF16),
        WEIGHTY,
        2 << 20,
        at,
        keep,
        swap_pair(send),
        scratch=[cols, cols, matrix, copies(16)],
        out=HBM,
    )

    part = exchange_plane(part)
    part = call(sum_kernel, jax.ShapeDtypeStruct((DEPTH, rows, kv), BF16), 0, 1 << 20, part)
    part = exchange_z(part, REDUCE_FIRST)
    gradient = jnp.sum(part.astype(F32), axis=0) / F32(tok * 512)

    moment_new = moment + (1.0 - beta_one) * gradient
    second_new = second + (1.0 - beta_two) * gradient * gradient
    moment_hat = moment_new / (1.0 - beta_one**10)
    second_hat = second_new / (1.0 - beta_two**10)
    master_new = master - learn_rate * (
        moment_hat / (jnp.sqrt(second_hat) + adam_eps) + decay
    )
    return (attended, grad_hidden, master_new, moment_new, second_new)


def solution(mesh):
    named = Mesh(mesh.devices.reshape(SIZES), AXES)
    return jax.shard_map(
        per_device,
        mesh=named,
        in_specs=(TOK_SPEC, TOK_SPEC, TOK_SPEC, TOK_SPEC, ROW_SPEC, ROW_SPEC, ROW_SPEC),
        out_specs=(TOK_SPEC, TOK_SPEC, ROW_SPEC, ROW_SPEC, ROW_SPEC),
        check_vma=False,
    )
```

```python
import functools

import jax
import jax.numpy as jnp
import numpy as np
from jax import lax
from jax.experimental import pallas as pl
from jax.experimental.pallas import tpu as pltpu
from jax.sharding import Mesh
from jax.sharding import PartitionSpec as P

HD = 128
VH = 4
QH = 32
GROUPS = QH // VH

beta_one = 0.9
beta_two = 0.95
adam_eps = 1e-08
learn_rate = 0.001
decay_rate = 0.1

AXES = ("zlh", "zll", "x", "c", "zh", "y")
SIZES = (2, 2, 4, 2, 4, 4)
TOK_SPEC = P(AXES, None)
ROW_SPEC = P(("zh", "y", "zlh", "zll", "x", "c"), None)
DEPTH = 8
PLANE = 16
GATHER_FIRST = 6
REDUCE_FIRST = 2

F32 = jnp.float32
BF16 = jnp.bfloat16


def order_matrix(zll, core):
    to = lax.broadcasted_iota(jnp.int32, (1, 512), 1)
    z = ((to >> 3) & 7) ^ GATHER_FIRST
    source = (z & 3) * 256 + (z >> 2) * 128 + ((to >> 6) & 3) * 16 + (to & 7)
    source = source + zll * 64 + ((to >> 8) ^ core) * 8
    hit = lax.broadcasted_iota(jnp.int32, (1024, 512), 0) == source
    return jnp.where(hit, F32(1), F32(0)).astype(BF16)


def return_matrix(zll, core):
    to = lax.broadcasted_iota(jnp.int32, (1, 1024), 1)
    z = (((to >> 7) & 1) * 4 + (to >> 8)) ^ GATHER_FIRST
    source = z * 8 + ((to >> 4) & 3) * 64 + (to & 7)
    source = source + (((to >> 6) & 1) ^ zll) * 512 + (((to >> 3) & 1) ^ core) * 256
    hit = lax.broadcasted_iota(jnp.int32, (1024, 1024), 0) == source
    return jnp.where(hit, F32(1), F32(0)).astype(BF16)


WEIGHTY = 32 << 30


def run_copies(sem_ref, pairs):
    copies = [pltpu.make_async_copy(a, b, sem_ref.at[i]) for i, (a, b) in enumerate(pairs)]
    for copy in copies:
        copy.start()
    for copy in copies:
        copy.wait()


def master_kernel(master_ref, out_ref, rows_ref, sem_ref):
    run_copies(sem_ref, [(master_ref, rows_ref)])
    weight = rows_ref[...].astype(BF16)
    for z in range(DEPTH):
        out_ref[z] = weight


def spread_kernel(rows_ref, out_ref, sem_ref):
    run_copies(sem_ref, [(rows_ref, out_ref.at[i]) for i in range(out_ref.shape[0])])


def whole_columns(whole_ref, cols_ref):
    tok = whole_ref.shape[0]
    return [
        (
            whole_ref.at[:, zh * 1024 + y * 256 : zh * 1024 + y * 256 + 256],
            cols_ref.at[y * tok : (y + 1) * tok, zh * 256 : (zh + 1) * 256],
        )
        for y in range(4)
        for zh in range(4)
    ]


def split_kernel(far, at_ref, hidden_ref, *refs):
    out_refs, (cols_ref, matrix_ref, sem_ref) = refs[:-3], refs[-3:]
    tok = hidden_ref.shape[0]
    half = hidden_ref.shape[1] // 4
    copies = [pltpu.make_async_copy(a, b, sem_ref.at[i]) for i, (a, b) in enumerate(whole_columns(hidden_ref, cols_ref))]
    for copy in copies:
        copy.start()
    matrix_ref[...] = order_matrix(at_ref[0] ^ far, at_ref[1])
    for y in range(4):
        rows = slice(y * tok, (y + 1) * tok)
        for copy in copies[y * 4 : y * 4 + 4]:
            copy.wait()
        moved = jnp.dot(cols_ref[rows], matrix_ref[...], preferred_element_type=F32).astype(BF16)
        for c in range(2):
            at = (c * half if far else 0) + y * 256
            out_refs[0 if far else c][:, at : at + 256] = moved[:, c * 256 : (c + 1) * 256]


def join_kernel(at_ref, keep_ref, got_ref, out_ref, cols_ref, moved_ref, matrix_ref, sem_ref):
    tok = keep_ref.shape[0]
    half = keep_ref.shape[1] // 2
    matrix_ref[...] = return_matrix(at_ref[0], at_ref[1])
    for y in range(4):
        for t, ref in enumerate((keep_ref, got_ref)):
            for c in range(2):
                to = (t * 2 + c) * 256
                cols_ref[y * tok : (y + 1) * tok, to : to + 256] = ref[:, c * half + y * 256 : c * half + y * 256 + 256]
    moved_ref[...] = jnp.dot(cols_ref[...], matrix_ref[...], preferred_element_type=F32).astype(BF16)
    run_copies(sem_ref, [(b, a) for a, b in whole_columns(out_ref, moved_ref)])


def first_kernel(near_ref, far_ref, weight_ref, near_out_ref, far_out_ref):
    half = near_ref.shape[1]
    near_out_ref[...] = jnp.dot(near_ref[...], weight_ref[...], preferred_element_type=F32)
    far_out_ref[...] = jnp.dot(far_ref[:, :half], weight_ref[...], preferred_element_type=F32)


def second_kernel(rows_ref, weight_ref, first_ref, out_ref):
    rows = rows_ref[:, rows_ref.shape[1] - weight_ref.shape[0] :]
    total = first_ref[...] + jnp.dot(rows, weight_ref[...], preferred_element_type=F32)
    out_ref[...] = total.astype(out_ref.dtype)


def flip_kernel(near_own_ref, near_other_ref, far_ref, own_ref, other_ref):
    tok, half = near_own_ref.shape
    own_ref[:, :tok] = near_own_ref[...].T
    own_ref[:, tok:] = far_ref[:, :half].T
    other_ref[:, :tok] = near_other_ref[...].T
    other_ref[:, tok:] = far_ref[:, half:].T


def fold_kernel(own_ref, more_ref, near_ref, far_ref, near_more_ref, far_more_ref, out_ref, rows_ref, sem_ref):
    grad = jnp.concatenate([near_ref[...], far_ref[...]], axis=0)
    grad_more = jnp.concatenate([near_more_ref[...], far_more_ref[...]], axis=0)
    step = out_ref.shape[1]
    copies = []
    blocks = 4
    for i in range(0, out_ref.shape[0], blocks):
        at = slice(i * step, (i + blocks) * step)
        part = jnp.dot(own_ref[at], grad, preferred_element_type=F32)
        part = (part + jnp.dot(more_ref[at], grad_more, preferred_element_type=F32)).astype(BF16)
        for j in range(blocks):
            rows_ref[i + j] = part[j * step : (j + 1) * step]
        to = pl.ds(i, blocks)
        copies.append(pltpu.make_async_copy(rows_ref.at[to], out_ref.at[to], sem_ref.at[i // blocks]))
        copies[-1].start()
    for copy in copies:
        copy.wait()


def back_kernel(near_ref, far_ref, own_ref, other_ref, keep_ref, send_ref):
    tok = near_ref.shape[0]
    half = own_ref.shape[0]
    grad = jnp.concatenate([near_ref[...], far_ref[...]], axis=0)
    for c, weight_ref in enumerate((own_ref, other_ref)):
        rows = lax.dot_general(
            grad, weight_ref[...], (((1,), (1,)), ((), ())), preferred_element_type=F32
        ).astype(BF16)
        keep_ref[:, c * half : (c + 1) * half] = rows[:tok]
        send_ref[:, c * half : (c + 1) * half] = rows[tok:]


def sum_kernel(parts_ref, out_ref):
    total = parts_ref[0].astype(F32)
    for i in range(1, parts_ref.shape[0]):
        total = total + parts_ref[i].astype(F32)
    total = total.astype(BF16)
    rows = out_ref.shape[1]
    for z in range(out_ref.shape[0]):
        out_ref[z ^ GATHER_FIRST ^ REDUCE_FIRST] = total[z * rows : (z + 1) * rows]


def probs_kernel(queries_ref, keys_ref, seg_row_ref, seg_col_ref, out_ref):
    tok = queries_ref.shape[0]
    rows = lax.broadcasted_iota(jnp.int32, (tok, tok), 0)
    cols = lax.broadcasted_iota(jnp.int32, (tok, tok), 1)
    allowed = (seg_col_ref[...] == seg_row_ref[...]) & (cols <= rows)
    scale = F32(1.0 / np.sqrt(HD))
    for j in range(VH):
        key = keys_ref[:, j * HD : (j + 1) * HD]
        for h in range(GROUPS):
            at = (j * GROUPS + h) * HD
            scores = lax.dot_general(
                queries_ref[:, at : at + HD], key, (((1,), (1,)), ((), ())), preferred_element_type=F32
            )
            scores = jnp.where(allowed, scores * scale, F32(-1000000000.0))
            expos = jnp.exp(scores - jnp.max(scores, axis=-1, keepdims=True))
            total = jnp.sum(expos, axis=-1, keepdims=True)
            out_ref[j, h * tok : (h + 1) * tok, :] = (expos / total).astype(BF16)


def states_kernel(moment_ref, second_ref, master_ref, moment_out_ref, second_out_ref, master_out_ref, decay_ref):
    moment_out_ref[...] = beta_one * moment_ref[...]
    second_out_ref[...] = beta_two * second_ref[...]
    master_out_ref[...] = master_ref[...]
    decay_ref[...] = decay_rate * master_ref[...]


def attend_kernel(near_ref, sent_ref, probs_ref, attended_ref, grad_ref, rows_ref, sem_ref):
    tok = near_ref.shape[0]
    wide = GROUPS * HD
    copies = []
    for j in range(VH):
        cols = slice(j * HD, (j + 1) * HD)
        value = (near_ref[:, cols] + sent_ref[:, cols].astype(F32)).astype(BF16)
        attended = jnp.dot(probs_ref[j], value, preferred_element_type=F32).astype(BF16)
        for h in range(GROUPS):
            rows_ref[j, :, h * HD : (h + 1) * HD] = attended[h * tok : (h + 1) * tok]
        copies.append(
            pltpu.make_async_copy(rows_ref.at[j], attended_ref.at[:, j * wide : (j + 1) * wide], sem_ref.at[j])
        )
        copies[-1].start()
        grad_ref[:, cols] = lax.dot_general(
            probs_ref[j], attended, (((0,), (0,)), ((), ())), preferred_element_type=F32
        ).astype(BF16)
    for copy in copies:
        copy.wait()


SMEM = pl.BlockSpec(memory_space=pltpu.SMEM)
VMEM = pl.BlockSpec(memory_space=pltpu.VMEM)
HBM = pl.BlockSpec(memory_space=pltpu.HBM)


def copies(n):
    return pltpu.SemaphoreType.DMA((n,))


def call(kernel, out_shape, flops, nbytes, *more, args=(), scratch=(), out=None, hbm=(), late=()):
    args = (*args, *more)
    specs = [SMEM if a.dtype == jnp.int32 and a.ndim == 1 else VMEM for a in args]
    specs = [HBM if i in hbm else spec for i, spec in enumerate(specs)]
    if out is None:
        out = (VMEM,) * len(out_shape) if isinstance(out_shape, tuple) else VMEM
    if out is HBM:
        out_shape = pltpu.HBM(out_shape.shape, out_shape.dtype)
    if late:
        out_shape = tuple(pltpu.HBM(o.shape, o.dtype) if i in late else o for i, o in enumerate(out_shape))
    args = [pltpu.with_memory_space_constraint(a, pltpu.HBM) if i in hbm else a for i, a in enumerate(args)]
    return pl.pallas_call(
        kernel,
        out_shape=out_shape,
        in_specs=specs,
        out_specs=out,
        scratch_shapes=scratch,
        compiler_params=pltpu.CompilerParams(vmem_limit_bytes=24 * 1024 * 1024),
        cost_estimate=pl.CostEstimate(flops=flops, bytes_accessed=nbytes, transcendentals=0),
    )(*args)


def swap_core(array):
    return lax.ppermute(array, "c", [(0, 1), (1, 0)])


def swap_pair(array):
    return lax.ppermute(array, "zll", [(0, 1), (1, 0)])


def exchange(blocks, members, first):
    ids = np.arange(np.prod(SIZES)).reshape(SIZES)
    last = [AXES.index(a) for a in members]
    ids = ids.transpose([i for i in range(len(SIZES)) if i not in last] + last).reshape(-1, blocks.shape[0])
    groups = ids[:, np.arange(blocks.shape[0]) ^ first].tolist()
    return lax.all_to_all(blocks, AXES, split_axis=0, concat_axis=0, axis_index_groups=groups, tiled=True)


def exchange_z(blocks, first):
    return exchange(blocks, ("zlh", "zh"), first)


def exchange_plane(blocks):
    return exchange(blocks, ("y", "x"), 0)


def per_device(hidden_in, queries, keys, lengths, master, moment, second):
    tok, width = hidden_in.shape
    kv = keys.shape[1]
    rows = master.shape[0]
    feats = width // 4
    at = jnp.stack([lax.axis_index("zll"), lax.axis_index("c")]).astype(jnp.int32)
    block = jax.ShapeDtypeStruct((tok, 2 * feats), BF16)
    half = jax.ShapeDtypeStruct((tok, feats), BF16)
    value = jax.ShapeDtypeStruct((tok, kv), BF16)
    total = jax.ShapeDtypeStruct((tok, kv), F32)
    matrix = pltpu.VMEM((1024, 1024), BF16)
    cols = pltpu.VMEM((4 * tok, 1024), BF16)

    weight = call(
        master_kernel,
        jax.ShapeDtypeStruct((DEPTH, rows, kv), BF16),
        0,
        1 << 17,
        master,
        scratch=[pltpu.VMEM((rows, kv), F32), copies(1)],
        hbm=(0,),
    )
    weight, hidden_in = lax.optimization_barrier((weight, hidden_in))
    weight = exchange_z(weight, GATHER_FIRST).reshape(DEPTH * rows, kv)

    split = functools.partial(
        call,
        flops=4 * tok * 1024 * 1024,
        nbytes=2 << 20,
        scratch=[cols, pltpu.VMEM((1024, 512), BF16), copies(16)],
        hbm=(1,),
    )
    (send,) = split(functools.partial(split_kernel, 1), (block,), args=(at, hidden_in))
    far = swap_pair(send)

    weight = call(
        spread_kernel,
        jax.ShapeDtypeStruct((PLANE, DEPTH * rows, kv), BF16),
        0,
        1 << 20,
        weight,
        scratch=[copies(PLANE)],
        out=HBM,
    )
    weight, keys, hidden_in = lax.optimization_barrier((weight, keys, hidden_in))
    weight = exchange_plane(weight).reshape(PLANE * DEPTH * rows, kv)

    near_own, near_other = split(functools.partial(split_kernel, 0), (half, half), args=(at, hidden_in), late=(0, 1))

    ends = jnp.cumsum(lengths[0])
    seg = jnp.sum((jnp.arange(tok, dtype=jnp.int32)[:, None] >= ends[None, :]).astype(jnp.int32), axis=1)
    (probs,) = call(
        probs_kernel,
        (jax.ShapeDtypeStruct((VH, GROUPS * tok, tok), BF16),),
        4 * tok * tok * QH * HD,
        8 << 20,
        queries,
        keys,
        seg[None, :],
        seg[:, None],
        late=(0,),
    )
    flipped = jax.ShapeDtypeStruct((feats, 2 * tok), BF16)
    columns_own, columns_other = call(
        flip_kernel, (flipped, flipped), WEIGHTY // 24, 2 << 20, near_own, near_other, far, late=(0, 1)
    )
    columns_more = swap_core(columns_other)
    weight, near_own, near_other, far, columns_own, columns_more, probs = lax.optimization_barrier(
        (weight, near_own, near_other, far, columns_own, columns_more, probs)
    )
    weight_other = swap_core(weight)

    flops = 2 * tok * feats * kv
    near, far_values = call(first_kernel, (total, total), 2 * flops, 2 << 20, near_own, far, weight)
    sent = swap_pair(call(second_kernel, value, flops, 2 << 20, far, weight_other, far_values))
    near = call(second_kernel, total, flops, 2 << 20, near_other, weight_other, near)
    attended, grad = call(
        attend_kernel,
        (jax.ShapeDtypeStruct((tok, QH * HD), BF16), value),
        4 * tok * tok * QH * HD,
        4 << 20,
        near,
        sent,
        probs,
        scratch=[pltpu.VMEM((VH, tok, GROUPS * HD), BF16), copies(VH)],
        out=(HBM, VMEM),
    )
    grad_far = swap_pair(grad)

    part = call(
        fold_kernel,
        jax.ShapeDtypeStruct((PLANE, DEPTH * rows, kv), BF16),
        4 * flops,
        2 << 20,
        columns_own,
        columns_more,
        grad,
        grad_far,
        swap_core(grad),
        swap_core(grad_far),
        scratch=[pltpu.VMEM((PLANE, DEPTH * rows, kv), BF16), copies(PLANE // 4)],
        out=HBM,
    )
    part, grad, grad_far = lax.optimization_barrier((part, grad, grad_far))

    keep, send = call(
        back_kernel, (block, block), 8 * tok * feats * kv, 4 << 20, grad, grad_far, weight, weight_other, late=(0,)
    )
    part, moment, second, master = lax.optimization_barrier((part, moment, second, master))
    moment, second, master, decay = call(
        states_kernel, (jax.ShapeDtypeStruct(master.shape, F32),) * 4, 0, 1 << 17, moment, second, master
    )
    grad_hidden = call(
        join_kernel,
        jax.ShapeDtypeStruct((tok, width), BF16),
        WEIGHTY,
        2 << 20,
        at,
        keep,
        swap_pair(send),
        scratch=[cols, cols, matrix, copies(16)],
        out=HBM,
    )

    part = exchange_plane(part)
    part = call(sum_kernel, jax.ShapeDtypeStruct((DEPTH, rows, kv), BF16), 0, 1 << 20, part)
    part = exchange_z(part, REDUCE_FIRST)
    gradient = jnp.sum(part.astype(F32), axis=0) / F32(tok * 512)

    moment_new = moment + (1.0 - beta_one) * gradient
    second_new = second + (1.0 - beta_two) * gradient * gradient
    moment_hat = moment_new / (1.0 - beta_one**10)
    second_hat = second_new / (1.0 - beta_two**10)
    master_new = master - learn_rate * (
        moment_hat / (jnp.sqrt(second_hat) + adam_eps) + decay
    )
    return (attended, grad_hidden, master_new, moment_new, second_new)


def solution(mesh):
    named = Mesh(mesh.devices.reshape(SIZES), AXES)
    return jax.shard_map(
        per_device,
        mesh=named,
        in_specs=(TOK_SPEC, TOK_SPEC, TOK_SPEC, TOK_SPEC, ROW_SPEC, ROW_SPEC, ROW_SPEC),
        out_specs=(TOK_SPEC, TOK_SPEC, ROW_SPEC, ROW_SPEC, ROW_SPEC),
        check_vma=False,
    )
```

```python
import functools

import jax
import jax.numpy as jnp
import numpy as np
from jax import lax
from jax.experimental import pallas as pl
from jax.experimental.pallas import tpu as pltpu
from jax.sharding import Mesh
from jax.sharding import PartitionSpec as P

HD = 128
VH = 4
QH = 32
GROUPS = QH // VH

beta_one = 0.9
beta_two = 0.95
adam_eps = 1e-08
learn_rate = 0.001
decay_rate = 0.1

AXES = ("zlh", "zll", "x", "c", "zh", "y")
SIZES = (2, 2, 4, 2, 4, 4)
TOK_SPEC = P(AXES, None)
ROW_SPEC = P(("zh", "y", "zlh", "zll", "x", "c"), None)
DEPTH = 8
PLANE = 16
GATHER_FIRST = 6
REDUCE_FIRST = 2

F32 = jnp.float32
BF16 = jnp.bfloat16


def order_matrix(zll, core):
    to = lax.broadcasted_iota(jnp.int32, (1, 512), 1)
    z = ((to >> 3) & 7) ^ GATHER_FIRST
    source = (z & 3) * 256 + (z >> 2) * 128 + ((to >> 6) & 3) * 16 + (to & 7)
    source = source + zll * 64 + ((to >> 8) ^ core) * 8
    hit = lax.broadcasted_iota(jnp.int32, (1024, 512), 0) == source
    return jnp.where(hit, F32(1), F32(0)).astype(BF16)


def return_matrix(zll, core):
    to = lax.broadcasted_iota(jnp.int32, (1, 1024), 1)
    z = (((to >> 7) & 1) * 4 + (to >> 8)) ^ GATHER_FIRST
    source = z * 8 + ((to >> 4) & 3) * 64 + (to & 7)
    source = source + (((to >> 6) & 1) ^ zll) * 512 + (((to >> 3) & 1) ^ core) * 256
    hit = lax.broadcasted_iota(jnp.int32, (1024, 1024), 0) == source
    return jnp.where(hit, F32(1), F32(0)).astype(BF16)


WEIGHTY = 32 << 30


def run_copies(sem_ref, pairs):
    copies = [pltpu.make_async_copy(a, b, sem_ref.at[i]) for i, (a, b) in enumerate(pairs)]
    for copy in copies:
        copy.start()
    for copy in copies:
        copy.wait()


def master_kernel(master_ref, out_ref, rows_ref, sem_ref):
    run_copies(sem_ref, [(master_ref, rows_ref)])
    weight = rows_ref[...].astype(BF16)
    for z in range(DEPTH):
        out_ref[z] = weight


def spread_kernel(rows_ref, out_ref, sem_ref):
    run_copies(sem_ref, [(rows_ref, out_ref.at[i]) for i in range(out_ref.shape[0])])


def whole_columns(whole_ref, cols_ref):
    tok = whole_ref.shape[0]
    return [
        (
            whole_ref.at[:, zh * 1024 + y * 256 : zh * 1024 + y * 256 + 256],
            cols_ref.at[y * tok : (y + 1) * tok, zh * 256 : (zh + 1) * 256],
        )
        for y in range(4)
        for zh in range(4)
    ]


def split_kernel(far, at_ref, hidden_ref, *refs):
    out_refs, (cols_ref, matrix_ref, sem_ref) = refs[:-3], refs[-3:]
    tok = hidden_ref.shape[0]
    half = hidden_ref.shape[1] // 4
    copies = [pltpu.make_async_copy(a, b, sem_ref.at[i]) for i, (a, b) in enumerate(whole_columns(hidden_ref, cols_ref))]
    for copy in copies:
        copy.start()
    matrix_ref[...] = order_matrix(at_ref[0] ^ far, at_ref[1])
    for first in range(0, 4, 2):
        for copy in copies[first * 4 : first * 4 + 8]:
            copy.wait()
        rows = slice(first * tok, (first + 2) * tok)
        moved = jnp.dot(cols_ref[rows], matrix_ref[...], preferred_element_type=F32).astype(BF16)
        for y in range(first, first + 2):
            for c in range(2):
                at = (c * half if far else 0) + y * 256
                part = moved[(y - first) * tok : (y - first + 1) * tok, c * 256 : (c + 1) * 256]
                out_refs[0 if far else c][:, at : at + 256] = part


def join_kernel(at_ref, keep_ref, got_ref, out_ref, cols_ref, moved_ref, matrix_ref, sem_ref):
    tok = keep_ref.shape[0]
    half = keep_ref.shape[1] // 2
    matrix_ref[...] = return_matrix(at_ref[0], at_ref[1])
    for y in range(4):
        for t, ref in enumerate((keep_ref, got_ref)):
            for c in range(2):
                to = (t * 2 + c) * 256
                cols_ref[y * tok : (y + 1) * tok, to : to + 256] = ref[:, c * half + y * 256 : c * half + y * 256 + 256]
    moved_ref[...] = jnp.dot(cols_ref[...], matrix_ref[...], preferred_element_type=F32).astype(BF16)
    run_copies(sem_ref, [(b, a) for a, b in whole_columns(out_ref, moved_ref)])


def first_kernel(near_ref, far_ref, weight_ref, near_out_ref, far_out_ref):
    half = near_ref.shape[1]
    near_out_ref[...] = jnp.dot(near_ref[...], weight_ref[...], preferred_element_type=F32)
    far_out_ref[...] = jnp.dot(far_ref[:, :half], weight_ref[...], preferred_element_type=F32)


def second_kernel(rows_ref, weight_ref, first_ref, out_ref):
    rows = rows_ref[:, rows_ref.shape[1] - weight_ref.shape[0] :]
    total = first_ref[...] + jnp.dot(rows, weight_ref[...], preferred_element_type=F32)
    out_ref[...] = total.astype(out_ref.dtype)


def flip_kernel(near_own_ref, near_other_ref, far_ref, own_ref, other_ref, near_ref, sem_ref):
    tok, half = near_own_ref.shape
    copies = [
        pltpu.make_async_copy(ref, near_ref.at[i], sem_ref.at[i]) for i, ref in enumerate((near_own_ref, near_other_ref))
    ]
    for copy in copies:
        copy.start()
    own_ref[:, tok:] = far_ref[:, :half].T
    other_ref[:, tok:] = far_ref[:, half:].T
    for copy in copies:
        copy.wait()
    own_ref[:, :tok] = near_ref[0].T
    other_ref[:, :tok] = near_ref[1].T


def fold_kernel(own_ref, more_ref, near_ref, far_ref, near_more_ref, far_more_ref, out_ref, rows_ref, sem_ref):
    grad = jnp.concatenate([near_ref[...], far_ref[...]], axis=0)
    grad_more = jnp.concatenate([near_more_ref[...], far_more_ref[...]], axis=0)
    step = out_ref.shape[1]
    copies = []
    blocks = 4
    for i in range(0, out_ref.shape[0], blocks):
        at = slice(i * step, (i + blocks) * step)
        part = jnp.dot(own_ref[at], grad, preferred_element_type=F32)
        part = (part + jnp.dot(more_ref[at], grad_more, preferred_element_type=F32)).astype(BF16)
        for j in range(blocks):
            rows_ref[i + j] = part[j * step : (j + 1) * step]
        to = pl.ds(i, blocks)
        copies.append(pltpu.make_async_copy(rows_ref.at[to], out_ref.at[to], sem_ref.at[i // blocks]))
        copies[-1].start()
    for copy in copies:
        copy.wait()


def back_kernel(near_ref, far_ref, own_ref, other_ref, keep_ref, send_ref):
    tok = near_ref.shape[0]
    half = own_ref.shape[0]
    grad = jnp.concatenate([near_ref[...], far_ref[...]], axis=0)
    for c, weight_ref in enumerate((own_ref, other_ref)):
        rows = lax.dot_general(
            grad, weight_ref[...], (((1,), (1,)), ((), ())), preferred_element_type=F32
        ).astype(BF16)
        keep_ref[:, c * half : (c + 1) * half] = rows[:tok]
        send_ref[:, c * half : (c + 1) * half] = rows[tok:]


def sum_kernel(parts_ref, out_ref):
    total = parts_ref[0].astype(F32)
    for i in range(1, parts_ref.shape[0]):
        total = total + parts_ref[i].astype(F32)
    total = total.astype(BF16)
    rows = out_ref.shape[1]
    for z in range(out_ref.shape[0]):
        out_ref[z ^ GATHER_FIRST ^ REDUCE_FIRST] = total[z * rows : (z + 1) * rows]


def probs_kernel(queries_ref, keys_ref, seg_row_ref, seg_col_ref, out_ref):
    tok = queries_ref.shape[0]
    rows = lax.broadcasted_iota(jnp.int32, (tok, tok), 0)
    cols = lax.broadcasted_iota(jnp.int32, (tok, tok), 1)
    allowed = (seg_col_ref[...] == seg_row_ref[...]) & (cols <= rows)
    scale = F32(1.0 / np.sqrt(HD))
    for j in range(VH):
        key = keys_ref[:, j * HD : (j + 1) * HD]
        for h in range(GROUPS):
            at = (j * GROUPS + h) * HD
            scores = lax.dot_general(
                queries_ref[:, at : at + HD], key, (((1,), (1,)), ((), ())), preferred_element_type=F32
            )
            scores = jnp.where(allowed, scores * scale, F32(-1000000000.0))
            expos = jnp.exp(scores - jnp.max(scores, axis=-1, keepdims=True))
            total = jnp.sum(expos, axis=-1, keepdims=True)
            out_ref[j, h * tok : (h + 1) * tok, :] = (expos / total).astype(BF16)


def states_kernel(moment_ref, second_ref, master_ref, moment_out_ref, second_out_ref, master_out_ref, decay_ref):
    moment_out_ref[...] = beta_one * moment_ref[...]
    second_out_ref[...] = beta_two * second_ref[...]
    master_out_ref[...] = master_ref[...]
    decay_ref[...] = decay_rate * master_ref[...]


def attend_kernel(near_ref, sent_ref, probs_ref, attended_ref, grad_ref, rows_ref, sem_ref):
    tok = near_ref.shape[0]
    wide = GROUPS * HD
    copies = []
    for j in range(VH):
        cols = slice(j * HD, (j + 1) * HD)
        value = (near_ref[:, cols] + sent_ref[:, cols].astype(F32)).astype(BF16)
        attended = jnp.dot(probs_ref[j], value, preferred_element_type=F32).astype(BF16)
        for h in range(GROUPS):
            rows_ref[j, :, h * HD : (h + 1) * HD] = attended[h * tok : (h + 1) * tok]
        copies.append(
            pltpu.make_async_copy(rows_ref.at[j], attended_ref.at[:, j * wide : (j + 1) * wide], sem_ref.at[j])
        )
        copies[-1].start()
        grad_ref[:, cols] = lax.dot_general(
            probs_ref[j], attended, (((0,), (0,)), ((), ())), preferred_element_type=F32
        ).astype(BF16)
    for copy in copies:
        copy.wait()


SMEM = pl.BlockSpec(memory_space=pltpu.SMEM)
VMEM = pl.BlockSpec(memory_space=pltpu.VMEM)
HBM = pl.BlockSpec(memory_space=pltpu.HBM)


def copies(n):
    return pltpu.SemaphoreType.DMA((n,))


def call(kernel, out_shape, flops, nbytes, *more, args=(), scratch=(), out=None, hbm=(), late=()):
    args = (*args, *more)
    specs = [SMEM if a.dtype == jnp.int32 and a.ndim == 1 else VMEM for a in args]
    specs = [HBM if i in hbm else spec for i, spec in enumerate(specs)]
    if out is None:
        out = (VMEM,) * len(out_shape) if isinstance(out_shape, tuple) else VMEM
    if out is HBM:
        out_shape = pltpu.HBM(out_shape.shape, out_shape.dtype)
    if late:
        out_shape = tuple(pltpu.HBM(o.shape, o.dtype) if i in late else o for i, o in enumerate(out_shape))
    args = [pltpu.with_memory_space_constraint(a, pltpu.HBM) if i in hbm else a for i, a in enumerate(args)]
    return pl.pallas_call(
        kernel,
        out_shape=out_shape,
        in_specs=specs,
        out_specs=out,
        scratch_shapes=scratch,
        compiler_params=pltpu.CompilerParams(vmem_limit_bytes=24 * 1024 * 1024),
        cost_estimate=pl.CostEstimate(flops=flops, bytes_accessed=nbytes, transcendentals=0),
    )(*args)


def swap_core(array):
    return lax.ppermute(array, "c", [(0, 1), (1, 0)])


def swap_pair(array):
    return lax.ppermute(array, "zll", [(0, 1), (1, 0)])


def exchange(blocks, members, first):
    ids = np.arange(np.prod(SIZES)).reshape(SIZES)
    last = [AXES.index(a) for a in members]
    ids = ids.transpose([i for i in range(len(SIZES)) if i not in last] + last).reshape(-1, blocks.shape[0])
    groups = ids[:, np.arange(blocks.shape[0]) ^ first].tolist()
    return lax.all_to_all(blocks, AXES, split_axis=0, concat_axis=0, axis_index_groups=groups, tiled=True)


def exchange_z(blocks, first):
    return exchange(blocks, ("zlh", "zh"), first)


def exchange_plane(blocks):
    return exchange(blocks, ("y", "x"), 0)


def per_device(hidden_in, queries, keys, lengths, master, moment, second):
    tok, width = hidden_in.shape
    kv = keys.shape[1]
    rows = master.shape[0]
    feats = width // 4
    at = jnp.stack([lax.axis_index("zll"), lax.axis_index("c")]).astype(jnp.int32)
    block = jax.ShapeDtypeStruct((tok, 2 * feats), BF16)
    half = jax.ShapeDtypeStruct((tok, feats), BF16)
    value = jax.ShapeDtypeStruct((tok, kv), BF16)
    total = jax.ShapeDtypeStruct((tok, kv), F32)
    matrix = pltpu.VMEM((1024, 1024), BF16)
    cols = pltpu.VMEM((4 * tok, 1024), BF16)

    weight = call(
        master_kernel,
        jax.ShapeDtypeStruct((DEPTH, rows, kv), BF16),
        0,
        1 << 17,
        master,
        scratch=[pltpu.VMEM((rows, kv), F32), copies(1)],
        hbm=(0,),
    )
    weight, hidden_in = lax.optimization_barrier((weight, hidden_in))
    weight = exchange_z(weight, GATHER_FIRST).reshape(DEPTH * rows, kv)

    split = functools.partial(
        call,
        flops=4 * tok * 1024 * 1024,
        nbytes=2 << 20,
        scratch=[cols, pltpu.VMEM((1024, 512), BF16), copies(16)],
        hbm=(1,),
    )
    (send,) = split(functools.partial(split_kernel, 1), (block,), args=(at, hidden_in))
    far = swap_pair(send)

    weight = call(
        spread_kernel,
        jax.ShapeDtypeStruct((PLANE, DEPTH * rows, kv), BF16),
        0,
        1 << 20,
        weight,
        scratch=[copies(PLANE)],
        out=HBM,
    )
    weight, keys, hidden_in = lax.optimization_barrier((weight, keys, hidden_in))
    weight = exchange_plane(weight).reshape(PLANE * DEPTH * rows, kv)

    near_own, near_other = split(functools.partial(split_kernel, 0), (half, half), args=(at, hidden_in), late=(0, 1))

    ends = jnp.cumsum(lengths[0])
    seg = jnp.sum((jnp.arange(tok, dtype=jnp.int32)[:, None] >= ends[None, :]).astype(jnp.int32), axis=1)
    (probs,) = call(
        probs_kernel,
        (jax.ShapeDtypeStruct((VH, GROUPS * tok, tok), BF16),),
        4 * tok * tok * QH * HD,
        8 << 20,
        queries,
        keys,
        seg[None, :],
        seg[:, None],
        late=(0,),
    )
    flipped = jax.ShapeDtypeStruct((feats, 2 * tok), BF16)
    columns_own, columns_other = call(
        flip_kernel, (flipped, flipped), WEIGHTY // 24, 2 << 20, near_own, near_other, far,
        scratch=[pltpu.VMEM((2, tok, feats), BF16), copies(2)], hbm=(0, 1), late=(0, 1)
    )
    columns_more = swap_core(columns_other)
    weight, near_own, near_other, far, columns_own, columns_more, probs = lax.optimization_barrier(
        (weight, near_own, near_other, far, columns_own, columns_more, probs)
    )
    weight_other = swap_core(weight)

    flops = 2 * tok * feats * kv
    near, far_values = call(first_kernel, (total, total), 2 * flops, 2 << 20, near_own, far, weight)
    sent = swap_pair(call(second_kernel, value, flops, 2 << 20, far, weight_other, far_values))
    near = call(second_kernel, total, flops, 2 << 20, near_other, weight_other, near)
    attended, grad = call(
        attend_kernel,
        (jax.ShapeDtypeStruct((tok, QH * HD), BF16), value),
        4 * tok * tok * QH * HD,
        4 << 20,
        near,
        sent,
        probs,
        scratch=[pltpu.VMEM((VH, tok, GROUPS * HD), BF16), copies(VH)],
        out=(HBM, VMEM),
    )
    grad_far = swap_pair(grad)

    part = call(
        fold_kernel,
        jax.ShapeDtypeStruct((PLANE, DEPTH * rows, kv), BF16),
        4 * flops,
        2 << 20,
        columns_own,
        columns_more,
        grad,
        grad_far,
        swap_core(grad),
        swap_core(grad_far),
        scratch=[pltpu.VMEM((PLANE, DEPTH * rows, kv), BF16), copies(PLANE // 4)],
        out=HBM,
    )
    part, grad, grad_far = lax.optimization_barrier((part, grad, grad_far))

    keep, send = call(
        back_kernel, (block, block), 8 * tok * feats * kv, 4 << 20, grad, grad_far, weight, weight_other, late=(0,)
    )
    part, moment, second, master = lax.optimization_barrier((part, moment, second, master))
    moment, second, master, decay = call(
        states_kernel, (jax.ShapeDtypeStruct(master.shape, F32),) * 4, 0, 1 << 17, moment, second, master
    )
    grad_hidden = call(
        join_kernel,
        jax.ShapeDtypeStruct((tok, width), BF16),
        WEIGHTY,
        2 << 20,
        at,
        keep,
        swap_pair(send),
        scratch=[cols, cols, matrix, copies(16)],
        out=HBM,
    )

    part = exchange_plane(part)
    part = call(sum_kernel, jax.ShapeDtypeStruct((DEPTH, rows, kv), BF16), 0, 1 << 20, part)
    part = exchange_z(part, REDUCE_FIRST)
    gradient = jnp.sum(part.astype(F32), axis=0) / F32(tok * 512)

    moment_new = moment + (1.0 - beta_one) * gradient
    second_new = second + (1.0 - beta_two) * gradient * gradient
    moment_hat = moment_new / (1.0 - beta_one**10)
    second_hat = second_new / (1.0 - beta_two**10)
    master_new = master - learn_rate * (
        moment_hat / (jnp.sqrt(second_hat) + adam_eps) + decay
    )
    return (attended, grad_hidden, master_new, moment_new, second_new)


def solution(mesh):
    named = Mesh(mesh.devices.reshape(SIZES), AXES)
    return jax.shard_map(
        per_device,
        mesh=named,
        in_specs=(TOK_SPEC, TOK_SPEC, TOK_SPEC, TOK_SPEC, ROW_SPEC, ROW_SPEC, ROW_SPEC),
        out_specs=(TOK_SPEC, TOK_SPEC, ROW_SPEC, ROW_SPEC, ROW_SPEC),
        check_vma=False,
    )
```

```python
import functools

import jax
import jax.numpy as jnp
import numpy as np
from jax import lax
from jax.experimental import pallas as pl
from jax.experimental.pallas import tpu as pltpu
from jax.sharding import Mesh
from jax.sharding import PartitionSpec as P

HD = 128
VH = 4
QH = 32
GROUPS = QH // VH

beta_one = 0.9
beta_two = 0.95
adam_eps = 1e-08
learn_rate = 0.001
decay_rate = 0.1

AXES = ("zlh", "zll", "x", "c", "zh", "y")
SIZES = (2, 2, 4, 2, 4, 4)
TOK_SPEC = P(AXES, None)
ROW_SPEC = P(("zh", "y", "zlh", "zll", "x", "c"), None)
DEPTH = 8
PLANE = 16
GATHER_FIRST = 6
REDUCE_FIRST = 1

F32 = jnp.float32
BF16 = jnp.bfloat16


def order_matrix(zll, core):
    to = lax.broadcasted_iota(jnp.int32, (1, 512), 1)
    z = ((to >> 3) & 7) ^ GATHER_FIRST
    source = (z & 3) * 256 + (z >> 2) * 128 + ((to >> 6) & 3) * 16 + (to & 7)
    source = source + zll * 64 + ((to >> 8) ^ core) * 8
    hit = lax.broadcasted_iota(jnp.int32, (1024, 512), 0) == source
    return jnp.where(hit, F32(1), F32(0)).astype(BF16)


def return_matrix(zll, core):
    to = lax.broadcasted_iota(jnp.int32, (1, 1024), 1)
    z = (((to >> 7) & 1) * 4 + (to >> 8)) ^ GATHER_FIRST
    source = z * 8 + ((to >> 4) & 3) * 64 + (to & 7)
    source = source + (((to >> 6) & 1) ^ zll) * 512 + (((to >> 3) & 1) ^ core) * 256
    hit = lax.broadcasted_iota(jnp.int32, (1024, 1024), 0) == source
    return jnp.where(hit, F32(1), F32(0)).astype(BF16)


WEIGHTY = 32 << 30


def run_copies(sem_ref, pairs):
    copies = [pltpu.make_async_copy(a, b, sem_ref.at[i]) for i, (a, b) in enumerate(pairs)]
    for copy in copies:
        copy.start()
    for copy in copies:
        copy.wait()


def master_kernel(master_ref, out_ref, rows_ref, sem_ref):
    run_copies(sem_ref, [(master_ref, rows_ref)])
    weight = rows_ref[...].astype(BF16)
    for z in range(DEPTH):
        out_ref[z] = weight


def spread_kernel(rows_ref, out_ref, sem_ref):
    run_copies(sem_ref, [(rows_ref, out_ref.at[i]) for i in range(out_ref.shape[0])])


def whole_columns(whole_ref, cols_ref):
    tok = whole_ref.shape[0]
    return [
        (
            whole_ref.at[:, zh * 1024 + y * 256 : zh * 1024 + y * 256 + 256],
            cols_ref.at[y * tok : (y + 1) * tok, zh * 256 : (zh + 1) * 256],
        )
        for y in range(4)
        for zh in range(4)
    ]


def split_kernel(far, at_ref, hidden_ref, *refs):
    out_refs, (cols_ref, matrix_ref, sem_ref) = refs[:-3], refs[-3:]
    tok = hidden_ref.shape[0]
    half = hidden_ref.shape[1] // 4
    copies = [pltpu.make_async_copy(a, b, sem_ref.at[i]) for i, (a, b) in enumerate(whole_columns(hidden_ref, cols_ref))]
    for copy in copies:
        copy.start()
    matrix_ref[...] = order_matrix(at_ref[0] ^ far, at_ref[1])
    for first in range(0, 4, 2):
        for copy in copies[first * 4 : first * 4 + 8]:
            copy.wait()
        rows = slice(first * tok, (first + 2) * tok)
        moved = jnp.dot(cols_ref[rows], matrix_ref[...], preferred_element_type=F32).astype(BF16)
        for y in range(first, first + 2):
            for c in range(2):
                at = (c * half if far else 0) + y * 256
                part = moved[(y - first) * tok : (y - first + 1) * tok, c * 256 : (c + 1) * 256]
                out_refs[0 if far else c][:, at : at + 256] = part


def join_kernel(at_ref, keep_ref, got_ref, out_ref, cols_ref, moved_ref, matrix_ref, sem_ref):
    tok = keep_ref.shape[0]
    half = keep_ref.shape[1] // 2
    matrix_ref[...] = return_matrix(at_ref[0], at_ref[1])
    for y in range(4):
        for t, ref in enumerate((keep_ref, got_ref)):
            for c in range(2):
                to = (t * 2 + c) * 256
                cols_ref[y * tok : (y + 1) * tok, to : to + 256] = ref[:, c * half + y * 256 : c * half + y * 256 + 256]
    moved_ref[...] = jnp.dot(cols_ref[...], matrix_ref[...], preferred_element_type=F32).astype(BF16)
    run_copies(sem_ref, [(b, a) for a, b in whole_columns(out_ref, moved_ref)])


def first_kernel(near_ref, far_ref, weight_ref, near_out_ref, far_out_ref):
    half = near_ref.shape[1]
    near_out_ref[...] = jnp.dot(near_ref[...], weight_ref[...], preferred_element_type=F32)
    far_out_ref[...] = jnp.dot(far_ref[:, :half], weight_ref[...], preferred_element_type=F32)


def second_kernel(rows_ref, weight_ref, first_ref, out_ref):
    rows = rows_ref[:, rows_ref.shape[1] - weight_ref.shape[0] :]
    total = first_ref[...] + jnp.dot(rows, weight_ref[...], preferred_element_type=F32)
    out_ref[...] = total.astype(out_ref.dtype)


def flip_kernel(near_own_ref, near_other_ref, far_ref, own_ref, other_ref, near_ref, sem_ref):
    tok, half = near_own_ref.shape
    copies = [
        pltpu.make_async_copy(ref, near_ref.at[i], sem_ref.at[i]) for i, ref in enumerate((near_own_ref, near_other_ref))
    ]
    for copy in copies:
        copy.start()
    own_ref[:, tok:] = far_ref[:, :half].T
    other_ref[:, tok:] = far_ref[:, half:].T
    for copy in copies:
        copy.wait()
    own_ref[:, :tok] = near_ref[0].T
    other_ref[:, :tok] = near_ref[1].T


def fold_kernel(own_ref, more_ref, near_ref, far_ref, near_more_ref, far_more_ref, out_ref, rows_ref, sem_ref):
    grad = jnp.concatenate([near_ref[...], far_ref[...]], axis=0)
    grad_more = jnp.concatenate([near_more_ref[...], far_more_ref[...]], axis=0)
    step = out_ref.shape[1]
    copies = []
    blocks = 4
    for i in range(0, out_ref.shape[0], blocks):
        at = slice(i * step, (i + blocks) * step)
        part = jnp.dot(own_ref[at], grad, preferred_element_type=F32)
        part = (part + jnp.dot(more_ref[at], grad_more, preferred_element_type=F32)).astype(BF16)
        for j in range(blocks):
            rows_ref[i + j] = part[j * step : (j + 1) * step]
        to = pl.ds(i, blocks)
        copies.append(pltpu.make_async_copy(rows_ref.at[to], out_ref.at[to], sem_ref.at[i // blocks]))
        copies[-1].start()
    for copy in copies:
        copy.wait()


def back_kernel(near_ref, far_ref, own_ref, other_ref, keep_ref, send_ref):
    tok = near_ref.shape[0]
    half = own_ref.shape[0]
    grad = jnp.concatenate([near_ref[...], far_ref[...]], axis=0)
    for c, weight_ref in enumerate((own_ref, other_ref)):
        rows = lax.dot_general(
            grad, weight_ref[...], (((1,), (1,)), ((), ())), preferred_element_type=F32
        ).astype(BF16)
        keep_ref[:, c * half : (c + 1) * half] = rows[:tok]
        send_ref[:, c * half : (c + 1) * half] = rows[tok:]


def sum_kernel(parts_ref, out_ref):
    total = parts_ref[0].astype(F32)
    for i in range(1, parts_ref.shape[0]):
        total = total + parts_ref[i].astype(F32)
    total = total.astype(BF16)
    rows = out_ref.shape[1]
    for z in range(out_ref.shape[0]):
        out_ref[z ^ GATHER_FIRST ^ REDUCE_FIRST] = total[z * rows : (z + 1) * rows]


def probs_kernel(queries_ref, keys_ref, seg_row_ref, seg_col_ref, out_ref):
    tok = queries_ref.shape[0]
    rows = lax.broadcasted_iota(jnp.int32, (tok, tok), 0)
    cols = lax.broadcasted_iota(jnp.int32, (tok, tok), 1)
    allowed = (seg_col_ref[...] == seg_row_ref[...]) & (cols <= rows)
    scale = F32(1.0 / np.sqrt(HD))
    for j in range(VH):
        key = keys_ref[:, j * HD : (j + 1) * HD]
        for h in range(GROUPS):
            at = (j * GROUPS + h) * HD
            scores = lax.dot_general(
                queries_ref[:, at : at + HD], key, (((1,), (1,)), ((), ())), preferred_element_type=F32
            )
            scores = jnp.where(allowed, scores * scale, F32(-1000000000.0))
            expos = jnp.exp(scores - jnp.max(scores, axis=-1, keepdims=True))
            total = jnp.sum(expos, axis=-1, keepdims=True)
            out_ref[j, h * tok : (h + 1) * tok, :] = (expos / total).astype(BF16)


def states_kernel(moment_ref, second_ref, master_ref, moment_out_ref, second_out_ref, master_out_ref, decay_ref):
    moment_out_ref[...] = beta_one * moment_ref[...]
    second_out_ref[...] = beta_two * second_ref[...]
    master_out_ref[...] = master_ref[...]
    decay_ref[...] = decay_rate * master_ref[...]


def attend_kernel(near_ref, sent_ref, probs_ref, attended_ref, grad_ref, rows_ref, sem_ref):
    tok = near_ref.shape[0]
    wide = GROUPS * HD
    copies = []
    for j in range(VH):
        cols = slice(j * HD, (j + 1) * HD)
        value = (near_ref[:, cols] + sent_ref[:, cols].astype(F32)).astype(BF16)
        attended = jnp.dot(probs_ref[j], value, preferred_element_type=F32).astype(BF16)
        for h in range(GROUPS):
            rows_ref[j, :, h * HD : (h + 1) * HD] = attended[h * tok : (h + 1) * tok]
        copies.append(
            pltpu.make_async_copy(rows_ref.at[j], attended_ref.at[:, j * wide : (j + 1) * wide], sem_ref.at[j])
        )
        copies[-1].start()
        grad_ref[:, cols] = lax.dot_general(
            probs_ref[j], attended, (((0,), (0,)), ((), ())), preferred_element_type=F32
        ).astype(BF16)
    for copy in copies:
        copy.wait()


SMEM = pl.BlockSpec(memory_space=pltpu.SMEM)
VMEM = pl.BlockSpec(memory_space=pltpu.VMEM)
HBM = pl.BlockSpec(memory_space=pltpu.HBM)


def copies(n):
    return pltpu.SemaphoreType.DMA((n,))


def call(kernel, out_shape, flops, nbytes, *more, args=(), scratch=(), out=None, hbm=(), late=()):
    args = (*args, *more)
    specs = [SMEM if a.dtype == jnp.int32 and a.ndim == 1 else VMEM for a in args]
    specs = [HBM if i in hbm else spec for i, spec in enumerate(specs)]
    if out is None:
        out = (VMEM,) * len(out_shape) if isinstance(out_shape, tuple) else VMEM
    if out is HBM:
        out_shape = pltpu.HBM(out_shape.shape, out_shape.dtype)
    if late:
        out_shape = tuple(pltpu.HBM(o.shape, o.dtype) if i in late else o for i, o in enumerate(out_shape))
    args = [pltpu.with_memory_space_constraint(a, pltpu.HBM) if i in hbm else a for i, a in enumerate(args)]
    return pl.pallas_call(
        kernel,
        out_shape=out_shape,
        in_specs=specs,
        out_specs=out,
        scratch_shapes=scratch,
        compiler_params=pltpu.CompilerParams(vmem_limit_bytes=24 * 1024 * 1024),
        cost_estimate=pl.CostEstimate(flops=flops, bytes_accessed=nbytes, transcendentals=0),
    )(*args)


def swap_core(array):
    return lax.ppermute(array, "c", [(0, 1), (1, 0)])


def swap_pair(array):
    return lax.ppermute(array, "zll", [(0, 1), (1, 0)])


def exchange(blocks, members, first):
    ids = np.arange(np.prod(SIZES)).reshape(SIZES)
    last = [AXES.index(a) for a in members]
    ids = ids.transpose([i for i in range(len(SIZES)) if i not in last] + last).reshape(-1, blocks.shape[0])
    groups = ids[:, np.arange(blocks.shape[0]) ^ first].tolist()
    return lax.all_to_all(blocks, AXES, split_axis=0, concat_axis=0, axis_index_groups=groups, tiled=True)


def exchange_z(blocks, first):
    return exchange(blocks, ("zlh", "zh"), first)


def exchange_plane(blocks):
    return exchange(blocks, ("y", "x"), 0)


def per_device(hidden_in, queries, keys, lengths, master, moment, second):
    tok, width = hidden_in.shape
    kv = keys.shape[1]
    rows = master.shape[0]
    feats = width // 4
    at = jnp.stack([lax.axis_index("zll"), lax.axis_index("c")]).astype(jnp.int32)
    block = jax.ShapeDtypeStruct((tok, 2 * feats), BF16)
    half = jax.ShapeDtypeStruct((tok, feats), BF16)
    value = jax.ShapeDtypeStruct((tok, kv), BF16)
    total = jax.ShapeDtypeStruct((tok, kv), F32)
    matrix = pltpu.VMEM((1024, 1024), BF16)
    cols = pltpu.VMEM((4 * tok, 1024), BF16)

    weight = call(
        master_kernel,
        jax.ShapeDtypeStruct((DEPTH, rows, kv), BF16),
        0,
        1 << 17,
        master,
        scratch=[pltpu.VMEM((rows, kv), F32), copies(1)],
        hbm=(0,),
    )
    weight, hidden_in = lax.optimization_barrier((weight, hidden_in))
    weight = exchange_z(weight, GATHER_FIRST).reshape(DEPTH * rows, kv)

    split = functools.partial(
        call,
        flops=4 * tok * 1024 * 1024,
        nbytes=2 << 20,
        scratch=[cols, pltpu.VMEM((1024, 512), BF16), copies(16)],
        hbm=(1,),
    )
    (send,) = split(functools.partial(split_kernel, 1), (block,), args=(at, hidden_in))
    far = swap_pair(send)

    weight = call(
        spread_kernel,
        jax.ShapeDtypeStruct((PLANE, DEPTH * rows, kv), BF16),
        0,
        1 << 20,
        weight,
        scratch=[copies(PLANE)],
        out=HBM,
    )
    weight, keys, hidden_in = lax.optimization_barrier((weight, keys, hidden_in))
    weight = exchange_plane(weight).reshape(PLANE * DEPTH * rows, kv)

    near_own, near_other = split(functools.partial(split_kernel, 0), (half, half), args=(at, hidden_in), late=(0, 1))

    ends = jnp.cumsum(lengths[0])
    seg = jnp.sum((jnp.arange(tok, dtype=jnp.int32)[:, None] >= ends[None, :]).astype(jnp.int32), axis=1)
    (probs,) = call(
        probs_kernel,
        (jax.ShapeDtypeStruct((VH, GROUPS * tok, tok), BF16),),
        4 * tok * tok * QH * HD,
        8 << 20,
        queries,
        keys,
        seg[None, :],
        seg[:, None],
        late=(0,),
    )
    flipped = jax.ShapeDtypeStruct((feats, 2 * tok), BF16)
    columns_own, columns_other = call(
        flip_kernel, (flipped, flipped), WEIGHTY // 24, 2 << 20, near_own, near_other, far,
        scratch=[pltpu.VMEM((2, tok, feats), BF16), copies(2)], hbm=(0, 1), late=(0, 1)
    )
    columns_more = swap_core(columns_other)
    weight, near_own, near_other, far, columns_own, columns_more, probs = lax.optimization_barrier(
        (weight, near_own, near_other, far, columns_own, columns_more, probs)
    )
    weight_other = swap_core(weight)

    flops = 2 * tok * feats * kv
    near, far_values = call(first_kernel, (total, total), 2 * flops, 2 << 20, near_own, far, weight)
    sent = swap_pair(call(second_kernel, value, flops, 2 << 20, far, weight_other, far_values))
    near = call(second_kernel, total, flops, 2 << 20, near_other, weight_other, near)
    attended, grad = call(
        attend_kernel,
        (jax.ShapeDtypeStruct((tok, QH * HD), BF16), value),
        4 * tok * tok * QH * HD,
        4 << 20,
        near,
        sent,
        probs,
        scratch=[pltpu.VMEM((VH, tok, GROUPS * HD), BF16), copies(VH)],
        out=(HBM, VMEM),
    )
    grad_far = swap_pair(grad)

    part = call(
        fold_kernel,
        jax.ShapeDtypeStruct((PLANE, DEPTH * rows, kv), BF16),
        4 * flops,
        2 << 20,
        columns_own,
        columns_more,
        grad,
        grad_far,
        swap_core(grad),
        swap_core(grad_far),
        scratch=[pltpu.VMEM((PLANE, DEPTH * rows, kv), BF16), copies(PLANE // 4)],
        out=HBM,
    )
    part, grad, grad_far = lax.optimization_barrier((part, grad, grad_far))

    keep, send = call(
        back_kernel, (block, block), 8 * tok * feats * kv, 4 << 20, grad, grad_far, weight, weight_other, late=(0,)
    )
    part, moment, second, master = lax.optimization_barrier((part, moment, second, master))
    moment, second, master, decay = call(
        states_kernel, (jax.ShapeDtypeStruct(master.shape, F32),) * 4, 0, 1 << 17, moment, second, master
    )
    grad_hidden = call(
        join_kernel,
        jax.ShapeDtypeStruct((tok, width), BF16),
        WEIGHTY,
        2 << 20,
        at,
        keep,
        swap_pair(send),
        scratch=[cols, cols, matrix, copies(16)],
        out=HBM,
    )

    part = exchange_plane(part)
    part = call(sum_kernel, jax.ShapeDtypeStruct((DEPTH, rows, kv), BF16), 0, 1 << 20, part)
    part = exchange_z(part, REDUCE_FIRST)
    gradient = jnp.sum(part.astype(F32), axis=0) / F32(tok * 512)

    moment_new = moment + (1.0 - beta_one) * gradient
    second_new = second + (1.0 - beta_two) * gradient * gradient
    moment_hat = moment_new / (1.0 - beta_one**10)
    second_hat = second_new / (1.0 - beta_two**10)
    master_new = master - learn_rate * (
        moment_hat / (jnp.sqrt(second_hat) + adam_eps) + decay
    )
    return (attended, grad_hidden, master_new, moment_new, second_new)


def solution(mesh):
    named = Mesh(mesh.devices.reshape(SIZES), AXES)
    return jax.shard_map(
        per_device,
        mesh=named,
        in_specs=(TOK_SPEC, TOK_SPEC, TOK_SPEC, TOK_SPEC, ROW_SPEC, ROW_SPEC, ROW_SPEC),
        out_specs=(TOK_SPEC, TOK_SPEC, ROW_SPEC, ROW_SPEC, ROW_SPEC),
        check_vma=False,
    )
```
